32 devices in a mesh: row: 4 (over z), col: 8 (over y, x, core).
Axes of the slice: x: 2, y: 2, z: 4, core: 2. Of those that a mesh axis runs over, the one named last changes fastest.
Arguments:
- green_blocks: bfloat16 [4, 8, 12, 2, 288, 288], P('row', 'col'), may hold values from -0.125 to 0.125
- slot_rows: int32 [4, 8, 12], P('row', 'col'), may hold values from 0 to 7, as said below
- slot_cols: int32 [4, 8, 12], P('row', 'col'), may hold values from 0 to 3
- slot_count: int32 [4, 8], P('row', 'col'), may hold values from 2 to 12, as said below
- cell_class: int32 [4, 8, 96], P(None, 'col'), may hold values from 0 to 15
- class_contrast: float32 [16, 2], replicated, may hold values from -0.6 to 0.6
- background: float32 [2, 32, 4, 8, 288], P(None, None, None, 'col'), may hold values from -6 to 6
Outputs:
- total_field: float32 [2, 32, 4, 8, 288], P(None, None, None, 'col')
The draws below stay inside these ranges and needn't reach their ends.
Inputs may be any that keep to these rules, and one draw needn't show every extreme that they name: slot_rows[r, c, s] and slot_cols[r, c, s] name different block pairs within one device's slots, and every slot, used or not, names a block in the upper triangle: (slot_rows // 2) * 8 + 2 r + slot_rows % 2 is at most slot_cols * 8 + c. Slots from slot_count[r, c] on are not used. `slot_count`: some device holds exactly 12 stored blocks.
All inputs are finite; a program needn't handle non-finite values.
Results may differ from the reference program's by a relative error of at most 0.0033.
Values may be sent and summed in bfloat16 or wider, within the bound.
No kernel may reach another device: no remote copies, remote signals or barrier semaphores. Data moves between devices by JAX's collectives and lax.ppermute only.
A program may use at most 64 MiB of HBM per device.

```python
import jax
import jax.numpy as jnp
from jax import lax

BLOCK = 96
ENTRIES = 288
SOURCES = 32
COL_BLOCKS = 4
ROW_BLOCKS = 8
SLOTS = 12
CLASSES = 16
PRODUCTS = 3
GRID_ROWS = 4
STRIDE = 8
BLOCKS = 32


def pattern_tables(key):
    base = jax.random.fold_in(key, 11)
    key_score, key_first, key_second, key_full = jax.random.split(base, 4)
    pairs = ROW_BLOCKS * COL_BLOCKS
    local_row = jnp.arange(ROW_BLOCKS, dtype=jnp.int32)[None, None, :, None]
    local_col = jnp.arange(COL_BLOCKS, dtype=jnp.int32)[None, None, None, :]
    grid_row = jnp.arange(GRID_ROWS, dtype=jnp.int32)[:, None, None, None]
    grid_col = jnp.arange(STRIDE, dtype=jnp.int32)[None, :, None, None]
    block_row = local_row // 2 * STRIDE + 2 * grid_row + local_row % 2
    block_col = local_col * STRIDE + grid_col
    upper = (block_row <= block_col).reshape(GRID_ROWS, STRIDE, pairs)
    scores = jax.random.randint(key_score, (GRID_ROWS, STRIDE, pairs), 0, 1024) * 64 + jnp.arange(pairs, dtype=jnp.int32)
    scores = jnp.where(upper, scores, scores + 131072)
    order = jnp.argsort(scores, axis=-1, stable=True)[:, :, :SLOTS]
    rows_out = (order // COL_BLOCKS).astype(jnp.int32)
    cols_out = (order % COL_BLOCKS).astype(jnp.int32)
    first = jax.random.randint(key_first, (GRID_ROWS, STRIDE), 0, 11)
    second = jax.random.randint(key_second, (GRID_ROWS, STRIDE), 0, 11)
    counts = 2 + first * second * (SLOTS - 2) // 100
    chosen = jax.random.randint(key_full, (), 0, GRID_ROWS * STRIDE)
    flat = jnp.arange(GRID_ROWS * STRIDE, dtype=jnp.int32).reshape(GRID_ROWS, STRIDE)
    counts = jnp.where(flat == chosen, SLOTS, counts).astype(jnp.int32)
    return (rows_out, cols_out, counts)


def draw_slot_rows(key, part):
    return pattern_tables(key)[0]


def draw_slot_cols(key, part):
    return pattern_tables(key)[1]


def draw_slot_count(key, part):
    return pattern_tables(key)[2]


def with_ends(result, stream_key, least, high):
    place = [jax.random.randint(jax.random.fold_in(stream_key, axis), (), 0, length) for axis, length in enumerate(result.shape)]
    widest = result.shape.index(max(result.shape))
    neighbour = place[:widest] + [(place[widest] + 1) % result.shape[widest]] + place[widest + 1:]
    return result.at[tuple(place)].set(least).at[tuple(neighbour)].set(high)


def levels(own_key, dims, cuts, smallest, high):
    factor_of, own = 1.0, jax.random.fold_in(own_key, 6)
    for dim, blocks in cuts:
        heights = jnp.exp(jax.random.uniform(jax.random.fold_in(own, dim), (blocks,), jnp.float32, smallest / len(cuts), high / len(cuts)))
        factor_of = factor_of * jnp.repeat(heights, dims[dim] // blocks).reshape([-1 if axis == dim else 1 for axis in range(len(dims))])
    return factor_of


def centred(key, dims, spread, most, shards=(), kind=jnp.bfloat16):
    result = spread * jax.random.normal(key, dims, jnp.float32)
    if shards:
        result = result * levels(key, dims, shards, -0.22, 0.18)
    return jnp.clip(result, -most, most).astype(kind)


def setup_inputs(seed: int = 0) -> dict:
    arg_keys = jax.random.split(jax.random.key(seed), 8)
    green_blocks = centred(arg_keys[0], (GRID_ROWS, STRIDE, SLOTS, 2, ENTRIES, ENTRIES), (STRIDE * ENTRIES) ** -0.5, 0.125, ((0, 4), (1, 8)))
    slot_rows = draw_slot_rows(jax.random.fold_in(arg_keys[7], 71), 0)
    slot_cols = draw_slot_cols(jax.random.fold_in(arg_keys[7], 71), 0)
    slot_count = draw_slot_count(jax.random.fold_in(arg_keys[7], 71), 0)
    cell_class = with_ends(jax.random.randint(arg_keys[4], (COL_BLOCKS, STRIDE, BLOCK), 0, CLASSES), jax.random.fold_in(arg_keys[4], 1), 0, CLASSES - 1).astype(jnp.int32)
    class_contrast = jnp.clip(jax.random.uniform(arg_keys[5], (CLASSES, 2), jnp.float32, -0.6, 0.6), -0.6, 0.6)
    background = centred(arg_keys[6], (2, SOURCES, COL_BLOCKS, STRIDE, ENTRIES), 1.0, 6.0, ((3, 8),), jnp.float32)
    return {"green_blocks": green_blocks, "slot_rows": slot_rows, "slot_cols": slot_cols, "slot_count": slot_count, "cell_class": cell_class, "class_contrast": class_contrast, "background": background}


def complex_scale(field_now, contrast_re, contrast_im):
    real_part = field_now[0]
    imag_part = field_now[1]
    scaled = jnp.stack([contrast_re * real_part - contrast_im * imag_part, contrast_re * imag_part + contrast_im * real_part])
    return scaled.astype(jnp.bfloat16)


def combine(products):
    return jnp.stack([products[0, 0] - products[1, 1], products[0, 1] + products[1, 0]])


def reference(green_blocks, slot_rows, slot_cols, slot_count, cell_class, class_contrast, background):
    lookup = class_contrast[cell_class].reshape(BLOCKS, BLOCK, 2)
    contrast_re = jnp.tile(lookup[:, :, 0], (1, 3))
    contrast_im = jnp.tile(lookup[:, :, 1], (1, 3))
    start_field = background.reshape(2, SOURCES, BLOCKS, ENTRIES)
    grid_row = jnp.arange(GRID_ROWS, dtype=jnp.int32)[:, None, None]
    grid_col = jnp.arange(STRIDE, dtype=jnp.int32)[None, :, None]
    block_rows = ((slot_rows // 2) * STRIDE + 2 * grid_row + slot_rows % 2).astype(jnp.int32)
    block_cols = (slot_cols * STRIDE + grid_col).astype(jnp.int32)
    living = (jnp.arange(SLOTS, dtype=jnp.int32)[None, None, :] < slot_count[:, :, None]).astype(jnp.float32)
    devices_all = GRID_ROWS * STRIDE
    tiles_all = green_blocks.reshape(devices_all, SLOTS, 2, ENTRIES, ENTRIES)
    rows_flat = block_rows.reshape(devices_all, SLOTS)
    cols_flat = block_cols.reshape(devices_all, SLOTS)
    live_flat = living.reshape(devices_all, SLOTS)

    def apply_operator(current):
        current_wide = lax.optimization_barrier(current).astype(jnp.float32)

        def visit(running, item):
            tiles, rows_here, cols_here, live_here = item
            tiles_wide = tiles.astype(jnp.float32)
            off_diagonal = (rows_here != cols_here).astype(jnp.float32)
            direct_in = jnp.take(current_wide, cols_here, axis=2)
            mirror_in = jnp.take(current_wide, rows_here, axis=2)
            direct_terms = combine(jnp.einsum('sqoi,pksi->qpkso', tiles_wide, direct_in)) * live_here[None, None, :, None]
            mirror_terms = combine(jnp.einsum('sqoi,pkso->qpksi', tiles_wide, mirror_in)) * (live_here * off_diagonal)[None, None, :, None]
            running = running.at[:, :, rows_here].add(direct_terms)
            running = running.at[:, :, cols_here].add(mirror_terms)
            return running, None

        start = jnp.zeros((2, SOURCES, BLOCKS, ENTRIES), jnp.float32)
        return lax.scan(visit, start, (tiles_all, rows_flat, cols_flat, live_flat))[0]

    field_now = start_field
    for step_index in range(PRODUCTS):
        current = complex_scale(field_now, contrast_re, contrast_im)
        field_now = start_field + apply_operator(current)
    return field_now.reshape(2, SOURCES, COL_BLOCKS, STRIDE, ENTRIES)
```

```python
import jax
import jax.numpy as jnp
from jax import lax
from jax.experimental import pallas as pl
from jax.experimental.pallas import tpu as pltpu
from jax.sharding import PartitionSpec as P

PRODUCTS = 3
LANES = 128
VMEM_BYTES = 8 * 1024 * 1024
BF = jnp.bfloat16
F32 = jnp.float32


def from_root(array, axis, root):
    mine = lax.axis_index(axis) == root
    return lax.psum(jnp.where(mine, array, jnp.zeros_like(array)), axis)


def complex_scale(field_now, contrast_re, contrast_im):
    real_part = field_now[0]
    imag_part = field_now[1]
    scaled = jnp.stack(
        [
            contrast_re * real_part - contrast_im * imag_part,
            contrast_re * imag_part + contrast_im * real_part,
        ]
    )
    return scaled.astype(BF)


def combine(products):
    return jnp.stack([products[0, 0] - products[1, 1], products[0, 1] + products[1, 0]])


def local_general(green_blocks, slot_rows, slot_cols, slot_count, cell_class, class_contrast, background):
    row_index = lax.axis_index("row")
    col_index = lax.axis_index("col")
    stride = lax.axis_size("col")
    green_tiles = green_blocks[0, 0]
    slot_total = green_tiles.shape[0]
    entries = green_tiles.shape[-1]
    sources = background.shape[1]
    col_blocks = background.shape[2]
    row_blocks = 2 * col_blocks
    local_rows = slot_rows[0, 0]
    local_cols = slot_cols[0, 0]
    global_rows = local_rows // 2 * stride + 2 * row_index + local_rows % 2
    global_cols = local_cols * stride + col_index
    off_diagonal = (global_rows != global_cols).astype(F32)
    living = (jnp.arange(slot_total) < slot_count[0, 0]).astype(F32)
    row_pick = (local_rows[:, None] == jnp.arange(row_blocks)[None, :]).astype(F32) * living[:, None]
    col_pick = (local_cols[:, None] == jnp.arange(col_blocks)[None, :]).astype(F32) * (
        living * off_diagonal
    )[:, None]
    classes = class_contrast.shape[0]
    lookup = (cell_class[:, 0, :, None] == jnp.arange(classes)[None, None, :]).astype(F32)
    values = jnp.einsum("bte,ec->btc", lookup, class_contrast, precision=lax.Precision.HIGHEST)
    contrast_re = jnp.tile(values[:, :, 0], (1, 3))
    contrast_im = jnp.tile(values[:, :, 1], (1, 3))
    start_field = background[:, :, :, 0, :]
    field_now = start_field
    current = complex_scale(field_now, contrast_re, contrast_im)
    for step_index in range(PRODUCTS):
        final_step = step_index + 1 == PRODUCTS
        halves = [from_root(current, "col", 2 * row_index + parity) for parity in range(2)]
        row_current = jnp.stack(halves, axis=3).reshape(2, sources, row_blocks, entries)
        direct_in = jnp.take(current, local_cols, axis=2)
        mirror_in = jnp.take(row_current, local_rows, axis=2)
        direct_terms = combine(
            jnp.einsum("sqoi,pksi->qpkso", green_tiles, direct_in, preferred_element_type=F32)
        )
        mirror_terms = combine(
            jnp.einsum("sqoi,pkso->qpksi", green_tiles, mirror_in, preferred_element_type=F32)
        )
        direct_part = jnp.einsum(
            "pkse,sb->pkbe", direct_terms, row_pick, precision=lax.Precision.HIGHEST
        )
        mirror_part = jnp.einsum(
            "pkse,sb->pkbe", mirror_terms, col_pick, precision=lax.Precision.HIGHEST
        )
        row_total = lax.psum(direct_part, "col")
        owned_part = lax.dynamic_index_in_dim(
            row_total.reshape(2, sources, col_blocks, 2, entries),
            col_index % 2,
            axis=3,
            keepdims=False,
        )
        direct_here = from_root(owned_part, "row", col_index // 2)
        column_total = lax.psum(mirror_part, "row")
        field_now = start_field + column_total + direct_here
        if not final_step:
            current = complex_scale(field_now, contrast_re, contrast_im)
    return field_now[:, :, :, None, :]


def turned(value):
    shape = value.shape
    tiles = value.reshape(shape[0] // 8, 8, shape[1])
    return jnp.concatenate([-tiles[:, 4:], tiles[:, :4]], axis=1).reshape(shape)


def put_block(xs_ref, xt_ref, at, piece, value, width):
    lanes = pl.ds(piece * LANES, width)
    xs_ref[at, :, lanes] = value[:, :width].astype(BF)
    xt_ref[at, :, lanes] = turned(value)[:, :width].astype(BF)


def unpack_half(msg_ref, q, half, xs_ref, xt_ref, at):
    groups = xs_ref.shape[1] // 8
    tail = xs_ref.shape[2] - 2 * LANES
    for piece in range(2):
        both = msg_ref[q * groups : (q + 1) * groups, piece * 16 : piece * 16 + 16, :].astype(F32)
        value = both[:, half * 8 : half * 8 + 8, :].reshape(groups * 8, LANES)
        put_block(xs_ref, xt_ref, at, piece, value, LANES)
    ends = msg_ref[q * groups : (q + 1) * groups, 32:40, :].astype(F32).reshape(groups * 8, LANES)
    if half:
        ends = pltpu.roll(ends, LANES - tail, 1)
    put_block(xs_ref, xt_ref, at, 2, ends, tail)


def copy_in(x_ref, xs_ref, xt_ref, offset):
    for q in range(x_ref.shape[0]):
        value = x_ref[q].astype(F32)
        xs_ref[offset + q] = x_ref[q]
        xt_ref[offset + q] = turned(value).astype(BF)


def slot_products(table_ref, g_ref, xs_ref, xt_ref, acc_ref, src_row, dst_row):
    acc_ref[...] = jnp.zeros_like(acc_ref)
    for s in range(g_ref.shape[0]):
        src = table_ref[src_row, s]
        dst = table_ref[dst_row, s]
        product = jnp.dot(xs_ref[src], g_ref[s, 0], preferred_element_type=F32)
        product += jnp.dot(xt_ref[src], g_ref[s, 1], preferred_element_type=F32)
        acc_ref[dst] += product


def start_kernel(table_ref, classes_ref, kinds_ref, back_ref, out_ref, extra_ref):
    r = table_ref[4, 0]
    blocks, rows, entries = out_ref.shape
    groups = rows // 8
    tail = entries - 2 * LANES
    kinds = kinds_ref[...]
    real = jnp.zeros(kinds.shape, F32)
    imag = jnp.zeros(kinds.shape, F32)
    for k in range(classes_ref.shape[0]):
        real = jnp.where(kinds == k, classes_ref[k, 0], real)
        imag = jnp.where(kinds == k, classes_ref[k, 1], imag)
    real = jnp.concatenate([real] * 3, axis=1)
    imag = jnp.concatenate([imag] * 3, axis=1)
    for q in range(blocks):
        back = back_ref[q]
        out_ref[q] = (real[q : q + 1] * back + imag[q : q + 1] * turned(back)).astype(BF)
        marks = []
        for value in (real[q : q + 1], imag[q : q + 1]):
            for _ in range(3):
                part = value.astype(BF).astype(F32)
                marks.append(part)
                value = value - part
        marks = jnp.concatenate(marks + [jnp.zeros((2, entries), F32)], axis=0)
        ends = jnp.concatenate([marks[:, 2 * LANES :], jnp.zeros((8, LANES - tail), F32)], axis=1)
        ends = pltpu.roll(ends, tail, 1)
        lane = lax.broadcasted_iota(jnp.int32, (8, LANES), 1)
        for g in range(groups):
            at = slice(g * 8, g * 8 + 8)
            pieces = [back[at, :LANES], back[at, LANES : 2 * LANES]]
            last = jnp.concatenate([back[at, 2 * LANES :], jnp.zeros((8, LANES - tail), F32)], axis=1)
            value = jnp.where(r == 0, pieces[0], jnp.where(r == 1, pieces[1], last))
            high = value.astype(BF).astype(F32)
            low = value - high
            high = jnp.where((r == 2) & (lane >= tail), ends, high)
            high = jnp.where(r == 3, marks[:, :LANES], high)
            low = jnp.where(r == 3, marks[:, LANES : 2 * LANES], low)
            extra_ref[q * groups + g] = jnp.concatenate([high, low], axis=0).astype(BF)


def turn_kernel(g_ref, gt_ref):
    for s in range(g_ref.shape[0]):
        for part in range(2):
            gt_ref[s, part] = g_ref[s, part].T


def direct_kernel(first, table_ref, gt_ref, x_ref, own_ref, other_ref, xs_ref, xt_ref, acc_ref):
    blocks = own_ref.shape[0]
    if first:
        copy_in(x_ref, xs_ref, xt_ref, 0)
    else:
        for q in range(blocks):
            unpack_half(x_ref, q, 0, xs_ref, xt_ref, q)
    slot_products(table_ref, gt_ref, xs_ref, xt_ref, acc_ref, 0, 1)
    for q in range(blocks):
        own_ref[q] = acc_ref[q]
        other_ref[q] = acc_ref[blocks + q]


def mirror_kernel(first, table_ref, g_ref, x_ref, x_other_ref, out_ref, xs_ref, xt_ref, acc_ref):
    blocks = out_ref.shape[0]
    if first:
        copy_in(x_ref, xs_ref, xt_ref, 0)
        copy_in(x_other_ref, xs_ref, xt_ref, blocks)
    else:
        for q in range(blocks):
            unpack_half(x_ref, q, 1, xs_ref, xt_ref, q)
            unpack_half(x_other_ref, q, 1, xs_ref, xt_ref, blocks + q)
    slot_products(table_ref, g_ref, xs_ref, xt_ref, acc_ref, 2, 3)
    for q in range(blocks):
        out_ref[q] = acc_ref[q]


def pack_kernel(mirror_ref, own_ref, got_ref, *rest):
    msg_ref = rest[-1]
    base = 0
    if len(rest) == 2:
        base = rest[0].shape[1]
        msg_ref[:, 0:base, :] = rest[0][...]
    blocks, rows, entries = own_ref.shape
    groups = rows // 8
    tail = entries - 2 * LANES
    for q in range(blocks):
        at = slice(q * groups, (q + 1) * groups)
        for piece in range(2):
            lanes = slice(piece * LANES, (piece + 1) * LANES)
            direct = (own_ref[q, :, lanes] + got_ref[q, :, lanes]).reshape(groups, 8, LANES)
            mirror = mirror_ref[q, :, lanes].reshape(groups, 8, LANES)
            start = base + piece * 16
            msg_ref[at, start : start + 16, :] = jnp.concatenate([direct, mirror], axis=1).astype(BF)
        lanes = slice(2 * LANES, entries)
        direct = own_ref[q, :, lanes] + got_ref[q, :, lanes]
        mirror = mirror_ref[q, :, lanes]
        filler = jnp.zeros((rows, LANES - 2 * tail), F32)
        ends = jnp.concatenate([direct, mirror, filler], axis=1).reshape(groups, 8, LANES)
        msg_ref[at, base + 32 : base + 40, :] = ends.astype(BF)


def update_kernel(first, final, rows, cols, tail, *refs):
    if first:
        msg_ref, out_ref, back_ref, contrast_ref = refs
        base = 16
    else:
        msg_ref, back_ref, contrast_ref, out_ref = refs
        base = 0
    lane = lax.broadcasted_iota(jnp.int32, (8, LANES), 1)
    sign = jnp.where(lax.broadcasted_iota(jnp.int32, (8, LANES), 0) < 4, -1.0, 1.0)
    direct = {}
    mirror = {}

    def add(store, key, value):
        store[key] = store[key] + value if key in store else value

    for r in range(rows):
        for c in range(cols):
            d = r * cols + c
            j = 2 * r + c % 2
            for piece in range(2):
                both = msg_ref[d, base + piece * 16 : base + piece * 16 + 16, :].astype(F32)
                add(direct, (j, piece), both[:8])
                add(mirror, (c, piece), both[8:])
            ends = msg_ref[d, base + 32 : base + 40, :].astype(F32)
            add(direct, (j, 2), ends)
            add(mirror, (c, 2), ends)
    current = {}
    for j in range(cols):
        if first:
            pairs = [msg_ref[r * cols + j, 0:16, :].astype(F32) for r in range(4)]
            background = [pair[:8] + pair[8:] for pair in pairs[:3]]
            marks = [pairs[3][:8], pairs[3][8:], pltpu.roll(pairs[2][:8], LANES - tail, 1)]
        for piece in range(3):
            total = direct[j, piece]
            more = mirror[j, piece]
            total = total + (pltpu.roll(more, LANES - tail, 1) if piece == 2 else more)
            if first:
                back = background[piece]
                back_ref[j, piece] = back
                mark = marks[piece]
                real = jnp.broadcast_to(mark[0:1] + mark[1:2] + mark[2:3], (8, LANES))
                imag = jnp.broadcast_to(mark[3:4] + mark[4:5] + mark[5:6], (8, LANES)) * sign
                contrast_ref[j, 0, piece] = real
                contrast_ref[j, 1, piece] = imag
            else:
                back = back_ref[j, piece]
                real = contrast_ref[j, 0, piece]
                imag = contrast_ref[j, 1, piece]
            total = total + back
            if final:
                current[j, piece] = total
            else:
                current[j, piece] = real * total + imag * pltpu.roll(total, 4, 0)
    for r in range(rows):
        for c in range(cols):
            d = r * cols + c
            if final:
                for piece in range(3):
                    out_ref[d, piece * 8 : piece * 8 + 8, :] = current[c, piece]
                continue
            k = 2 * r + c % 2
            for piece in range(2):
                out_ref[d, piece * 16 : piece * 16 + 16, :] = jnp.concatenate(
                    [current[c, piece], current[k, piece]], axis=0
                ).astype(BF)
            ends = jnp.where(lane < tail, current[c, 2], pltpu.roll(current[k, 2], tail, 1))
            out_ref[d, 32:40, :] = ends.astype(BF)


def whole_call(kernel, out_shape, smem, operands, scratch, name):
    spaces = [pltpu.SMEM] * smem + [pltpu.VMEM] * (len(operands) - smem)
    return pl.pallas_call(
        kernel,
        out_shape=out_shape,
        in_specs=[pl.BlockSpec(memory_space=space) for space in spaces],
        out_specs=jax.tree.map(lambda _: pl.BlockSpec(memory_space=pltpu.VMEM), out_shape),
        scratch_shapes=scratch,
        compiler_params=pltpu.CompilerParams(vmem_limit_bytes=VMEM_BYTES),
        name=name,
    )(*operands)


def local_owners(green_blocks, slot_rows, slot_cols, slot_count, cell_class, class_contrast, background):
    r = lax.axis_index("row")
    c = lax.axis_index("col")
    rows = lax.axis_size("row")
    cols = lax.axis_size("col")
    parity = c % 2
    green = green_blocks[0, 0]
    slots, _, entries, _ = green.shape
    sources, blocks = background.shape[1:3]
    groups = sources // 4
    tail = entries - 2 * LANES
    both = ("row", "col")

    local_rows = slot_rows[0, 0]
    local_cols = slot_cols[0, 0]
    living = jnp.arange(slots) < slot_count[0, 0]
    off_diagonal = (local_rows // 2 * cols + 2 * r + local_rows % 2) != (local_cols * cols + c)
    place = (local_rows % 2 ^ parity) * blocks + local_rows // 2
    table = jnp.stack(
        [
            local_cols,
            jnp.where(living, place, 2 * blocks),
            place,
            jnp.where(living & off_diagonal, local_cols, blocks),
            jnp.full_like(local_cols, r),
        ]
    ).astype(jnp.int32)

    block = (groups * 8, entries)
    back = background[:, :, :, 0, :].reshape(2, groups, 4, blocks, entries)
    back = back.transpose(3, 1, 0, 2, 4).reshape((blocks,) + block)
    start, extra = whole_call(
        start_kernel,
        (
            jax.ShapeDtypeStruct((blocks,) + block, BF),
            jax.ShapeDtypeStruct((rows * cols, 16, LANES), BF),
        ),
        2,
        (table, class_contrast, cell_class[:, 0, :], back),
        [],
        "start",
    )

    core_pairs = [(i, i ^ 1) for i in range(cols)]
    arrived = []
    for hop in range(1, cols // 2):
        pairs = [
            (a * cols + 2 * a + p, a * cols + 2 * ((a + hop) % (cols // 2)) + p)
            for a in range(rows)
            for p in range(2)
        ]
        arrived.append(lax.ppermute(start, both, pairs))
    row_mine = jnp.where(c // 2 == r, start, sum(arrived))
    row_other = lax.ppermute(row_mine, "col", core_pairs)

    green_turned = whole_call(turn_kernel, jax.ShapeDtypeStruct(green.shape, BF), 0, (green,), [], "turn")
    part = jax.ShapeDtypeStruct((blocks,) + block, F32)
    message = jax.ShapeDtypeStruct((rows * cols, 40, LANES), BF)
    for step in range(PRODUCTS):
        first = step == 0
        final = step + 1 == PRODUCTS
        if first:
            direct_in, mirror_in = start, (row_mine, row_other)
        else:
            direct_in, mirror_in = x_msg, (x_msg, lax.ppermute(x_msg, "col", core_pairs))
        own, other = whole_call(
            lambda *refs, first=first: direct_kernel(first, *refs),
            (part, part),
            1,
            (table, green_turned, direct_in),
            [
                pltpu.VMEM((blocks,) + block, BF),
                pltpu.VMEM((blocks,) + block, BF),
                pltpu.VMEM((2 * blocks + 1,) + block, F32),
            ],
            f"direct_{step}",
        )
        got = lax.ppermute(other, "col", core_pairs)
        mirror = whole_call(
            lambda *refs, first=first: mirror_kernel(first, *refs),
            part,
            1,
            (table, green) + mirror_in,
            [
                pltpu.VMEM((2 * blocks,) + block, BF),
                pltpu.VMEM((2 * blocks,) + block, BF),
                pltpu.VMEM((blocks + 1,) + block, F32),
            ],
            f"mirror_{step}",
        )
        y_shape = jax.ShapeDtypeStruct((rows * cols, 56, LANES), BF) if first else message
        operands = (mirror, own, got) + ((extra,) if first else ())
        y_msg = whole_call(pack_kernel, y_shape, 0, operands, [], f"pack_{step}")
        y_msg = lax.all_to_all(y_msg, both, 0, 0, tiled=True)
        run = lambda *refs, first=first, final=final: update_kernel(first, final, rows, cols, tail, *refs)
        if first:
            x_msg, owner_back, owner_contrast = whole_call(
                run,
                (
                    message,
                    jax.ShapeDtypeStruct((cols, 3, 8, LANES), F32),
                    jax.ShapeDtypeStruct((cols, 2, 3, 8, LANES), F32),
                ),
                0,
                (y_msg,),
                [],
                f"update_{step}",
            )
        else:
            x_shape = jax.ShapeDtypeStruct((rows * cols, 24, LANES), F32) if final else message
            x_msg = whole_call(run, x_shape, 0, (y_msg, owner_back, owner_contrast), [], f"update_{step}")
        x_msg = lax.all_to_all(x_msg, both, 0, 0, tiled=True)
    field = x_msg.reshape(blocks, groups, 3, 2, 4, LANES).transpose(3, 1, 4, 0, 2, 5)
    field = field.reshape(2, sources, blocks, 3 * LANES)[..., :entries]
    return field[:, :, :, None, :]


def solution(mesh):
    in_specs = (
        P("row", "col", None, None, None, None),
        P("row", "col", None),
        P("row", "col", None),
        P("row", "col"),
        P(None, "col", None),
        P(),
        P(None, None, None, "col", None),
    )
    out_specs = P(None, None, None, "col", None)
    rows, cols = mesh.shape["row"], mesh.shape["col"]

    def local(*args):
        sources, blocks = args[6].shape[1:3]
        entries = args[6].shape[4]
        owners = (
            rows == blocks == 4
            and cols == 2 * rows
            and sources == 4 * cols
            and 2 * LANES < entries <= 2 * LANES + LANES // 2
            and args[5].shape[0] <= 256
        )
        return (local_owners if owners else local_general)(*args)

    return jax.shard_map(local, mesh=mesh, in_specs=in_specs, out_specs=out_specs, check_vma=False)
```

```python
import jax
import jax.numpy as jnp
from jax import lax
from jax.experimental import pallas as pl
from jax.experimental.pallas import tpu as pltpu
from jax.sharding import PartitionSpec as P

PRODUCTS = 3
LANES = 128
SMALLEST = 2.0**-100
VMEM_BYTES = 8 * 1024 * 1024
BF = jnp.bfloat16
F32 = jnp.float32


def from_root(array, axis, root):
    mine = lax.axis_index(axis) == root
    return lax.psum(jnp.where(mine, array, jnp.zeros_like(array)), axis)


def complex_scale(field_now, contrast_re, contrast_im):
    real_part = field_now[0]
    imag_part = field_now[1]
    scaled = jnp.stack(
        [
            contrast_re * real_part - contrast_im * imag_part,
            contrast_re * imag_part + contrast_im * real_part,
        ]
    )
    return scaled.astype(BF)


def combine(products):
    return jnp.stack([products[0, 0] - products[1, 1], products[0, 1] + products[1, 0]])


def local_general(green_blocks, slot_rows, slot_cols, slot_count, cell_class, class_contrast, background):
    row_index = lax.axis_index("row")
    col_index = lax.axis_index("col")
    stride = lax.axis_size("col")
    green_tiles = green_blocks[0, 0]
    slot_total = green_tiles.shape[0]
    entries = green_tiles.shape[-1]
    sources = background.shape[1]
    col_blocks = background.shape[2]
    row_blocks = 2 * col_blocks
    local_rows = slot_rows[0, 0]
    local_cols = slot_cols[0, 0]
    global_rows = local_rows // 2 * stride + 2 * row_index + local_rows % 2
    global_cols = local_cols * stride + col_index
    off_diagonal = (global_rows != global_cols).astype(F32)
    living = (jnp.arange(slot_total) < slot_count[0, 0]).astype(F32)
    row_pick = (local_rows[:, None] == jnp.arange(row_blocks)[None, :]).astype(F32) * living[:, None]
    col_pick = (local_cols[:, None] == jnp.arange(col_blocks)[None, :]).astype(F32) * (
        living * off_diagonal
    )[:, None]
    classes = class_contrast.shape[0]
    lookup = (cell_class[:, 0, :, None] == jnp.arange(classes)[None, None, :]).astype(F32)
    values = jnp.einsum("bte,ec->btc", lookup, class_contrast, precision=lax.Precision.HIGHEST)
    contrast_re = jnp.tile(values[:, :, 0], (1, 3))
    contrast_im = jnp.tile(values[:, :, 1], (1, 3))
    start_field = background[:, :, :, 0, :]
    field_now = start_field
    current = complex_scale(field_now, contrast_re, contrast_im)
    for step_index in range(PRODUCTS):
        final_step = step_index + 1 == PRODUCTS
        halves = [from_root(current, "col", 2 * row_index + parity) for parity in range(2)]
        row_current = jnp.stack(halves, axis=3).reshape(2, sources, row_blocks, entries)
        direct_in = jnp.take(current, local_cols, axis=2)
        mirror_in = jnp.take(row_current, local_rows, axis=2)
        direct_terms = combine(
            jnp.einsum("sqoi,pksi->qpkso", green_tiles, direct_in, preferred_element_type=F32)
        )
        mirror_terms = combine(
            jnp.einsum("sqoi,pkso->qpksi", green_tiles, mirror_in, preferred_element_type=F32)
        )
        direct_part = jnp.einsum(
            "pkse,sb->pkbe", direct_terms, row_pick, precision=lax.Precision.HIGHEST
        )
        mirror_part = jnp.einsum(
            "pkse,sb->pkbe", mirror_terms, col_pick, precision=lax.Precision.HIGHEST
        )
        row_total = lax.psum(direct_part, "col")
        owned_part = lax.dynamic_index_in_dim(
            row_total.reshape(2, sources, col_blocks, 2, entries),
            col_index % 2,
            axis=3,
            keepdims=False,
        )
        direct_here = from_root(owned_part, "row", col_index // 2)
        column_total = lax.psum(mirror_part, "row")
        field_now = start_field + column_total + direct_here
        if not final_step:
            current = complex_scale(field_now, contrast_re, contrast_im)
    return field_now[:, :, :, None, :]


def turned(value):
    shape = value.shape
    tiles = value.reshape(shape[0] // 8, 8, shape[1])
    return jnp.concatenate([-tiles[:, 4:], tiles[:, :4]], axis=1).reshape(shape)


def put_block(xs_ref, at, value):
    entries = value.shape[1]
    xs_ref[at, :, :entries] = value.astype(BF)
    xs_ref[at, :, entries:] = turned(value).astype(BF)


def unpack_half(msg_ref, q, half, xs_ref, at):
    groups = xs_ref.shape[1] // 8
    tail = xs_ref.shape[2] // 2 - 2 * LANES
    pieces = []
    for piece in range(2):
        both = msg_ref[q * groups : (q + 1) * groups, piece * 16 : piece * 16 + 16, :].astype(F32)
        pieces.append(both[:, half * 8 : half * 8 + 8, :].reshape(groups * 8, LANES))
    ends = msg_ref[q * groups : (q + 1) * groups, 32:40, :].astype(F32).reshape(groups * 8, LANES)
    if half:
        ends = pltpu.roll(ends, LANES - tail, 1)
    put_block(xs_ref, at, jnp.concatenate(pieces + [ends[:, :tail]], axis=1))


def copy_in(x_ref, xs_ref, offset):
    for q in range(x_ref.shape[0]):
        put_block(xs_ref, offset + q, x_ref[q].astype(F32))


def slot_products(table_ref, g_ref, xs_ref, acc_ref, mirror, cols):
    acc_ref[...] = jnp.zeros_like(acc_ref)
    slots, _, depth, entries = g_ref.shape
    r = table_ref[3, 0]
    c = table_ref[4, 0]
    blocks = (acc_ref.shape[0] - 1) // (1 if mirror else 2)
    for s in range(slots):
        local_row = table_ref[0, s]
        local_col = table_ref[1, s]
        living = s < table_ref[2, 0]
        half = local_row // 2
        place = (local_row % 2 ^ c % 2) * blocks + half
        if mirror:
            off_diagonal = half * cols + 2 * r + local_row % 2 != local_col * cols + c
            both = g_ref[s].reshape(2 * depth, entries)
            value = jnp.dot(xs_ref[place], both, preferred_element_type=F32)
            acc_ref[jnp.where(living & off_diagonal, local_col, blocks)] += value
        else:
            over = (((1,), (1,)), ((), ()))
            left = xs_ref[local_col, :, :entries]
            value = lax.dot_general(left, g_ref[s, 0], over, preferred_element_type=F32)
            left = xs_ref[local_col, :, entries:]
            value += lax.dot_general(left, g_ref[s, 1], over, preferred_element_type=F32)
            acc_ref[jnp.where(living, place, 2 * blocks)] += value


def start_kernel(classes, small_ref, back_ref, out_ref, contrast_ref):
    blocks = out_ref.shape[0]
    cells = contrast_ref.shape[2]
    kinds = small_ref[0:blocks, :cells]
    tables = small_ref[blocks : blocks + 2, :]
    contrast = []
    for part in range(2):
        value = jnp.zeros(kinds.shape, F32)
        for k in range(classes):
            value = jnp.where(kinds == float(k), tables[part : part + 1, k : k + 1], value)
        contrast_ref[part] = value
        contrast.append(jnp.concatenate([value] * 3, axis=1))
    real, imag = contrast
    for q in range(blocks):
        back = back_ref[q]
        out_ref[q] = (real[q : q + 1] * back + imag[q : q + 1] * turned(back)).astype(BF)


def share_kernel(table_ref, contrast_ref, back_ref, extra_ref):
    r = table_ref[3, 0]
    blocks, rows, entries = back_ref.shape
    half = LANES // 2
    cells = contrast_ref.shape[2]
    lane = lax.broadcasted_iota(jnp.int32, (8, LANES), 1)
    for q in range(blocks):
        marks = []
        for part in range(2):
            value = contrast_ref[part, q : q + 1]
            for _ in range(3):
                piece = value.astype(BF).astype(F32)
                marks.append(piece)
                value = value - piece
        marks = jnp.concatenate(marks + [jnp.zeros((2, cells), F32)], axis=0)
        marks = jnp.concatenate([marks, jnp.zeros((8, LANES - cells), F32)], axis=1)
        marks = jnp.where(r == 1, pltpu.roll(marks, half, 1), marks)
        for g in range(rows // 8):
            at = slice(g * 8, g * 8 + 8)
            value = jnp.where(r % 2 == 0, back_ref[q, at, :LANES], back_ref[q, at, LANES : 2 * LANES])
            high = value.astype(BF).astype(F32)
            value = jnp.where(r < 2, high, value - high)
            last = back_ref[q, at, 2 * LANES :]
            high = last.astype(BF).astype(F32)
            ends = jnp.concatenate([jnp.zeros((8, half), F32), high, last - high], axis=1)
            beside = jnp.where(r == 0, ends, jnp.where(r == 3, jnp.zeros_like(ends), marks))
            beside = jnp.where(lane < half, 0.0, beside)
            extra_ref[q * rows // 8 + g] = jnp.concatenate([beside, value], axis=0).astype(BF)


def direct_kernel(first, table_ref, g_ref, x_ref, own_ref, other_ref, xs_ref, acc_ref):
    blocks = own_ref.shape[0]
    if first:
        copy_in(x_ref, xs_ref, 0)
    else:
        for q in range(blocks):
            unpack_half(x_ref, q, 0, xs_ref, q)
    slot_products(table_ref, g_ref, xs_ref, acc_ref, False, 0)
    for q in range(blocks):
        own_ref[q] = acc_ref[q]
        other_ref[q] = acc_ref[blocks + q]


def mirror_kernel(first, cols, table_ref, g_ref, x_ref, x_other_ref, out_ref, xs_ref, acc_ref):
    blocks = out_ref.shape[0]
    if first:
        copy_in(x_ref, xs_ref, 0)
        copy_in(x_other_ref, xs_ref, blocks)
    else:
        for q in range(blocks):
            unpack_half(x_ref, q, 1, xs_ref, q)
            unpack_half(x_other_ref, q, 1, xs_ref, blocks + q)
    slot_products(table_ref, g_ref, xs_ref, acc_ref, True, cols)
    for q in range(blocks):
        out_ref[q] = acc_ref[q]


def pack_kernel(mirror_ref, own_ref, got_ref, *rest):
    msg_ref = rest[-1]
    blocks, rows, entries = own_ref.shape
    groups = rows // 8
    tail = entries - 2 * LANES
    for q in range(blocks):
        at = slice(q * groups, (q + 1) * groups)
        for piece in range(2):
            lanes = slice(piece * LANES, (piece + 1) * LANES)
            direct = (own_ref[q, :, lanes] + got_ref[q, :, lanes]).reshape(groups, 8, LANES)
            mirror = mirror_ref[q, :, lanes].reshape(groups, 8, LANES)
            start = piece * 16
            msg_ref[at, start : start + 16, :] = jnp.concatenate([direct, mirror], axis=1).astype(BF)
        lanes = slice(2 * LANES, entries)
        direct = own_ref[q, :, lanes] + got_ref[q, :, lanes]
        mirror = mirror_ref[q, :, lanes]
        filler = jnp.zeros((rows, LANES - 2 * tail), F32)
        ends = jnp.concatenate([direct, mirror, filler], axis=1).reshape(groups, 8, LANES)
        if len(rest) == 2:
            extra = rest[0][at].astype(F32)
            ends = jnp.concatenate([ends + extra[:, :8], extra[:, 8:]], axis=1)
        msg_ref[at, 32 : 32 + ends.shape[1], :] = ends.astype(BF)


def update_kernel(first, rows, cols, tail, msg_ref, *refs):
    back_ref, contrast_ref, out_ref = refs[1:] + refs[:1] if first else refs
    lane = lax.broadcasted_iota(jnp.int32, (8, LANES), 1)
    sign = jnp.where(lax.broadcasted_iota(jnp.int32, (8, LANES), 0) < 4, -1.0, 1.0)
    sums, ends = partial_sums(msg_ref, rows, cols, tail)
    half = LANES // 2
    cells = (2 * LANES + tail) // 3
    current = {}
    for j in range(cols):
        if first:
            parts = [msg_ref[r * cols + j, 40:48, :].astype(F32) for r in range(4)]
            beside = [ends[r * cols + j] for r in range(3)]
            last = pltpu.roll(beside[0], half, 1) + pltpu.roll(beside[0], half - tail, 1)
            background = [parts[0] + parts[2], parts[1] + parts[3], last]
            marks = jnp.where(lane < half, pltpu.roll(beside[1], half, 1), beside[2])
            contrast = []
            for start in (0, 3):
                value = marks[start : start + 1] + marks[start + 1 : start + 2] + marks[start + 2 : start + 3]
                value = jnp.broadcast_to(value, (8, LANES))
                contrast.append(
                    [
                        jnp.where(lane < cells, value, pltpu.roll(value, cells, 1)),
                        jnp.where(lane < half, pltpu.roll(value, cells, 1), pltpu.roll(value, half, 1)),
                        pltpu.roll(value, half, 1),
                    ]
                )
        for piece in range(3):
            if first:
                back, real, imag = background[piece], contrast[0][piece], contrast[1][piece] * sign
                back_ref[j, piece] = back
                contrast_ref[j, 0, piece] = real
                contrast_ref[j, 1, piece] = imag
            else:
                back, real, imag = back_ref[j, piece], contrast_ref[j, 0, piece], contrast_ref[j, 1, piece]
            total = sums[j, piece] + back
            current[j, piece] = real * total + imag * pltpu.roll(total, 4, 0)
    for r in range(rows):
        for c in range(cols):
            d = r * cols + c
            k = 2 * r + c % 2
            for piece in range(2):
                out_ref[d, piece * 16 : piece * 16 + 16, :] = jnp.concatenate(
                    [current[c, piece], current[k, piece]], axis=0
                ).astype(BF)
            ends = jnp.where(lane < tail, current[c, 2], pltpu.roll(current[k, 2], tail, 1))
            out_ref[d, 32:40, :] = ends.astype(BF)


def partial_sums(msg_ref, rows, cols, tail):
    direct = {}
    mirror = {}
    tails = []

    def add(store, key, value):
        store[key] = store[key] + value if key in store else value

    for r in range(rows):
        for c in range(cols):
            d = r * cols + c
            j = 2 * r + c % 2
            for piece in range(2):
                both = msg_ref[d, piece * 16 : piece * 16 + 16, :].astype(F32)
                add(direct, (j, piece), both[:8])
                add(mirror, (c, piece), both[8:])
            ends = msg_ref[d, 32:40, :].astype(F32)
            tails.append(ends)
            add(direct, (j, 2), ends)
            add(mirror, (c, 2), ends)
    for j in range(cols):
        mirror[j, 2] = pltpu.roll(mirror[j, 2], LANES - tail, 1)
    return {key: direct[key] + mirror[key] for key in direct}, tails


def last_kernel(rows, cols, tail, msg_ref, out_ref):
    lane = lax.broadcasted_iota(jnp.int32, (8, LANES), 1)
    sums, _ = partial_sums(msg_ref, rows, cols, tail)
    for j in range(cols):
        pieces = [sums[j, 0], sums[j, 1], jnp.where(lane < tail, sums[j, 2], 0.0)]
        most = jnp.maximum(jnp.maximum(jnp.abs(pieces[0]), jnp.abs(pieces[1])), jnp.abs(pieces[2]))
        most = jnp.max(most, axis=1, keepdims=True)
        power = jnp.floor(jnp.log2(jnp.maximum(most, SMALLEST)))
        scale = jnp.exp2(14.0 - power)
        coded = [jnp.clip(jnp.round(piece * scale), -32767.0, 32767.0) for piece in pieces]
        coded[2] = jnp.where(lane == tail, power, coded[2])
        coded = [piece.astype(jnp.int32) for piece in coded]
        main = jnp.concatenate(coded[:2], axis=0).astype(jnp.int16)
        last = coded[2].astype(jnp.int16)
        for r in range(rows):
            out_ref[r * cols + j, 0:16, :] = main
            out_ref[r * cols + j, 16:24, :] = last


def finish_kernel(msg_ref, back_ref, out_ref):
    blocks, rows, entries = out_ref.shape
    groups = rows // 8
    tail = entries - 2 * LANES
    for q in range(blocks):
        at = slice(q * groups, (q + 1) * groups)
        main = msg_ref[at, 0:16, :].astype(jnp.int32).astype(F32)
        last = msg_ref[at, 16:24, :].astype(jnp.int32).astype(F32).reshape(rows, LANES)
        scale = jnp.exp2(last[:, tail : tail + 1] - 14.0)
        for piece in range(2):
            lanes = slice(piece * LANES, (piece + 1) * LANES)
            value = main[:, piece * 8 : piece * 8 + 8, :].reshape(rows, LANES)
            out_ref[q, :, lanes] = back_ref[q, :, lanes] + value * scale
        lanes = slice(2 * LANES, entries)
        out_ref[q, :, lanes] = back_ref[q, :, lanes] + last[:, :tail] * scale


def whole_call(kernel, out_shape, spaces, operands, scratch, name):
    spaces = list(spaces) + [pltpu.VMEM] * (len(operands) - len(spaces))
    return pl.pallas_call(
        kernel,
        out_shape=out_shape,
        in_specs=[pl.BlockSpec(memory_space=space) for space in spaces],
        out_specs=jax.tree.map(lambda _: pl.BlockSpec(memory_space=pltpu.VMEM), out_shape),
        scratch_shapes=scratch,
        compiler_params=pltpu.CompilerParams(vmem_limit_bytes=VMEM_BYTES),
        name=name,
    )(*operands)


def stacked(arrays, dtype):
    rows = sum(array.shape[0] for array in arrays)
    total = 0
    at = 0
    for array in arrays:
        height, width = array.shape
        total += lax.pad(
            array,
            jnp.zeros((), array.dtype),
            ((at, rows - at - height, 0), (0, LANES - width, 0)),
        ).astype(dtype)
        at += height
    return total


def local_owners(green_blocks, slot_rows, slot_cols, slot_count, cell_class, class_contrast, background):
    r = lax.axis_index("row")
    c = lax.axis_index("col")
    rows = lax.axis_size("row")
    cols = lax.axis_size("col")
    green = green_blocks[0, 0]
    slots, _, entries, _ = green.shape
    sources, blocks = background.shape[1:3]
    groups = sources // 4
    tail = entries - 2 * LANES
    both = ("row", "col")

    floats = stacked([cell_class[:, 0, :], class_contrast.T], F32)
    here = jnp.stack([r, c]).astype(jnp.int32)[:, None]
    table = stacked([slot_rows[0], slot_cols[0], slot_count, here], jnp.int32)

    block = (groups * 8, entries)
    back = background[:, :, :, 0, :].reshape(2, groups, 4, blocks, entries)
    back = back.transpose(3, 1, 0, 2, 4).reshape((blocks,) + block)
    start, contrast = whole_call(
        lambda *refs: start_kernel(class_contrast.shape[0], *refs),
        (
            jax.ShapeDtypeStruct((blocks,) + block, BF),
            jax.ShapeDtypeStruct((2, blocks, entries // 3), F32),
        ),
        [],
        (floats, back),
        [],
        "start",
    )

    core_pairs = [(i, i ^ 1) for i in range(cols)]
    arrived = []
    for hop in range(1, cols // 2):
        pairs = [
            (a * cols + 2 * a + p, a * cols + 2 * ((a + hop) % (cols // 2)) + p)
            for a in range(rows)
            for p in range(2)
        ]
        arrived.append(lax.ppermute(start, both, pairs))
    row_mine = jnp.where(c // 2 == r, start, sum(arrived))
    row_other = lax.ppermute(row_mine, "col", core_pairs)

    extra = whole_call(
        share_kernel,
        jax.ShapeDtypeStruct((rows * cols, 16, LANES), BF),
        [pltpu.SMEM],
        (table, contrast, back),
        [],
        "share",
    )
    part = jax.ShapeDtypeStruct((blocks,) + block, F32)
    message = jax.ShapeDtypeStruct((rows * cols, 40, LANES), BF)
    for step in range(PRODUCTS):
        first = step == 0
        final = step + 1 == PRODUCTS
        if first:
            direct_in, mirror_in = start, (row_mine, row_other)
        else:
            direct_in, mirror_in = x_msg, (x_msg, lax.ppermute(x_msg, "col", core_pairs))
        own, other = whole_call(
            lambda *refs, first=first: direct_kernel(first, *refs),
            (part, part),
            [pltpu.SMEM],
            (table, green, direct_in),
            [
                pltpu.VMEM((blocks, groups * 8, 2 * entries), BF),
                pltpu.VMEM((2 * blocks + 1,) + block, F32),
            ],
            f"direct_{step}",
        )
        got = lax.ppermute(other, "col", core_pairs)
        mirror = whole_call(
            lambda *refs, first=first: mirror_kernel(first, cols, *refs),
            part,
            [pltpu.SMEM],
            (table, green) + mirror_in,
            [
                pltpu.VMEM((2 * blocks, groups * 8, 2 * entries), BF),
                pltpu.VMEM((blocks + 1,) + block, F32),
            ],
            f"mirror_{step}",
        )
        y_shape = jax.ShapeDtypeStruct((rows * cols, 48, LANES), BF) if first else message
        operands = (mirror, own, got) + ((extra,) if first else ())
        y_msg = whole_call(pack_kernel, y_shape, [], operands, [], f"pack_{step}")
        y_msg = lax.all_to_all(y_msg, both, 0, 0, tiled=True)
        run = lambda *refs, first=first: update_kernel(first, rows, cols, tail, *refs)
        if first:
            x_msg, owner_back, owner_contrast = whole_call(
                run,
                (
                    message,
                    jax.ShapeDtypeStruct((cols, 3, 8, LANES), F32),
                    jax.ShapeDtypeStruct((cols, 2, 3, 8, LANES), F32),
                ),
                [],
                (y_msg,),
                [],
                f"update_{step}",
            )
        elif not final:
            operands = (y_msg, owner_back, owner_contrast)
            x_msg = whole_call(run, message, [], operands, [], f"update_{step}")
        else:
            run = lambda *refs: last_kernel(rows, cols, tail, *refs)
            x_shape = jax.ShapeDtypeStruct((rows * cols, 24, LANES), jnp.int16)
            x_msg = whole_call(run, x_shape, [], (y_msg,), [], "last")
        x_msg = lax.all_to_all(x_msg, both, 0, 0, tiled=True)
    field = whole_call(finish_kernel, part, [], (x_msg, back), [], "finish")
    field = field.reshape(blocks, groups, 2, 4, entries).transpose(2, 1, 3, 0, 4)
    return field.reshape(2, sources, blocks, 1, entries)


def solution(mesh):
    in_specs = (
        P("row", "col", None, None, None, None),
        P("row", "col", None),
        P("row", "col", None),
        P("row", "col"),
        P(None, "col", None),
        P(),
        P(None, None, None, "col", None),
    )
    out_specs = P(None, None, None, "col", None)
    rows, cols = mesh.shape["row"], mesh.shape["col"]

    def local(*args):
        sources, blocks = args[6].shape[1:3]
        entries = args[6].shape[4]
        owners = (
            rows == blocks == 4
            and cols == 2 * rows
            and sources == 4 * cols
            and max(args[5].shape[0], args[1].shape[2]) <= LANES
            and entries == 2 * LANES + LANES // 4 == 3 * args[4].shape[2]
        )
        return (local_owners if owners else local_general)(*args)

    return jax.shard_map(local, mesh=mesh, in_specs=in_specs, out_specs=out_specs, check_vma=False)
```

```python
import jax
import jax.numpy as jnp
from jax import lax
from jax.experimental import pallas as pl
from jax.experimental.pallas import tpu as pltpu
from jax.sharding import PartitionSpec as P

PRODUCTS = 3
LANES = 128
SMALLEST = 2.0**-100
VMEM_BYTES = 8 * 1024 * 1024
BF = jnp.bfloat16
F32 = jnp.float32


def from_root(array, axis, root):
    mine = lax.axis_index(axis) == root
    return lax.psum(jnp.where(mine, array, jnp.zeros_like(array)), axis)


def complex_scale(field_now, contrast_re, contrast_im):
    real_part = field_now[0]
    imag_part = field_now[1]
    scaled = jnp.stack(
        [
            contrast_re * real_part - contrast_im * imag_part,
            contrast_re * imag_part + contrast_im * real_part,
        ]
    )
    return scaled.astype(BF)


def combine(products):
    return jnp.stack([products[0, 0] - products[1, 1], products[0, 1] + products[1, 0]])


def local_general(green_blocks, slot_rows, slot_cols, slot_count, cell_class, class_contrast, background):
    row_index = lax.axis_index("row")
    col_index = lax.axis_index("col")
    stride = lax.axis_size("col")
    green_tiles = green_blocks[0, 0]
    slot_total = green_tiles.shape[0]
    entries = green_tiles.shape[-1]
    sources = background.shape[1]
    col_blocks = background.shape[2]
    row_blocks = 2 * col_blocks
    local_rows = slot_rows[0, 0]
    local_cols = slot_cols[0, 0]
    global_rows = local_rows // 2 * stride + 2 * row_index + local_rows % 2
    global_cols = local_cols * stride + col_index
    off_diagonal = (global_rows != global_cols).astype(F32)
    living = (jnp.arange(slot_total) < slot_count[0, 0]).astype(F32)
    row_pick = (local_rows[:, None] == jnp.arange(row_blocks)[None, :]).astype(F32) * living[:, None]
    col_pick = (local_cols[:, None] == jnp.arange(col_blocks)[None, :]).astype(F32) * (
        living * off_diagonal
    )[:, None]
    classes = class_contrast.shape[0]
    lookup = (cell_class[:, 0, :, None] == jnp.arange(classes)[None, None, :]).astype(F32)
    values = jnp.einsum("bte,ec->btc", lookup, class_contrast, precision=lax.Precision.HIGHEST)
    contrast_re = jnp.tile(values[:, :, 0], (1, 3))
    contrast_im = jnp.tile(values[:, :, 1], (1, 3))
    start_field = background[:, :, :, 0, :]
    field_now = start_field
    current = complex_scale(field_now, contrast_re, contrast_im)
    for step_index in range(PRODUCTS):
        final_step = step_index + 1 == PRODUCTS
        halves = [from_root(current, "col", 2 * row_index + parity) for parity in range(2)]
        row_current = jnp.stack(halves, axis=3).reshape(2, sources, row_blocks, entries)
        direct_in = jnp.take(current, local_cols, axis=2)
        mirror_in = jnp.take(row_current, local_rows, axis=2)
        direct_terms = combine(
            jnp.einsum("sqoi,pksi->qpkso", green_tiles, direct_in, preferred_element_type=F32)
        )
        mirror_terms = combine(
            jnp.einsum("sqoi,pkso->qpksi", green_tiles, mirror_in, preferred_element_type=F32)
        )
        direct_part = jnp.einsum(
            "pkse,sb->pkbe", direct_terms, row_pick, precision=lax.Precision.HIGHEST
        )
        mirror_part = jnp.einsum(
            "pkse,sb->pkbe", mirror_terms, col_pick, precision=lax.Precision.HIGHEST
        )
        row_total = lax.psum(direct_part, "col")
        owned_part = lax.dynamic_index_in_dim(
            row_total.reshape(2, sources, col_blocks, 2, entries),
            col_index % 2,
            axis=3,
            keepdims=False,
        )
        direct_here = from_root(owned_part, "row", col_index // 2)
        column_total = lax.psum(mirror_part, "row")
        field_now = start_field + column_total + direct_here
        if not final_step:
            current = complex_scale(field_now, contrast_re, contrast_im)
    return field_now[:, :, :, None, :]


def turned(value):
    shape = value.shape
    tiles = value.reshape(shape[0] // 8, 8, shape[1])
    return jnp.concatenate([-tiles[:, 4:], tiles[:, :4]], axis=1).reshape(shape)


def put_block(xs_ref, at, value, mirror):
    entries = value.shape[1]
    main = 2 * LANES
    both = [value.astype(BF), turned(value).astype(BF)]
    if mirror:
        xs_ref[at, :, :entries] = both[0]
        xs_ref[at, :, entries:] = both[1]
    else:
        xs_ref[at, :, :main] = both[0][:, :main]
        xs_ref[at, :, main : 2 * main] = both[1][:, :main]
        xs_ref[at, :, 2 * main :] = jnp.concatenate([part[:, main:] for part in both], axis=1)


def unpack_half(msg_ref, q, half, xs_ref, at):
    groups = xs_ref.shape[1] // 8
    tail = xs_ref.shape[2] // 2 - 2 * LANES
    pieces = []
    for piece in range(2):
        both = msg_ref[q * groups : (q + 1) * groups, piece * 16 : piece * 16 + 16, :].astype(F32)
        pieces.append(both[:, half * 8 : half * 8 + 8, :].reshape(groups * 8, LANES))
    ends = msg_ref[q * groups : (q + 1) * groups, 32:40, :].astype(F32).reshape(groups * 8, LANES)
    if half:
        ends = pltpu.roll(ends, LANES - tail, 1)
    put_block(xs_ref, at, jnp.concatenate(pieces + [ends[:, :tail]], axis=1), half)


def copy_in(x_ref, xs_ref, offset, mirror):
    for q in range(x_ref.shape[0]):
        put_block(xs_ref, offset + q, x_ref[q].astype(F32), mirror)


def across(left, right):
    return lax.dot_general(left, right, (((1,), (1,)), ((), ())), preferred_element_type=F32)


def slot_products(count_ref, table_ref, g_ref, xs_ref, acc_ref, mirror, cols):
    acc_ref[...] = jnp.zeros_like(acc_ref)
    slots, _, depth, entries = g_ref.shape
    r, c = [table_ref[row, 0].astype(jnp.int32) for row in (2, 3)]
    count = count_ref[0, 0]
    blocks = (acc_ref.shape[0] - 1) // (1 if mirror else 2)
    for s in range(slots):
        local_row = table_ref[0, s].astype(jnp.int32)
        local_col = table_ref[1, s].astype(jnp.int32)
        living = s < count
        half = local_row // 2
        place = (local_row % 2 ^ c % 2) * blocks + half
        if mirror:
            off_diagonal = half * cols + 2 * r + local_row % 2 != local_col * cols + c
            both = g_ref[s].reshape(2 * depth, entries)
            value = jnp.dot(xs_ref[place], both, preferred_element_type=F32)
            acc_ref[jnp.where(living & off_diagonal, local_col, blocks)] += value
        else:
            main = 2 * LANES
            left = xs_ref[local_col]
            ends = jnp.concatenate([g_ref[s, 0, :, main:], g_ref[s, 1, :, main:]], axis=1)
            value = across(left[:, :main], g_ref[s, 0, :, :main])
            value += across(left[:, main : 2 * main], g_ref[s, 1, :, :main])
            value += across(left[:, 2 * main :], ends)
            acc_ref[jnp.where(living, place, 2 * blocks)] += value


def start_kernel(classes, small_ref, back_ref, out_ref, contrast_ref):
    blocks = out_ref.shape[0]
    cells = contrast_ref.shape[2]
    kinds = small_ref[4 : 4 + blocks, :cells]
    tables = small_ref[4 + blocks : 6 + blocks, :]
    contrast = []
    for part in range(2):
        value = jnp.zeros(kinds.shape, F32)
        for k in range(classes):
            value = jnp.where(kinds == float(k), tables[part : part + 1, k : k + 1], value)
        contrast_ref[part] = value
        contrast.append(jnp.concatenate([value] * 3, axis=1))
    real, imag = contrast
    for q in range(blocks):
        back = back_ref[q]
        out_ref[q] = (real[q : q + 1] * back + imag[q : q + 1] * turned(back)).astype(BF)


def share_kernel(table_ref, contrast_ref, back_ref, _, extra_ref):
    r = table_ref[2, 0].astype(jnp.int32)
    blocks, rows, entries = back_ref.shape
    half = LANES // 2
    cells = contrast_ref.shape[2]
    lane = lax.broadcasted_iota(jnp.int32, (8, LANES), 1)
    for q in range(blocks):
        marks = []
        for part in range(2):
            value = contrast_ref[part, q : q + 1]
            for _ in range(3):
                piece = value.astype(BF).astype(F32)
                marks.append(piece)
                value = value - piece
        marks = jnp.concatenate(marks + [jnp.zeros((2, cells), F32)], axis=0)
        marks = jnp.concatenate([marks, jnp.zeros((8, LANES - cells), F32)], axis=1)
        marks = jnp.where(r == 1, pltpu.roll(marks, half, 1), marks)
        for g in range(rows // 8):
            at = slice(g * 8, g * 8 + 8)
            value = jnp.where(r % 2 == 0, back_ref[q, at, :LANES], back_ref[q, at, LANES : 2 * LANES])
            high = value.astype(BF).astype(F32)
            value = jnp.where(r < 2, high, value - high)
            last = back_ref[q, at, 2 * LANES :]
            high = last.astype(BF).astype(F32)
            ends = jnp.concatenate([jnp.zeros((8, half), F32), high, last - high], axis=1)
            beside = jnp.where(r == 0, ends, jnp.where(r == 3, jnp.zeros_like(ends), marks))
            beside = jnp.where(lane < half, 0.0, beside)
            extra_ref[q * rows // 8 + g] = jnp.concatenate([beside, value], axis=0).astype(BF)


def direct_kernel(first, count_ref, table_ref, g_ref, x_ref, own_ref, other_ref, xs_ref, acc_ref):
    blocks = own_ref.shape[0]
    if first:
        copy_in(x_ref, xs_ref, 0, False)
    else:
        for q in range(blocks):
            unpack_half(x_ref, q, 0, xs_ref, q)
    slot_products(count_ref, table_ref, g_ref, xs_ref, acc_ref, False, 0)
    for q in range(blocks):
        own_ref[q] = acc_ref[q]
        other_ref[q] = acc_ref[blocks + q]


def mirror_kernel(first, cols, count_ref, table_ref, g_ref, x_ref, x_other_ref, out_ref, xs_ref, acc_ref):
    blocks = out_ref.shape[0]
    if first:
        copy_in(x_ref, xs_ref, 0, True)
        copy_in(x_other_ref, xs_ref, blocks, True)
    else:
        for q in range(blocks):
            unpack_half(x_ref, q, 1, xs_ref, q)
            unpack_half(x_other_ref, q, 1, xs_ref, blocks + q)
    slot_products(count_ref, table_ref, g_ref, xs_ref, acc_ref, True, cols)
    for q in range(blocks):
        out_ref[q] = acc_ref[q]


def pack_kernel(mirror_ref, own_ref, got_ref, *rest):
    msg_ref = rest[-1]
    blocks, rows, entries = own_ref.shape
    groups = rows // 8
    tail = entries - 2 * LANES
    for q in range(blocks):
        at = slice(q * groups, (q + 1) * groups)
        for piece in range(2):
            lanes = slice(piece * LANES, (piece + 1) * LANES)
            direct = (own_ref[q, :, lanes] + got_ref[q, :, lanes]).reshape(groups, 8, LANES)
            mirror = mirror_ref[q, :, lanes].reshape(groups, 8, LANES)
            start = piece * 16
            msg_ref[at, start : start + 16, :] = jnp.concatenate([direct, mirror], axis=1).astype(BF)
        lanes = slice(2 * LANES, entries)
        direct = own_ref[q, :, lanes] + got_ref[q, :, lanes]
        mirror = mirror_ref[q, :, lanes]
        filler = jnp.zeros((rows, LANES - 2 * tail), F32)
        ends = jnp.concatenate([direct, mirror, filler], axis=1).reshape(groups, 8, LANES)
        if len(rest) == 2:
            extra = rest[0][at].astype(F32)
            ends = jnp.concatenate([ends + extra[:, :8], extra[:, 8:]], axis=1)
        msg_ref[at, 32 : 32 + ends.shape[1], :] = ends.astype(BF)


def update_kernel(first, rows, cols, tail, msg_ref, *refs):
    back_ref, contrast_ref, out_ref = refs[1:] + refs[:1] if first else refs
    lane = lax.broadcasted_iota(jnp.int32, (8, LANES), 1)
    sign = jnp.where(lax.broadcasted_iota(jnp.int32, (8, LANES), 0) < 4, -1.0, 1.0)
    sums, ends = partial_sums(msg_ref, rows, cols, tail)
    half = LANES // 2
    cells = (2 * LANES + tail) // 3
    current = {}
    for j in range(cols):
        if first:
            parts = [msg_ref[r * cols + j, 40:48, :].astype(F32) for r in range(4)]
            beside = [ends[r * cols + j] for r in range(3)]
            last = pltpu.roll(beside[0], half, 1) + pltpu.roll(beside[0], half - tail, 1)
            background = [parts[0] + parts[2], parts[1] + parts[3], last]
            marks = jnp.where(lane < half, pltpu.roll(beside[1], half, 1), beside[2])
            contrast = []
            for start in (0, 3):
                value = marks[start : start + 1] + marks[start + 1 : start + 2] + marks[start + 2 : start + 3]
                value = jnp.broadcast_to(value, (8, LANES))
                contrast.append(
                    [
                        jnp.where(lane < cells, value, pltpu.roll(value, cells, 1)),
                        jnp.where(lane < half, pltpu.roll(value, cells, 1), pltpu.roll(value, half, 1)),
                        pltpu.roll(value, half, 1),
                    ]
                )
        for piece in range(3):
            if first:
                back, real, imag = background[piece], contrast[0][piece], contrast[1][piece] * sign
                back_ref[j, piece] = back
                contrast_ref[j, 0, piece] = real
                contrast_ref[j, 1, piece] = imag
            else:
                back, real, imag = back_ref[j, piece], contrast_ref[j, 0, piece], contrast_ref[j, 1, piece]
            total = sums[j, piece] + back
            current[j, piece] = real * total + imag * pltpu.roll(total, 4, 0)
    for r in range(rows):
        for c in range(cols):
            d = r * cols + c
            k = 2 * r + c % 2
            for piece in range(2):
                out_ref[d, piece * 16 : piece * 16 + 16, :] = jnp.concatenate(
                    [current[c, piece], current[k, piece]], axis=0
                ).astype(BF)
            ends = jnp.where(lane < tail, current[c, 2], pltpu.roll(current[k, 2], tail, 1))
            out_ref[d, 32:40, :] = ends.astype(BF)


def partial_sums(msg_ref, rows, cols, tail):
    direct = {}
    mirror = {}
    tails = []

    def add(store, key, value):
        store[key] = store[key] + value if key in store else value

    for r in range(rows):
        for c in range(cols):
            d = r * cols + c
            j = 2 * r + c % 2
            for piece in range(2):
                both = msg_ref[d, piece * 16 : piece * 16 + 16, :].astype(F32)
                add(direct, (j, piece), both[:8])
                add(mirror, (c, piece), both[8:])
            ends = msg_ref[d, 32:40, :].astype(F32)
            tails.append(ends)
            add(direct, (j, 2), ends)
            add(mirror, (c, 2), ends)
    for j in range(cols):
        mirror[j, 2] = pltpu.roll(mirror[j, 2], LANES - tail, 1)
    return {key: direct[key] + mirror[key] for key in direct}, tails


def last_kernel(rows, cols, tail, msg_ref, out_ref):
    lane = lax.broadcasted_iota(jnp.int32, (8, LANES), 1)
    sums, _ = partial_sums(msg_ref, rows, cols, tail)
    for j in range(cols):
        pieces = [sums[j, 0], sums[j, 1], jnp.where(lane < tail, sums[j, 2], 0.0)]
        most = jnp.maximum(jnp.maximum(jnp.abs(pieces[0]), jnp.abs(pieces[1])), jnp.abs(pieces[2]))
        most = jnp.max(most, axis=1, keepdims=True)
        power = jnp.floor(jnp.log2(jnp.maximum(most, SMALLEST)))
        scale = jnp.exp2(14.0 - power)
        coded = [jnp.clip(jnp.round(piece * scale), -32767.0, 32767.0) for piece in pieces]
        coded[2] = jnp.where(lane == tail, power, coded[2])
        coded = [piece.astype(jnp.int32) for piece in coded]
        main = jnp.concatenate(coded[:2], axis=0).astype(jnp.int16)
        last = coded[2].astype(jnp.int16)
        for r in range(rows):
            out_ref[r * cols + j, 0:16, :] = main
            out_ref[r * cols + j, 16:24, :] = last


def finish_kernel(msg_ref, back_ref, out_ref):
    blocks, rows, entries = out_ref.shape
    groups = rows // 8
    tail = entries - 2 * LANES
    for q in range(blocks):
        at = slice(q * groups, (q + 1) * groups)
        main = msg_ref[at, 0:16, :].astype(jnp.int32).astype(F32)
        last = msg_ref[at, 16:24, :].astype(jnp.int32).astype(F32).reshape(rows, LANES)
        scale = jnp.exp2(last[:, tail : tail + 1] - 14.0)
        for piece in range(2):
            lanes = slice(piece * LANES, (piece + 1) * LANES)
            value = main[:, piece * 8 : piece * 8 + 8, :].reshape(rows, LANES)
            out_ref[q, :, lanes] = back_ref[q, :, lanes] + value * scale
        lanes = slice(2 * LANES, entries)
        out_ref[q, :, lanes] = back_ref[q, :, lanes] + last[:, :tail] * scale


def whole_call(kernel, out_shape, spaces, operands, scratch, name):
    spaces = list(spaces) + [pltpu.VMEM] * (len(operands) - len(spaces))
    return pl.pallas_call(
        kernel,
        out_shape=out_shape,
        in_specs=[pl.BlockSpec(memory_space=space) for space in spaces],
        out_specs=jax.tree.map(lambda _: pl.BlockSpec(memory_space=pltpu.VMEM), out_shape),
        scratch_shapes=scratch,
        compiler_params=pltpu.CompilerParams(vmem_limit_bytes=VMEM_BYTES),
        name=name,
    )(*operands)


def stacked(arrays):
    heights = [1 if array is None else array.shape[0] for array in arrays]
    total = 0
    at = 0
    for array, height in zip(arrays, heights):
        if array is not None:
            edges = ((at, sum(heights) - at - height, 0), (0, LANES - array.shape[1], 0))
            total += lax.pad(array, jnp.zeros((), array.dtype), edges).astype(F32)
        at += height
    return total


def local_owners(green_blocks, slot_rows, slot_cols, slot_count, cell_class, class_contrast, background):
    r = lax.axis_index("row")
    c = lax.axis_index("col")
    rows = lax.axis_size("row")
    cols = lax.axis_size("col")
    green = green_blocks[0, 0]
    slots, _, entries, _ = green.shape
    sources, blocks = background.shape[1:3]
    groups = sources // 4
    tail = entries - 2 * LANES
    both = ("row", "col")

    small = stacked([slot_rows[0], slot_cols[0], None, None, cell_class[:, 0, :], class_contrast.T])
    line = lax.broadcasted_iota(jnp.int32, small.shape, 0)
    small = jnp.where(line == 2, r.astype(F32), jnp.where(line == 3, c.astype(F32), small))

    block = (groups * 8, entries)
    back = background[:, :, :, 0, :].reshape(2, groups, 4, blocks, entries)
    back = back.transpose(3, 1, 0, 2, 4).reshape((blocks,) + block)
    start, contrast = whole_call(
        lambda *refs: start_kernel(class_contrast.shape[0], *refs),
        (
            jax.ShapeDtypeStruct((blocks,) + block, BF),
            jax.ShapeDtypeStruct((2, blocks, entries // 3), F32),
        ),
        [],
        (small, back),
        [],
        "start",
    )

    core_pairs = [(i, i ^ 1) for i in range(cols)]
    chips = cols // 2
    arrived = []
    for hop in range(1, chips):
        pairs = []
        for a in range(rows):
            far = (a + hop) % chips
            for k in range(chips):
                for p in range(2):
                    to = {a: 2 * far + p, far: 2 * a + p}.get(k, 2 * k + 1 - p)
                    pairs.append((a * cols + 2 * k + p, a * cols + to))
        arrived.append(lax.ppermute(start, both, pairs))
    extra = whole_call(
        share_kernel,
        jax.ShapeDtypeStruct((rows * cols, 16, LANES), BF),
        [pltpu.SMEM],
        (small, contrast, back, green),
        [],
        "share",
    )
    extra, *arrived = lax.optimization_barrier((extra, *arrived))
    row_mine = start
    for hop in range(1, chips):
        row_mine = jnp.where(c // 2 == (r + hop) % chips, arrived[hop - 1], row_mine)
    row_other = lax.ppermute(row_mine, "col", core_pairs)

    part = jax.ShapeDtypeStruct((blocks,) + block, F32)
    message = jax.ShapeDtypeStruct((rows * cols, 40, LANES), BF)
    for step in range(PRODUCTS):
        first = step == 0
        final = step + 1 == PRODUCTS
        if first:
            direct_in, mirror_in = start, (row_mine, row_other)
        else:
            direct_in, mirror_in = x_msg, (x_msg, lax.ppermute(x_msg, "col", core_pairs))
        own, other = whole_call(
            lambda *refs, first=first: direct_kernel(first, *refs),
            (part, part),
            [pltpu.SMEM] * 2,
            (slot_count, small, green, direct_in),
            [
                pltpu.VMEM((blocks, groups * 8, 2 * entries), BF),
                pltpu.VMEM((2 * blocks + 1,) + block, F32),
            ],
            f"direct_{step}",
        )
        got = lax.ppermute(other, "col", core_pairs)
        mirror = whole_call(
            lambda *refs, first=first: mirror_kernel(first, cols, *refs),
            part,
            [pltpu.SMEM] * 2,
            (slot_count, small, green) + mirror_in,
            [
                pltpu.VMEM((2 * blocks, groups * 8, 2 * entries), BF),
                pltpu.VMEM((blocks + 1,) + block, F32),
            ],
            f"mirror_{step}",
        )
        y_shape = jax.ShapeDtypeStruct((rows * cols, 48, LANES), BF) if first else message
        operands = (mirror, own, got) + ((extra,) if first else ())
        y_msg = whole_call(pack_kernel, y_shape, [], operands, [], f"pack_{step}")
        y_msg = lax.all_to_all(y_msg, both, 0, 0, tiled=True)
        run = lambda *refs, first=first: update_kernel(first, rows, cols, tail, *refs)
        if first:
            x_msg, owner_back, owner_contrast = whole_call(
                run,
                (
                    message,
                    jax.ShapeDtypeStruct((cols, 3, 8, LANES), F32),
                    jax.ShapeDtypeStruct((cols, 2, 3, 8, LANES), F32),
                ),
                [],
                (y_msg,),
                [],
                f"update_{step}",
            )
        elif not final:
            operands = (y_msg, owner_back, owner_contrast)
            x_msg = whole_call(run, message, [], operands, [], f"update_{step}")
        else:
            run = lambda *refs: last_kernel(rows, cols, tail, *refs)
            x_shape = jax.ShapeDtypeStruct((rows * cols, 24, LANES), jnp.int16)
            x_msg = whole_call(run, x_shape, [], (y_msg,), [], "last")
        x_msg = lax.all_to_all(x_msg, both, 0, 0, tiled=True)
    field = whole_call(finish_kernel, part, [], (x_msg, back), [], "finish")
    field = field.reshape(blocks, groups, 2, 4, entries).transpose(2, 1, 3, 0, 4)
    return field.reshape(2, sources, blocks, 1, entries)


def solution(mesh):
    in_specs = (
        P("row", "col", None, None, None, None),
        P("row", "col", None),
        P("row", "col", None),
        P("row", "col"),
        P(None, "col", None),
        P(),
        P(None, None, None, "col", None),
    )
    out_specs = P(None, None, None, "col", None)
    rows, cols = mesh.shape["row"], mesh.shape["col"]

    def local(*args):
        sources, blocks = args[6].shape[1:3]
        entries = args[6].shape[4]
        owners = (
            rows == blocks == 4
            and cols == 2 * rows
            and sources == 4 * cols
            and max(args[5].shape[0], args[1].shape[2]) <= LANES
            and entries == 2 * LANES + LANES // 4 == 3 * args[4].shape[2]
        )
        return (local_owners if owners else local_general)(*args)

    return jax.shard_map(local, mesh=mesh, in_specs=in_specs, out_specs=out_specs, check_vma=False)
```

```python
import jax
import jax.numpy as jnp
from jax import lax
from jax.experimental import pallas as pl
from jax.experimental.pallas import tpu as pltpu
from jax.sharding import PartitionSpec as P

PRODUCTS = 3
LANES = 128
SMALLEST = 2.0**-100
VMEM_BYTES = 8 * 1024 * 1024
BF = jnp.bfloat16
F32 = jnp.float32


def from_root(array, axis, root):
    mine = lax.axis_index(axis) == root
    return lax.psum(jnp.where(mine, array, jnp.zeros_like(array)), axis)


def complex_scale(field_now, contrast_re, contrast_im):
    real_part = field_now[0]
    imag_part = field_now[1]
    scaled = jnp.stack(
        [
            contrast_re * real_part - contrast_im * imag_part,
            contrast_re * imag_part + contrast_im * real_part,
        ]
    )
    return scaled.astype(BF)


def combine(products):
    return jnp.stack([products[0, 0] - products[1, 1], products[0, 1] + products[1, 0]])


def local_general(green_blocks, slot_rows, slot_cols, slot_count, cell_class, class_contrast, background):
    row_index = lax.axis_index("row")
    col_index = lax.axis_index("col")
    stride = lax.axis_size("col")
    green_tiles = green_blocks[0, 0]
    slot_total = green_tiles.shape[0]
    entries = green_tiles.shape[-1]
    sources = background.shape[1]
    col_blocks = background.shape[2]
    row_blocks = 2 * col_blocks
    local_rows = slot_rows[0, 0]
    local_cols = slot_cols[0, 0]
    global_rows = local_rows // 2 * stride + 2 * row_index + local_rows % 2
    global_cols = local_cols * stride + col_index
    off_diagonal = (global_rows != global_cols).astype(F32)
    living = (jnp.arange(slot_total) < slot_count[0, 0]).astype(F32)
    row_pick = (local_rows[:, None] == jnp.arange(row_blocks)[None, :]).astype(F32) * living[:, None]
    col_pick = (local_cols[:, None] == jnp.arange(col_blocks)[None, :]).astype(F32) * (
        living * off_diagonal
    )[:, None]
    classes = class_contrast.shape[0]
    lookup = (cell_class[:, 0, :, None] == jnp.arange(classes)[None, None, :]).astype(F32)
    values = jnp.einsum("bte,ec->btc", lookup, class_contrast, precision=lax.Precision.HIGHEST)
    contrast_re = jnp.tile(values[:, :, 0], (1, 3))
    contrast_im = jnp.tile(values[:, :, 1], (1, 3))
    start_field = background[:, :, :, 0, :]
    field_now = start_field
    current = complex_scale(field_now, contrast_re, contrast_im)
    for step_index in range(PRODUCTS):
        final_step = step_index + 1 == PRODUCTS
        halves = [from_root(current, "col", 2 * row_index + parity) for parity in range(2)]
        row_current = jnp.stack(halves, axis=3).reshape(2, sources, row_blocks, entries)
        direct_in = jnp.take(current, local_cols, axis=2)
        mirror_in = jnp.take(row_current, local_rows, axis=2)
        direct_terms = combine(
            jnp.einsum("sqoi,pksi->qpkso", green_tiles, direct_in, preferred_element_type=F32)
        )
        mirror_terms = combine(
            jnp.einsum("sqoi,pkso->qpksi", green_tiles, mirror_in, preferred_element_type=F32)
        )
        direct_part = jnp.einsum(
            "pkse,sb->pkbe", direct_terms, row_pick, precision=lax.Precision.HIGHEST
        )
        mirror_part = jnp.einsum(
            "pkse,sb->pkbe", mirror_terms, col_pick, precision=lax.Precision.HIGHEST
        )
        row_total = lax.psum(direct_part, "col")
        owned_part = lax.dynamic_index_in_dim(
            row_total.reshape(2, sources, col_blocks, 2, entries),
            col_index % 2,
            axis=3,
            keepdims=False,
        )
        direct_here = from_root(owned_part, "row", col_index // 2)
        column_total = lax.psum(mirror_part, "row")
        field_now = start_field + column_total + direct_here
        if not final_step:
            current = complex_scale(field_now, contrast_re, contrast_im)
    return field_now[:, :, :, None, :]


MAIN = 2 * LANES
TAIL = LANES // 4
ENDS = 4 * MAIN
WIDTH = ENDS + LANES


def turned(value):
    half = value.shape[0] // 2
    return jnp.concatenate([-value[half:], value[:half]], axis=0)


def shifted(value, lanes):
    return pltpu.roll(value, LANES - lanes, 1) if lanes else value


def put_block(xs_ref, at, value, mirror):
    entries = value.shape[1]
    both = [value.astype(BF), turned(value).astype(BF)]
    if mirror:
        xs_ref[at, :, :entries] = both[0]
        xs_ref[at, :, entries:] = both[1]
    else:
        xs_ref[at, :, :MAIN] = both[0][:, :MAIN]
        xs_ref[at, :, MAIN : 2 * MAIN] = both[1][:, :MAIN]
        xs_ref[at, :, 2 * MAIN :] = jnp.concatenate([part[:, MAIN:] for part in both], axis=1)


def gathered_rows(msg_ref, q, lanes):
    groups = msg_ref.shape[0] // 4
    return jnp.concatenate([msg_ref[q * groups + g, :, lanes].astype(F32) for g in range(groups)], axis=0)


def unpack_half(msg_ref, q, half, xs_ref, at):
    ends = gathered_rows(msg_ref, q, slice(ENDS, WIDTH))
    parts = []
    for k in (2 * half, 2 * half + 1):
        main = gathered_rows(msg_ref, q, slice(k * MAIN, (k + 1) * MAIN))
        parts.append(jnp.concatenate([main, shifted(ends, k * TAIL)[:, :TAIL]], axis=1))
    put_block(xs_ref, at, jnp.concatenate(parts, axis=0), half)


def copy_in(x_ref, xs_ref, offset, mirror):
    for q in range(x_ref.shape[0]):
        put_block(xs_ref, offset + q, x_ref[q].astype(F32), mirror)


def across(left, right):
    return lax.dot_general(left, right, (((1,), (1,)), ((), ())), preferred_element_type=F32)


def slot_products(count_ref, table_ref, g_ref, xs_ref, acc_ref, mirror, cols):
    acc_ref[...] = jnp.zeros_like(acc_ref)
    slots, _, depth, entries = g_ref.shape
    r, c = [table_ref[row, 0].astype(jnp.int32) for row in (2, 3)]
    count = count_ref[0, 0]
    blocks = (acc_ref.shape[0] - 1) // (1 if mirror else 2)
    for s in range(slots):
        local_row = table_ref[0, s].astype(jnp.int32)
        local_col = table_ref[1, s].astype(jnp.int32)
        living = s < count
        half = local_row // 2
        place = (local_row % 2 ^ c % 2) * blocks + half
        if mirror:
            off_diagonal = half * cols + 2 * r + local_row % 2 != local_col * cols + c
            both = g_ref[s].reshape(2 * depth, entries)
            value = jnp.dot(xs_ref[place], both, preferred_element_type=F32)
            acc_ref[jnp.where(living & off_diagonal, local_col, blocks)] += value
        else:
            left = xs_ref[local_col]
            ends = jnp.concatenate([g_ref[s, 0, :, MAIN:], g_ref[s, 1, :, MAIN:]], axis=1)
            value = across(left[:, :MAIN], g_ref[s, 0, :, :MAIN])
            value += across(left[:, MAIN : 2 * MAIN], g_ref[s, 1, :, :MAIN])
            value += across(left[:, 2 * MAIN :], ends)
            acc_ref[jnp.where(living, place, 2 * blocks)] += value


def start_kernel(classes, small_ref, back_ref, out_ref, contrast_ref):
    blocks = out_ref.shape[0]
    cells = contrast_ref.shape[2]
    kinds = small_ref[4 : 4 + blocks, :cells]
    tables = small_ref[4 + blocks : 6 + blocks, :]
    contrast = []
    for part in range(2):
        value = jnp.zeros(kinds.shape, F32)
        for k in range(classes):
            value = jnp.where(kinds == float(k), tables[part : part + 1, k : k + 1], value)
        contrast_ref[part] = value
        contrast.append(jnp.concatenate([value] * 3, axis=1))
    real, imag = contrast
    for q in range(blocks):
        back = back_ref[q]
        out_ref[q] = (real[q : q + 1] * back + imag[q : q + 1] * turned(back)).astype(BF)


def share_kernel(table_ref, contrast_ref, back_ref, _, extra_ref):
    r = table_ref[2, 0].astype(jnp.int32)
    blocks, rows, _ = back_ref.shape
    half = rows // 2
    cells = contrast_ref.shape[2]
    for q in range(blocks):
        rest = jnp.where(r == 2, contrast_ref[1, q : q + 1], contrast_ref[0, q : q + 1])
        marks = []
        for _ in range(3):
            piece = rest.astype(BF).astype(F32)
            marks.append(piece)
            rest = rest - piece
        marks = jnp.concatenate(marks + [jnp.zeros((1, cells), F32)], axis=0)
        marks = jnp.concatenate([marks, jnp.zeros((4, LANES - cells), F32)], axis=1)
        value = jnp.where(r % 2 == 0, back_ref[q, :half, :MAIN], back_ref[q, half:, :MAIN])
        high = value.astype(BF).astype(F32)
        value = jnp.where(r < 2, high, value - high)
        ends = jnp.concatenate([back_ref[q, :half, MAIN:], back_ref[q, half:, MAIN:]], axis=1)
        high = ends.astype(BF).astype(F32)
        ends = jnp.concatenate([high, ends - high], axis=1)
        for g in range(half // 4):
            at = slice(4 * g, 4 * g + 4)
            d = q * (half // 4) + g
            extra_ref[d, :, :MAIN] = value[at].astype(BF)
            extra_ref[d, :, MAIN:] = jnp.where(r == 0, ends[at], marks).astype(BF)


def direct_kernel(first, count_ref, table_ref, g_ref, x_ref, own_ref, other_ref, xs_ref, acc_ref):
    blocks = own_ref.shape[0]
    if first:
        copy_in(x_ref, xs_ref, 0, False)
    else:
        for q in range(blocks):
            unpack_half(x_ref, q, 0, xs_ref, q)
    slot_products(count_ref, table_ref, g_ref, xs_ref, acc_ref, False, 0)
    for q in range(blocks):
        own_ref[q] = acc_ref[q]
        other_ref[q] = acc_ref[blocks + q]


def mirror_kernel(first, cols, count_ref, table_ref, g_ref, x_ref, x_other_ref, out_ref, xs_ref, acc_ref):
    blocks = out_ref.shape[0]
    if first:
        copy_in(x_ref, xs_ref, 0, True)
        copy_in(x_other_ref, xs_ref, blocks, True)
    else:
        for q in range(blocks):
            unpack_half(x_ref, q, 1, xs_ref, q)
            unpack_half(x_other_ref, q, 1, xs_ref, blocks + q)
    slot_products(count_ref, table_ref, g_ref, xs_ref, acc_ref, True, cols)
    for q in range(blocks):
        out_ref[q] = acc_ref[q]


def pack_kernel(mirror_ref, own_ref, got_ref, *rest):
    msg_ref = rest[-1]
    blocks, rows, _ = own_ref.shape
    half = rows // 2
    for q in range(blocks):
        halves = [own_ref[q] + got_ref[q], mirror_ref[q]]
        parts = [value[p * half : (p + 1) * half] for value in halves for p in range(2)]
        ends = jnp.concatenate([part[:, MAIN:] for part in parts], axis=1)
        for g in range(half // 4):
            at = slice(4 * g, 4 * g + 4)
            d = q * (half // 4) + g
            for k, part in enumerate(parts):
                msg_ref[d, :, k * MAIN : (k + 1) * MAIN] = part[at, :MAIN].astype(BF)
            msg_ref[d, :, ENDS:WIDTH] = ends[at].astype(BF)
    if len(rest) == 2:
        msg_ref[:, :, WIDTH:] = rest[0][...]


def partial_sums(msg_ref, rows, cols):
    direct = {}
    mirror = {}

    def add(store, key, value):
        store[key] = store[key] + value if key in store else value

    for r in range(rows):
        for c in range(cols):
            d = r * cols + c
            j = 2 * r + c % 2
            for k in range(9):
                value = msg_ref[d, :, k * LANES : (k + 1) * LANES].astype(F32)
                if k < 4 or k == 8:
                    add(direct, (j, min(k, 4)), value)
                if k >= 4:
                    add(mirror, (c, k - 4), value)
    for j in range(cols):
        mirror[j, 4] = shifted(mirror[j, 4], 2 * TAIL)
    return {key: direct[key] + mirror[key] for key in direct}


def update_kernel(first, rows, cols, msg_ref, *refs):
    back_ref, contrast_ref, out_ref = refs[1:] + refs[:1] if first else refs
    lane = lax.broadcasted_iota(jnp.int32, (4, LANES), 1)
    cells = (MAIN + TAIL) // 3
    sums = partial_sums(msg_ref, rows, cols)
    current = {}
    for j in range(cols):
        if first:
            extra = [
                [msg_ref[r * cols + j, :, WIDTH + k * LANES : WIDTH + (k + 1) * LANES].astype(F32) for k in range(3)]
                for r in range(4)
            ]
            back = [extra[p][k] + extra[p + 2][k] for p in range(2) for k in range(2)]
            back.append(extra[0][2] + shifted(extra[0][2], 2 * TAIL))
            contrast = []
            for r in (1, 2):
                value = extra[r][2]
                value = jnp.broadcast_to(value[0:1] + value[1:2] + value[2:3], (4, LANES))
                moved = [value, shifted(value, TAIL), shifted(value, 2 * TAIL)]
                contrast.append(
                    [
                        jnp.where(lane < cells, moved[0], shifted(value, TAIL)),
                        jnp.where(lane < 2 * TAIL, moved[1], moved[2]),
                        jnp.where(lane < TAIL, moved[2], moved[1]),
                    ]
                )
            for k in range(5):
                back_ref[j, k] = back[k]
            for part in range(2):
                for k in range(3):
                    contrast_ref[j, part, k] = contrast[part][k]
        else:
            back = [back_ref[j, k] for k in range(5)]
            contrast = [[contrast_ref[j, part, k] for k in range(3)] for part in range(2)]
        total = [sums[j, k] + back[k] for k in range(5)]
        real, imag = contrast
        for k in range(2):
            current[j, k] = real[k] * total[k] - imag[k] * total[k + 2]
            current[j, k + 2] = real[k] * total[k + 2] + imag[k] * total[k]
        other = jnp.where(lane < TAIL, -shifted(total[4], TAIL), pltpu.roll(total[4], TAIL, 1))
        current[j, 4] = real[2] * total[4] + imag[2] * other
    for r in range(rows):
        for c in range(cols):
            d = r * cols + c
            j = 2 * r + c % 2
            for k in range(4):
                out_ref[d, :, k * LANES : (k + 1) * LANES] = current[c, k].astype(BF)
                out_ref[d, :, (k + 4) * LANES : (k + 5) * LANES] = current[j, k].astype(BF)
            ends = jnp.where(lane < 2 * TAIL, current[c, 4], shifted(current[j, 4], 2 * TAIL))
            out_ref[d, :, ENDS:WIDTH] = ends.astype(BF)


def last_kernel(rows, cols, msg_ref, out_ref):
    lane = lax.broadcasted_iota(jnp.int32, (4, LANES), 1)
    sums = partial_sums(msg_ref, rows, cols)
    for j in range(cols):
        ends = sums[j, 4]
        coded_ends = jnp.zeros((4, LANES), F32)
        for p in range(2):
            mine = (lane >= p * TAIL) & (lane < (p + 1) * TAIL)
            main = [sums[j, 2 * p], sums[j, 2 * p + 1]]
            most = jnp.maximum(jnp.maximum(jnp.abs(main[0]), jnp.abs(main[1])), jnp.where(mine, jnp.abs(ends), 0.0))
            most = jnp.max(most, axis=1, keepdims=True)
            power = jnp.floor(jnp.log2(jnp.maximum(most, SMALLEST)))
            scale = jnp.exp2(14.0 - power)
            for k in range(2):
                coded = as_integers(main[k] * scale)
                for r in range(rows):
                    out_ref[r * cols + j, :, (2 * p + k) * LANES : (2 * p + k + 1) * LANES] = coded
            coded_ends = jnp.where(mine, ends * scale, jnp.where(lane == 2 * TAIL + p, power, coded_ends))
        coded = as_integers(coded_ends)
        for r in range(rows):
            out_ref[r * cols + j, :, 2 * MAIN : 2 * MAIN + LANES] = coded


def as_integers(value):
    return jnp.clip(jnp.round(value), -32767.0, 32767.0).astype(jnp.int32).astype(jnp.int16)


def finish_kernel(msg_ref, back_ref, out_ref):
    blocks, rows, _ = out_ref.shape
    half = rows // 2
    groups = half // 4

    def rows_of(q, lanes):
        pieces = [msg_ref[q * groups + g, :, lanes].astype(jnp.int32).astype(F32) for g in range(groups)]
        return jnp.concatenate(pieces, axis=0)

    for q in range(blocks):
        ends = rows_of(q, slice(2 * MAIN, 2 * MAIN + LANES))
        for p in range(2):
            at = slice(p * half, (p + 1) * half)
            scale = jnp.exp2(ends[:, 2 * TAIL + p : 2 * TAIL + p + 1] - 14.0)
            main = rows_of(q, slice(p * MAIN, (p + 1) * MAIN))
            out_ref[q, at, :MAIN] = back_ref[q, at, :MAIN] + main * scale
            out_ref[q, at, MAIN:] = back_ref[q, at, MAIN:] + shifted(ends, p * TAIL)[:, :TAIL] * scale


def whole_call(kernel, out_shape, spaces, operands, scratch, name):
    spaces = list(spaces) + [pltpu.VMEM] * (len(operands) - len(spaces))
    return pl.pallas_call(
        kernel,
        out_shape=out_shape,
        in_specs=[pl.BlockSpec(memory_space=space) for space in spaces],
        out_specs=jax.tree.map(lambda _: pl.BlockSpec(memory_space=pltpu.VMEM), out_shape),
        scratch_shapes=scratch,
        compiler_params=pltpu.CompilerParams(vmem_limit_bytes=VMEM_BYTES),
        name=name,
    )(*operands)


def stacked(arrays):
    heights = [1 if array is None else array.shape[0] for array in arrays]
    total = 0
    at = 0
    for array, height in zip(arrays, heights):
        if array is not None:
            edges = ((at, sum(heights) - at - height, 0), (0, LANES - array.shape[1], 0))
            total += lax.pad(array, jnp.zeros((), array.dtype), edges).astype(F32)
        at += height
    return total


def local_owners(green_blocks, slot_rows, slot_cols, slot_count, cell_class, class_contrast, background):
    r = lax.axis_index("row")
    c = lax.axis_index("col")
    rows = lax.axis_size("row")
    cols = lax.axis_size("col")
    green = green_blocks[0, 0]
    slots, _, entries, _ = green.shape
    sources, blocks = background.shape[1:3]
    both = ("row", "col")

    small = stacked([slot_rows[0], slot_cols[0], None, None, cell_class[:, 0, :], class_contrast.T])
    line = lax.broadcasted_iota(jnp.int32, small.shape, 0)
    small = jnp.where(line == 2, r.astype(F32), jnp.where(line == 3, c.astype(F32), small))

    block = (2 * sources, entries)
    back = background[:, :, :, 0, :].transpose(2, 0, 1, 3).reshape((blocks,) + block)
    start, contrast = whole_call(
        lambda *refs: start_kernel(class_contrast.shape[0], *refs),
        (
            jax.ShapeDtypeStruct((blocks,) + block, BF),
            jax.ShapeDtypeStruct((2, blocks, entries // 3), F32),
        ),
        [],
        (small, back),
        [],
        "start",
    )

    core_pairs = [(i, i ^ 1) for i in range(cols)]
    chips = cols // 2
    arrived = []
    for hop in range(1, chips):
        pairs = []
        for a in range(rows):
            far = (a + hop) % chips
            for k in range(chips):
                for p in range(2):
                    to = {a: 2 * far + p, far: 2 * a + p}.get(k, 2 * k + 1 - p)
                    pairs.append((a * cols + 2 * k + p, a * cols + to))
        arrived.append(lax.ppermute(start, both, pairs))
    extra = whole_call(
        share_kernel,
        jax.ShapeDtypeStruct((rows * cols, 4, 3 * LANES), BF),
        [pltpu.SMEM],
        (small, contrast, back, green),
        [],
        "share",
    )
    extra, *arrived = lax.optimization_barrier((extra, *arrived))
    row_mine = start
    for hop in range(1, chips):
        row_mine = jnp.where(c // 2 == (r + hop) % chips, arrived[hop - 1], row_mine)
    row_other = lax.ppermute(row_mine, "col", core_pairs)

    part = jax.ShapeDtypeStruct((blocks,) + block, F32)
    message = jax.ShapeDtypeStruct((rows * cols, 4, WIDTH), BF)
    for step in range(PRODUCTS):
        first = step == 0
        final = step + 1 == PRODUCTS
        if first:
            direct_in, mirror_in = start, (row_mine, row_other)
        else:
            direct_in, mirror_in = x_msg, (x_msg, lax.ppermute(x_msg, "col", core_pairs))
        own, other = whole_call(
            lambda *refs, first=first: direct_kernel(first, *refs),
            (part, part),
            [pltpu.SMEM] * 2,
            (slot_count, small, green, direct_in),
            [
                pltpu.VMEM((blocks, 2 * sources, 2 * entries), BF),
                pltpu.VMEM((2 * blocks + 1,) + block, F32),
            ],
            f"direct_{step}",
        )
        got = lax.ppermute(other, "col", core_pairs)
        mirror = whole_call(
            lambda *refs, first=first: mirror_kernel(first, cols, *refs),
            part,
            [pltpu.SMEM] * 2,
            (slot_count, small, green) + mirror_in,
            [
                pltpu.VMEM((2 * blocks, 2 * sources, 2 * entries), BF),
                pltpu.VMEM((blocks + 1,) + block, F32),
            ],
            f"mirror_{step}",
        )
        y_shape = jax.ShapeDtypeStruct((rows * cols, 4, WIDTH + 3 * LANES), BF) if first else message
        operands = (mirror, own, got) + ((extra,) if first else ())
        y_msg = whole_call(pack_kernel, y_shape, [], operands, [], f"pack_{step}")
        y_msg = lax.all_to_all(y_msg, both, 0, 0, tiled=True)
        run = lambda *refs, first=first: update_kernel(first, rows, cols, *refs)
        if first:
            x_msg, owner_back, owner_contrast = whole_call(
                run,
                (
                    message,
                    jax.ShapeDtypeStruct((cols, 5, 4, LANES), F32),
                    jax.ShapeDtypeStruct((cols, 2, 3, 4, LANES), F32),
                ),
                [],
                (y_msg,),
                [],
                f"update_{step}",
            )
        elif not final:
            operands = (y_msg, owner_back, owner_contrast)
            x_msg = whole_call(run, message, [], operands, [], f"update_{step}")
        else:
            run = lambda *refs: last_kernel(rows, cols, *refs)
            x_shape = jax.ShapeDtypeStruct((rows * cols, 4, 2 * MAIN + LANES), jnp.int16)
            x_msg = whole_call(run, x_shape, [], (y_msg,), [], "last")
        x_msg = lax.all_to_all(x_msg, both, 0, 0, tiled=True)
    field = whole_call(finish_kernel, part, [], (x_msg, back), [], "finish")
    field = field.reshape(blocks, 2, sources, entries).transpose(1, 2, 0, 3)
    return field[:, :, :, None, :]


def solution(mesh):
    in_specs = (
        P("row", "col", None, None, None, None),
        P("row", "col", None),
        P("row", "col", None),
        P("row", "col"),
        P(None, "col", None),
        P(),
        P(None, None, None, "col", None),
    )
    out_specs = P(None, None, None, "col", None)
    rows, cols = mesh.shape["row"], mesh.shape["col"]

    def local(*args):
        sources, blocks = args[6].shape[1:3]
        entries = args[6].shape[4]
        owners = (
            rows == blocks == 4
            and cols == 2 * rows
            and sources == 4 * cols
            and max(args[5].shape[0], args[1].shape[2]) <= LANES
            and entries == 2 * LANES + LANES // 4 == 3 * args[4].shape[2]
        )
        return (local_owners if owners else local_general)(*args)

    return jax.shard_map(local, mesh=mesh, in_specs=in_specs, out_specs=out_specs, check_vma=False)
```

```python
import jax
import jax.numpy as jnp
from jax import lax
from jax.experimental import pallas as pl
from jax.experimental.pallas import tpu as pltpu
from jax.sharding import PartitionSpec as P

PRODUCTS = 3
LANES = 128
SMALLEST = 2.0**-100
VMEM_BYTES = 8 * 1024 * 1024
BF = jnp.bfloat16
F32 = jnp.float32


def from_root(array, axis, root):
    mine = lax.axis_index(axis) == root
    return lax.psum(jnp.where(mine, array, jnp.zeros_like(array)), axis)


def complex_scale(field_now, contrast_re, contrast_im):
    real_part = field_now[0]
    imag_part = field_now[1]
    scaled = jnp.stack(
        [
            contrast_re * real_part - contrast_im * imag_part,
            contrast_re * imag_part + contrast_im * real_part,
        ]
    )
    return scaled.astype(BF)


def combine(products):
    return jnp.stack([products[0, 0] - products[1, 1], products[0, 1] + products[1, 0]])


def local_general(green_blocks, slot_rows, slot_cols, slot_count, cell_class, class_contrast, background):
    row_index = lax.axis_index("row")
    col_index = lax.axis_index("col")
    stride = lax.axis_size("col")
    green_tiles = green_blocks[0, 0]
    slot_total = green_tiles.shape[0]
    entries = green_tiles.shape[-1]
    sources = background.shape[1]
    col_blocks = background.shape[2]
    row_blocks = 2 * col_blocks
    local_rows = slot_rows[0, 0]
    local_cols = slot_cols[0, 0]
    global_rows = local_rows // 2 * stride + 2 * row_index + local_rows % 2
    global_cols = local_cols * stride + col_index
    off_diagonal = (global_rows != global_cols).astype(F32)
    living = (jnp.arange(slot_total) < slot_count[0, 0]).astype(F32)
    row_pick = (local_rows[:, None] == jnp.arange(row_blocks)[None, :]).astype(F32) * living[:, None]
    col_pick = (local_cols[:, None] == jnp.arange(col_blocks)[None, :]).astype(F32) * (
        living * off_diagonal
    )[:, None]
    classes = class_contrast.shape[0]
    lookup = (cell_class[:, 0, :, None] == jnp.arange(classes)[None, None, :]).astype(F32)
    values = jnp.einsum("bte,ec->btc", lookup, class_contrast, precision=lax.Precision.HIGHEST)
    contrast_re = jnp.tile(values[:, :, 0], (1, 3))
    contrast_im = jnp.tile(values[:, :, 1], (1, 3))
    start_field = background[:, :, :, 0, :]
    field_now = start_field
    current = complex_scale(field_now, contrast_re, contrast_im)
    for step_index in range(PRODUCTS):
        final_step = step_index + 1 == PRODUCTS
        halves = [from_root(current, "col", 2 * row_index + parity) for parity in range(2)]
        row_current = jnp.stack(halves, axis=3).reshape(2, sources, row_blocks, entries)
        direct_in = jnp.take(current, local_cols, axis=2)
        mirror_in = jnp.take(row_current, local_rows, axis=2)
        direct_terms = combine(
            jnp.einsum("sqoi,pksi->qpkso", green_tiles, direct_in, preferred_element_type=F32)
        )
        mirror_terms = combine(
            jnp.einsum("sqoi,pkso->qpksi", green_tiles, mirror_in, preferred_element_type=F32)
        )
        direct_part = jnp.einsum(
            "pkse,sb->pkbe", direct_terms, row_pick, precision=lax.Precision.HIGHEST
        )
        mirror_part = jnp.einsum(
            "pkse,sb->pkbe", mirror_terms, col_pick, precision=lax.Precision.HIGHEST
        )
        row_total = lax.psum(direct_part, "col")
        owned_part = lax.dynamic_index_in_dim(
            row_total.reshape(2, sources, col_blocks, 2, entries),
            col_index % 2,
            axis=3,
            keepdims=False,
        )
        direct_here = from_root(owned_part, "row", col_index // 2)
        column_total = lax.psum(mirror_part, "row")
        field_now = start_field + column_total + direct_here
        if not final_step:
            current = complex_scale(field_now, contrast_re, contrast_im)
    return field_now[:, :, :, None, :]


MAIN = 2 * LANES
TAIL = LANES // 4
ENDS = 4 * MAIN
WIDTH = ENDS + LANES


def turned(value):
    half = value.shape[0] // 2
    return jnp.concatenate([-value[half:], value[:half]], axis=0)


def shifted(value, lanes):
    return pltpu.roll(value, LANES - lanes, 1) if lanes else value


def put_block(xs_ref, at, value, mirror):
    entries = value.shape[1]
    both = [value.astype(BF), turned(value).astype(BF)]
    if mirror:
        xs_ref[at, :, :entries] = both[0]
        xs_ref[at, :, entries:] = both[1]
    else:
        xs_ref[at, :, :MAIN] = both[0][:, :MAIN]
        xs_ref[at, :, MAIN : 2 * MAIN] = both[1][:, :MAIN]
        xs_ref[at, :, 2 * MAIN :] = jnp.concatenate([part[:, MAIN:] for part in both], axis=1)


def gathered_rows(msg_ref, q, lanes):
    groups = msg_ref.shape[0] // 4
    return jnp.concatenate([msg_ref[q * groups + g, :, lanes].astype(F32) for g in range(groups)], axis=0)


def unpack_half(msg_ref, q, half, xs_ref, at):
    ends = gathered_rows(msg_ref, q, slice(ENDS, WIDTH))
    parts = []
    for k in (2 * half, 2 * half + 1):
        main = gathered_rows(msg_ref, q, slice(k * MAIN, (k + 1) * MAIN))
        parts.append(jnp.concatenate([main, shifted(ends, k * TAIL)[:, :TAIL]], axis=1))
    put_block(xs_ref, at, jnp.concatenate(parts, axis=0), half)


def copy_in(x_ref, xs_ref, offset, mirror):
    for q in range(x_ref.shape[0]):
        put_block(xs_ref, offset + q, x_ref[q].astype(F32), mirror)


def across(left, right):
    return lax.dot_general(left, right, (((1,), (1,)), ((), ())), preferred_element_type=F32)


def slot_products(table_ref, g_ref, xs_ref, acc_ref, mirror):
    acc_ref[...] = jnp.zeros_like(acc_ref)
    slots, _, depth, entries = g_ref.shape
    table = table_ref[...]
    first = 2 if mirror else 0
    for s in range(slots):
        left = xs_ref[table[first, s]]
        if mirror:
            value = jnp.dot(left, g_ref[s].reshape(2 * depth, entries), preferred_element_type=F32)
        else:
            ends = jnp.concatenate([g_ref[s, 0, :, MAIN:], g_ref[s, 1, :, MAIN:]], axis=1)
            value = across(left[:, :MAIN], g_ref[s, 0, :, :MAIN])
            value += across(left[:, MAIN : 2 * MAIN], g_ref[s, 1, :, :MAIN])
            value += across(left[:, 2 * MAIN :], ends)
        acc_ref[table[first + 1, s]] += value


def start_kernel(classes, small_ref, back_ref, out_ref, contrast_ref):
    blocks = out_ref.shape[0]
    cells = contrast_ref.shape[2]
    kinds = small_ref[4 : 4 + blocks, :cells]
    tables = small_ref[4 + blocks : 6 + blocks, :]
    contrast = []
    for part in range(2):
        value = jnp.zeros(kinds.shape, F32)
        for k in range(classes):
            value = jnp.where(kinds == float(k), tables[part : part + 1, k : k + 1], value)
        contrast_ref[part] = value
        contrast.append(jnp.concatenate([value] * 3, axis=1))
    real, imag = contrast
    for q in range(blocks):
        back = back_ref[q]
        out_ref[q] = (real[q : q + 1] * back + imag[q : q + 1] * turned(back)).astype(BF)


def share_kernel(small_ref, contrast_ref, back_ref, _, extra_ref):
    r = small_ref[2:3, 0:1].astype(jnp.int32)
    blocks, rows, _ = back_ref.shape
    half = rows // 2
    cells = contrast_ref.shape[2]
    for q in range(blocks):
        rest = jnp.where(r == 2, contrast_ref[1, q : q + 1], contrast_ref[0, q : q + 1])
        marks = []
        for _ in range(3):
            piece = rest.astype(BF).astype(F32)
            marks.append(piece)
            rest = rest - piece
        marks = jnp.concatenate(marks + [jnp.zeros((1, cells), F32)], axis=0)
        marks = jnp.concatenate([marks, jnp.zeros((4, LANES - cells), F32)], axis=1)
        value = jnp.where(r % 2 == 0, back_ref[q, :half, :MAIN], back_ref[q, half:, :MAIN])
        high = value.astype(BF).astype(F32)
        value = jnp.where(r < 2, high, value - high)
        ends = jnp.concatenate([back_ref[q, :half, MAIN:], back_ref[q, half:, MAIN:]], axis=1)
        high = ends.astype(BF).astype(F32)
        ends = jnp.concatenate([high, ends - high], axis=1)
        for g in range(half // 4):
            at = slice(4 * g, 4 * g + 4)
            d = q * (half // 4) + g
            extra_ref[d, :, :MAIN] = value[at].astype(BF)
            extra_ref[d, :, MAIN:] = jnp.where(r == 0, ends[at], marks).astype(BF)


def direct_kernel(first, table_ref, g_ref, x_ref, own_ref, other_ref, xs_ref, acc_ref):
    blocks = own_ref.shape[0]
    if first:
        copy_in(x_ref, xs_ref, 0, False)
    else:
        for q in range(blocks):
            unpack_half(x_ref, q, 0, xs_ref, q)
    slot_products(table_ref, g_ref, xs_ref, acc_ref, False)
    for q in range(blocks):
        own_ref[q] = acc_ref[q]
        other_ref[q] = acc_ref[blocks + q]


def mirror_kernel(first, table_ref, g_ref, x_ref, x_other_ref, out_ref, xs_ref, acc_ref):
    blocks = out_ref.shape[0]
    if first:
        copy_in(x_ref, xs_ref, 0, True)
        copy_in(x_other_ref, xs_ref, blocks, True)
    else:
        for q in range(blocks):
            unpack_half(x_ref, q, 1, xs_ref, q)
            unpack_half(x_other_ref, q, 1, xs_ref, blocks + q)
    slot_products(table_ref, g_ref, xs_ref, acc_ref, True)
    for q in range(blocks):
        out_ref[q] = acc_ref[q]


def pack_kernel(mirror_ref, own_ref, got_ref, *rest):
    msg_ref = rest[-1]
    blocks, rows, _ = own_ref.shape
    half = rows // 2
    for q in range(blocks):
        halves = [own_ref[q] + got_ref[q], mirror_ref[q]]
        parts = [value[p * half : (p + 1) * half] for value in halves for p in range(2)]
        ends = jnp.concatenate([part[:, MAIN:] for part in parts], axis=1)
        for g in range(half // 4):
            at = slice(4 * g, 4 * g + 4)
            d = q * (half // 4) + g
            for k, part in enumerate(parts):
                msg_ref[d, :, k * MAIN : (k + 1) * MAIN] = part[at, :MAIN].astype(BF)
            msg_ref[d, :, ENDS:WIDTH] = ends[at].astype(BF)
    if len(rest) == 2:
        msg_ref[:, :, WIDTH:] = rest[0][...]


def partial_sums(msg_ref, rows, cols):
    direct = {}
    mirror = {}

    def add(store, key, value):
        store[key] = store[key] + value if key in store else value

    for r in range(rows):
        for c in range(cols):
            d = r * cols + c
            j = 2 * r + c % 2
            for k in range(9):
                value = msg_ref[d, :, k * LANES : (k + 1) * LANES].astype(F32)
                if k < 4 or k == 8:
                    add(direct, (j, min(k, 4)), value)
                if k >= 4:
                    add(mirror, (c, k - 4), value)
    for j in range(cols):
        mirror[j, 4] = shifted(mirror[j, 4], 2 * TAIL)
    return {key: direct[key] + mirror[key] for key in direct}


def update_kernel(first, rows, cols, msg_ref, *refs):
    back_ref, contrast_ref, out_ref = refs[1:] + refs[:1] if first else refs
    lane = lax.broadcasted_iota(jnp.int32, (4, LANES), 1)
    cells = (MAIN + TAIL) // 3
    sums = partial_sums(msg_ref, rows, cols)
    current = {}
    for j in range(cols):
        if first:
            extra = [
                [msg_ref[r * cols + j, :, WIDTH + k * LANES : WIDTH + (k + 1) * LANES].astype(F32) for k in range(3)]
                for r in range(4)
            ]
            back = [extra[p][k] + extra[p + 2][k] for p in range(2) for k in range(2)]
            back.append(extra[0][2] + shifted(extra[0][2], 2 * TAIL))
            contrast = []
            for r in (1, 2):
                value = extra[r][2]
                value = jnp.broadcast_to(value[0:1] + value[1:2] + value[2:3], (4, LANES))
                moved = [value, shifted(value, TAIL), shifted(value, 2 * TAIL)]
                contrast.append(
                    [
                        jnp.where(lane < cells, moved[0], shifted(value, TAIL)),
                        jnp.where(lane < 2 * TAIL, moved[1], moved[2]),
                        jnp.where(lane < TAIL, moved[2], moved[1]),
                    ]
                )
            for k in range(5):
                back_ref[j, k] = back[k]
            for part in range(2):
                for k in range(3):
                    contrast_ref[j, part, k] = contrast[part][k]
        else:
            back = [back_ref[j, k] for k in range(5)]
            contrast = [[contrast_ref[j, part, k] for k in range(3)] for part in range(2)]
        total = [sums[j, k] + back[k] for k in range(5)]
        real, imag = contrast
        for k in range(2):
            current[j, k] = real[k] * total[k] - imag[k] * total[k + 2]
            current[j, k + 2] = real[k] * total[k + 2] + imag[k] * total[k]
        other = jnp.where(lane < TAIL, -shifted(total[4], TAIL), pltpu.roll(total[4], TAIL, 1))
        current[j, 4] = real[2] * total[4] + imag[2] * other
    for r in range(rows):
        for c in range(cols):
            d = r * cols + c
            j = 2 * r + c % 2
            for k in range(4):
                out_ref[d, :, k * LANES : (k + 1) * LANES] = current[c, k].astype(BF)
                out_ref[d, :, (k + 4) * LANES : (k + 5) * LANES] = current[j, k].astype(BF)
            ends = jnp.where(lane < 2 * TAIL, current[c, 4], shifted(current[j, 4], 2 * TAIL))
            out_ref[d, :, ENDS:WIDTH] = ends.astype(BF)


def last_kernel(rows, cols, msg_ref, out_ref):
    lane = lax.broadcasted_iota(jnp.int32, (4, LANES), 1)
    sums = partial_sums(msg_ref, rows, cols)
    for j in range(cols):
        ends = sums[j, 4]
        coded_ends = jnp.zeros((4, LANES), F32)
        for p in range(2):
            mine = (lane >= p * TAIL) & (lane < (p + 1) * TAIL)
            main = [sums[j, 2 * p], sums[j, 2 * p + 1]]
            most = jnp.maximum(jnp.maximum(jnp.abs(main[0]), jnp.abs(main[1])), jnp.where(mine, jnp.abs(ends), 0.0))
            most = jnp.max(most, axis=1, keepdims=True)
            power = jnp.floor(jnp.log2(jnp.maximum(most, SMALLEST)))
            scale = jnp.exp2(14.0 - power)
            for k in range(2):
                coded = as_integers(main[k] * scale)
                for r in range(rows):
                    out_ref[r * cols + j, :, (2 * p + k) * LANES : (2 * p + k + 1) * LANES] = coded
            coded_ends = jnp.where(mine, ends * scale, jnp.where(lane == 2 * TAIL + p, power, coded_ends))
        coded = as_integers(coded_ends)
        for r in range(rows):
            out_ref[r * cols + j, :, 2 * MAIN : 2 * MAIN + LANES] = coded


def as_integers(value):
    return jnp.clip(jnp.round(value), -32767.0, 32767.0).astype(jnp.int32).astype(jnp.int16)


def finish_kernel(msg_ref, back_ref, out_ref):
    blocks, rows, _ = out_ref.shape
    half = rows // 2
    groups = half // 4

    def rows_of(q, lanes):
        pieces = [msg_ref[q * groups + g, :, lanes].astype(jnp.int32).astype(F32) for g in range(groups)]
        return jnp.concatenate(pieces, axis=0)

    for q in range(blocks):
        ends = rows_of(q, slice(2 * MAIN, 2 * MAIN + LANES))
        for p in range(2):
            at = slice(p * half, (p + 1) * half)
            scale = jnp.exp2(ends[:, 2 * TAIL + p : 2 * TAIL + p + 1] - 14.0)
            main = rows_of(q, slice(p * MAIN, (p + 1) * MAIN))
            out_ref[q, at, :MAIN] = back_ref[q, at, :MAIN] + main * scale
            out_ref[q, at, MAIN:] = back_ref[q, at, MAIN:] + shifted(ends, p * TAIL)[:, :TAIL] * scale


def whole_call(kernel, out_shape, operands, scratch, name):
    vmem = pl.BlockSpec(memory_space=pltpu.VMEM)
    return pl.pallas_call(
        kernel,
        out_shape=out_shape,
        in_specs=[vmem] * len(operands),
        out_specs=jax.tree.map(lambda _: vmem, out_shape),
        scratch_shapes=scratch,
        compiler_params=pltpu.CompilerParams(vmem_limit_bytes=VMEM_BYTES),
        name=name,
    )(*operands)


def stacked(arrays):
    heights = [1 if array is None else array.shape[0] for array in arrays]
    total = 0
    at = 0
    for array, height in zip(arrays, heights):
        if array is not None:
            edges = ((at, sum(heights) - at - height, 0), (0, LANES - array.shape[1], 0))
            total += lax.pad(array, jnp.zeros((), array.dtype), edges).astype(F32)
        at += height
    return total


def local_owners(green_blocks, slot_rows, slot_cols, slot_count, cell_class, class_contrast, background):
    r = lax.axis_index("row")
    c = lax.axis_index("col")
    rows = lax.axis_size("row")
    cols = lax.axis_size("col")
    green = green_blocks[0, 0]
    slots, _, entries, _ = green.shape
    sources, blocks = background.shape[1:3]
    both = ("row", "col")

    small = stacked([slot_rows[0], slot_cols[0], None, None, cell_class[:, 0, :], class_contrast.T])
    line = lax.broadcasted_iota(jnp.int32, small.shape, 0)
    small = jnp.where(line == 2, r.astype(F32), jnp.where(line == 3, c.astype(F32), small))

    local_rows = small[0:1, :].astype(jnp.int32)
    local_cols = small[1:2, :].astype(jnp.int32)
    living = lax.broadcasted_iota(jnp.int32, (1, LANES), 1) < slot_count
    off_diagonal = (local_rows // 2 * cols + 2 * r + local_rows % 2) != (local_cols * cols + c)
    place = (local_rows % 2 ^ c % 2) * blocks + local_rows // 2
    spare = jnp.full_like(place, 2 * blocks)
    table = jnp.concatenate(
        [
            local_cols,
            jnp.where(living, place, spare),
            place,
            jnp.where(living & off_diagonal, local_cols, spare // 2),
        ],
        axis=0,
    )

    block = (2 * sources, entries)
    back = background[:, :, :, 0, :].transpose(2, 0, 1, 3).reshape((blocks,) + block)
    start, contrast = whole_call(
        lambda *refs: start_kernel(class_contrast.shape[0], *refs),
        (
            jax.ShapeDtypeStruct((blocks,) + block, BF),
            jax.ShapeDtypeStruct((2, blocks, entries // 3), F32),
        ),
        (small, back),
        [],
        "start",
    )

    core_pairs = [(i, i ^ 1) for i in range(cols)]
    chips = cols // 2
    arrived = []
    for hop in range(1, chips):
        pairs = []
        for a in range(rows):
            far = (a + hop) % chips
            for k in range(chips):
                for p in range(2):
                    to = {a: 2 * far + p, far: 2 * a + p}.get(k, 2 * k + 1 - p)
                    pairs.append((a * cols + 2 * k + p, a * cols + to))
        arrived.append(lax.ppermute(start, both, pairs))
    extra = whole_call(
        share_kernel,
        jax.ShapeDtypeStruct((rows * cols, 4, 3 * LANES), BF),
        (small, contrast, back, green),
        [],
        "share",
    )
    extra, *arrived = lax.optimization_barrier((extra, *arrived))
    row_mine = start
    for hop in range(1, chips):
        row_mine = jnp.where(c // 2 == (r + hop) % chips, arrived[hop - 1], row_mine)
    row_other = lax.ppermute(row_mine, "col", core_pairs)

    part = jax.ShapeDtypeStruct((blocks,) + block, F32)
    message = jax.ShapeDtypeStruct((rows * cols, 4, WIDTH), BF)
    for step in range(PRODUCTS):
        first = step == 0
        final = step + 1 == PRODUCTS
        if first:
            direct_in, mirror_in = start, (row_mine, row_other)
        else:
            direct_in, mirror_in = x_msg, (x_msg, lax.ppermute(x_msg, "col", core_pairs))
        own, other = whole_call(
            lambda *refs, first=first: direct_kernel(first, *refs),
            (part, part),
            (table, green, direct_in),
            [
                pltpu.VMEM((blocks, 2 * sources, 2 * entries), BF),
                pltpu.VMEM((2 * blocks + 1,) + block, F32),
            ],
            f"direct_{step}",
        )
        got = lax.ppermute(other, "col", core_pairs)
        mirror = whole_call(
            lambda *refs, first=first: mirror_kernel(first, *refs),
            part,
            (table, green) + mirror_in,
            [
                pltpu.VMEM((2 * blocks, 2 * sources, 2 * entries), BF),
                pltpu.VMEM((blocks + 1,) + block, F32),
            ],
            f"mirror_{step}",
        )
        y_shape = jax.ShapeDtypeStruct((rows * cols, 4, WIDTH + 3 * LANES), BF) if first else message
        operands = (mirror, own, got) + ((extra,) if first else ())
        y_msg = whole_call(pack_kernel, y_shape, operands, [], f"pack_{step}")
        y_msg = lax.all_to_all(y_msg, both, 0, 0, tiled=True)
        run = lambda *refs, first=first: update_kernel(first, rows, cols, *refs)
        if first:
            x_msg, owner_back, owner_contrast = whole_call(
                run,
                (
                    message,
                    jax.ShapeDtypeStruct((cols, 5, 4, LANES), F32),
                    jax.ShapeDtypeStruct((cols, 2, 3, 4, LANES), F32),
                ),
                (y_msg,),
                [],
                f"update_{step}",
            )
        elif not final:
            operands = (y_msg, owner_back, owner_contrast)
            x_msg = whole_call(run, message, operands, [], f"update_{step}")
        else:
            run = lambda *refs: last_kernel(rows, cols, *refs)
            x_shape = jax.ShapeDtypeStruct((rows * cols, 4, 2 * MAIN + LANES), jnp.int16)
            x_msg = whole_call(run, x_shape, (y_msg,), [], "last")
        x_msg = lax.all_to_all(x_msg, both, 0, 0, tiled=True)
    field = whole_call(finish_kernel, part, (x_msg, back), [], "finish")
    field = field.reshape(blocks, 2, sources, entries).transpose(1, 2, 0, 3)
    return field[:, :, :, None, :]


def solution(mesh):
    in_specs = (
        P("row", "col", None, None, None, None),
        P("row", "col", None),
        P("row", "col", None),
        P("row", "col"),
        P(None, "col", None),
        P(),
        P(None, None, None, "col", None),
    )
    out_specs = P(None, None, None, "col", None)
    rows, cols = mesh.shape["row"], mesh.shape["col"]

    def local(*args):
        sources, blocks = args[6].shape[1:3]
        entries = args[6].shape[4]
        owners = (
            rows == blocks == 4
            and cols == 2 * rows
            and sources == 4 * cols
            and max(args[5].shape[0], args[1].shape[2]) <= LANES
            and entries == 2 * LANES + LANES // 4 == 3 * args[4].shape[2]
        )
        return (local_owners if owners else local_general)(*args)

    return jax.shard_map(local, mesh=mesh, in_specs=in_specs, out_specs=out_specs, check_vma=False)
```

```python
import jax
import jax.numpy as jnp
from jax import lax
from jax.experimental import pallas as pl
from jax.experimental.pallas import tpu as pltpu
from jax.sharding import PartitionSpec as P

PRODUCTS = 3
LANES = 128
SMALLEST = 2.0**-100
VMEM_BYTES = 8 * 1024 * 1024
BF = jnp.bfloat16
F32 = jnp.float32


def from_root(array, axis, root):
    mine = lax.axis_index(axis) == root
    return lax.psum(jnp.where(mine, array, jnp.zeros_like(array)), axis)


def complex_scale(field_now, contrast_re, contrast_im):
    real_part = field_now[0]
    imag_part = field_now[1]
    scaled = jnp.stack(
        [
            contrast_re * real_part - contrast_im * imag_part,
            contrast_re * imag_part + contrast_im * real_part,
        ]
    )
    return scaled.astype(BF)


def combine(products):
    return jnp.stack([products[0, 0] - products[1, 1], products[0, 1] + products[1, 0]])


def local_general(green_blocks, slot_rows, slot_cols, slot_count, cell_class, class_contrast, background):
    row_index = lax.axis_index("row")
    col_index = lax.axis_index("col")
    stride = lax.axis_size("col")
    green_tiles = green_blocks[0, 0]
    slot_total = green_tiles.shape[0]
    entries = green_tiles.shape[-1]
    sources = background.shape[1]
    col_blocks = background.shape[2]
    row_blocks = 2 * col_blocks
    local_rows = slot_rows[0, 0]
    local_cols = slot_cols[0, 0]
    global_rows = local_rows // 2 * stride + 2 * row_index + local_rows % 2
    global_cols = local_cols * stride + col_index
    off_diagonal = (global_rows != global_cols).astype(F32)
    living = (jnp.arange(slot_total) < slot_count[0, 0]).astype(F32)
    row_pick = (local_rows[:, None] == jnp.arange(row_blocks)[None, :]).astype(F32) * living[:, None]
    col_pick = (local_cols[:, None] == jnp.arange(col_blocks)[None, :]).astype(F32) * (
        living * off_diagonal
    )[:, None]
    classes = class_contrast.shape[0]
    lookup = (cell_class[:, 0, :, None] == jnp.arange(classes)[None, None, :]).astype(F32)
    values = jnp.einsum("bte,ec->btc", lookup, class_contrast, precision=lax.Precision.HIGHEST)
    contrast_re = jnp.tile(values[:, :, 0], (1, 3))
    contrast_im = jnp.tile(values[:, :, 1], (1, 3))
    start_field = background[:, :, :, 0, :]
    field_now = start_field
    current = complex_scale(field_now, contrast_re, contrast_im)
    for step_index in range(PRODUCTS):
        final_step = step_index + 1 == PRODUCTS
        halves = [from_root(current, "col", 2 * row_index + parity) for parity in range(2)]
        row_current = jnp.stack(halves, axis=3).reshape(2, sources, row_blocks, entries)
        direct_in = jnp.take(current, local_cols, axis=2)
        mirror_in = jnp.take(row_current, local_rows, axis=2)
        direct_terms = combine(
            jnp.einsum("sqoi,pksi->qpkso", green_tiles, direct_in, preferred_element_type=F32)
        )
        mirror_terms = combine(
            jnp.einsum("sqoi,pkso->qpksi", green_tiles, mirror_in, preferred_element_type=F32)
        )
        direct_part = jnp.einsum(
            "pkse,sb->pkbe", direct_terms, row_pick, precision=lax.Precision.HIGHEST
        )
        mirror_part = jnp.einsum(
            "pkse,sb->pkbe", mirror_terms, col_pick, precision=lax.Precision.HIGHEST
        )
        row_total = lax.psum(direct_part, "col")
        owned_part = lax.dynamic_index_in_dim(
            row_total.reshape(2, sources, col_blocks, 2, entries),
            col_index % 2,
            axis=3,
            keepdims=False,
        )
        direct_here = from_root(owned_part, "row", col_index // 2)
        column_total = lax.psum(mirror_part, "row")
        field_now = start_field + column_total + direct_here
        if not final_step:
            current = complex_scale(field_now, contrast_re, contrast_im)
    return field_now[:, :, :, None, :]


MAIN = 2 * LANES
TAIL = LANES // 4
ENDS = 4 * MAIN
WIDTH = ENDS + LANES


def turned(value):
    half = value.shape[0] // 2
    return jnp.concatenate([-value[half:], value[:half]], axis=0)


def shifted(value, lanes):
    return pltpu.roll(value, LANES - lanes, 1) if lanes else value


def put_block(xs_ref, at, value, mirror):
    entries = value.shape[1]
    both = [value.astype(BF), turned(value).astype(BF)]
    if mirror:
        xs_ref[at, :, :entries] = both[0]
        xs_ref[at, :, entries:] = both[1]
    else:
        xs_ref[at, :, :MAIN] = both[0][:, :MAIN]
        xs_ref[at, :, MAIN : 2 * MAIN] = both[1][:, :MAIN]
        xs_ref[at, :, 2 * MAIN :] = jnp.concatenate([part[:, MAIN:] for part in both], axis=1)


def gathered_rows(msg_ref, q, lanes):
    groups = msg_ref.shape[0] // 4
    return jnp.concatenate([msg_ref[q * groups + g, :, lanes].astype(F32) for g in range(groups)], axis=0)


def unpack_half(msg_ref, q, half, xs_ref, at):
    ends = gathered_rows(msg_ref, q, slice(ENDS, WIDTH))
    parts = []
    for k in (2 * half, 2 * half + 1):
        main = gathered_rows(msg_ref, q, slice(k * MAIN, (k + 1) * MAIN))
        parts.append(jnp.concatenate([main, shifted(ends, k * TAIL)[:, :TAIL]], axis=1))
    put_block(xs_ref, at, jnp.concatenate(parts, axis=0), half)


def put_side_by_side(out_ref, values):
    for q, value in enumerate(values):
        out_ref[:, q * MAIN : (q + 1) * MAIN] = value[:, :MAIN].astype(out_ref.dtype)
    out_ref[:, ENDS:] = jnp.concatenate([value[:, MAIN:] for value in values], axis=1).astype(out_ref.dtype)


def side_by_side(ref):
    ends = ref[:, ENDS:].astype(F32)
    mains = [ref[:, q * MAIN : (q + 1) * MAIN].astype(F32) for q in range(4)]
    return [jnp.concatenate([main, shifted(ends, q * TAIL)[:, :TAIL]], axis=1) for q, main in enumerate(mains)]


def copy_in(x_ref, xs_ref, offset, mirror):
    for q, value in enumerate(side_by_side(x_ref)):
        put_block(xs_ref, offset + q, value, mirror)


def across(left, right):
    return lax.dot_general(left, right, (((1,), (1,)), ((), ())), preferred_element_type=F32)


def slot_products(table_ref, g_ref, xs_ref, acc_ref, mirror):
    acc_ref[...] = jnp.zeros_like(acc_ref)
    slots, _, depth, entries = g_ref.shape
    table = table_ref[...]
    first = 2 if mirror else 0
    for s in range(slots):
        left = xs_ref[table[first, s]]
        if mirror:
            value = jnp.dot(left, g_ref[s].reshape(2 * depth, entries), preferred_element_type=F32)
        else:
            ends = jnp.concatenate([g_ref[s, 0, :, MAIN:], g_ref[s, 1, :, MAIN:]], axis=1)
            value = across(left[:, :MAIN], g_ref[s, 0, :, :MAIN])
            value += across(left[:, MAIN : 2 * MAIN], g_ref[s, 1, :, :MAIN])
            value += across(left[:, 2 * MAIN :], ends)
        acc_ref[table[first + 1, s]] += value


def start_kernel(classes, small_ref, back_ref, out_ref, contrast_ref):
    blocks = back_ref.shape[0]
    cells = contrast_ref.shape[2]
    kinds = small_ref[4 : 4 + blocks, :cells]
    tables = small_ref[4 + blocks : 6 + blocks, :]
    contrast = []
    for part in range(2):
        value = jnp.zeros(kinds.shape, F32)
        for k in range(classes):
            value = jnp.where(kinds == float(k), tables[part : part + 1, k : k + 1], value)
        contrast_ref[part] = value
        contrast.append(jnp.concatenate([value] * 3, axis=1))
    real, imag = contrast
    values = []
    for q in range(blocks):
        back = back_ref[q]
        values.append(real[q : q + 1] * back + imag[q : q + 1] * turned(back))
    put_side_by_side(out_ref, values)


def share_kernel(small_ref, contrast_ref, back_ref, _, extra_ref):
    r = small_ref[2:3, 0:1].astype(jnp.int32)
    blocks, rows, _ = back_ref.shape
    half = rows // 2
    cells = contrast_ref.shape[2]
    for q in range(blocks):
        rest = jnp.where(r == 2, contrast_ref[1, q : q + 1], contrast_ref[0, q : q + 1])
        marks = []
        for _ in range(3):
            piece = rest.astype(BF).astype(F32)
            marks.append(piece)
            rest = rest - piece
        marks = jnp.concatenate(marks + [jnp.zeros((1, cells), F32)], axis=0)
        marks = jnp.concatenate([marks, jnp.zeros((4, LANES - cells), F32)], axis=1)
        value = jnp.where(r % 2 == 0, back_ref[q, :half, :MAIN], back_ref[q, half:, :MAIN])
        high = value.astype(BF).astype(F32)
        value = jnp.where(r < 2, high, value - high)
        ends = jnp.concatenate([back_ref[q, :half, MAIN:], back_ref[q, half:, MAIN:]], axis=1)
        high = ends.astype(BF).astype(F32)
        ends = jnp.concatenate([high, ends - high], axis=1)
        for g in range(half // 4):
            at = slice(4 * g, 4 * g + 4)
            d = q * (half // 4) + g
            extra_ref[d, :, :MAIN] = value[at].astype(BF)
            extra_ref[d, :, MAIN:] = jnp.where(r == 0, ends[at], marks).astype(BF)


def direct_kernel(first, table_ref, g_ref, x_ref, own_ref, other_ref, xs_ref, acc_ref):
    blocks = own_ref.shape[0]
    if first:
        copy_in(x_ref, xs_ref, 0, False)
    else:
        for q in range(blocks):
            unpack_half(x_ref, q, 0, xs_ref, q)
    slot_products(table_ref, g_ref, xs_ref, acc_ref, False)
    for q in range(blocks):
        own_ref[q] = acc_ref[q]
    put_side_by_side(other_ref, [acc_ref[blocks + q] for q in range(blocks)])


def mirror_kernel(first, table_ref, g_ref, x_ref, x_other_ref, out_ref, xs_ref, acc_ref):
    blocks = out_ref.shape[0]
    if first:
        copy_in(x_ref, xs_ref, 0, True)
        copy_in(x_other_ref, xs_ref, blocks, True)
    else:
        for q in range(blocks):
            unpack_half(x_ref, q, 1, xs_ref, q)
            unpack_half(x_other_ref, q, 1, xs_ref, blocks + q)
    slot_products(table_ref, g_ref, xs_ref, acc_ref, True)
    for q in range(blocks):
        out_ref[q] = acc_ref[q]


def pack_kernel(mirror_ref, own_ref, got_ref, *rest):
    msg_ref = rest[-1]
    blocks, rows, _ = own_ref.shape
    half = rows // 2
    got = side_by_side(got_ref)
    for q in range(blocks):
        halves = [own_ref[q] + got[q], mirror_ref[q]]
        parts = [value[p * half : (p + 1) * half] for value in halves for p in range(2)]
        ends = jnp.concatenate([part[:, MAIN:] for part in parts], axis=1)
        for g in range(half // 4):
            at = slice(4 * g, 4 * g + 4)
            d = q * (half // 4) + g
            for k, part in enumerate(parts):
                msg_ref[d, :, k * MAIN : (k + 1) * MAIN] = part[at, :MAIN].astype(BF)
            msg_ref[d, :, ENDS:WIDTH] = ends[at].astype(BF)
    if len(rest) == 2:
        msg_ref[:, :, WIDTH:] = rest[0][...]


def partial_sums(msg_ref, rows, cols):
    direct = {}
    mirror = {}

    def add(store, key, value):
        store[key] = store[key] + value if key in store else value

    for r in range(rows):
        for c in range(cols):
            d = r * cols + c
            j = 2 * r + c % 2
            for k in range(9):
                value = msg_ref[d, :, k * LANES : (k + 1) * LANES].astype(F32)
                if k < 4 or k == 8:
                    add(direct, (j, min(k, 4)), value)
                if k >= 4:
                    add(mirror, (c, k - 4), value)
    for j in range(cols):
        mirror[j, 4] = shifted(mirror[j, 4], 2 * TAIL)
    return {key: direct[key] + mirror[key] for key in direct}


def update_kernel(first, rows, cols, msg_ref, *refs):
    back_ref, contrast_ref, out_ref = refs[1:] + refs[:1] if first else refs
    lane = lax.broadcasted_iota(jnp.int32, (4, LANES), 1)
    cells = (MAIN + TAIL) // 3
    sums = partial_sums(msg_ref, rows, cols)
    current = {}
    for j in range(cols):
        if first:
            extra = [
                [msg_ref[r * cols + j, :, WIDTH + k * LANES : WIDTH + (k + 1) * LANES].astype(F32) for k in range(3)]
                for r in range(4)
            ]
            back = [extra[p][k] + extra[p + 2][k] for p in range(2) for k in range(2)]
            back.append(extra[0][2] + shifted(extra[0][2], 2 * TAIL))
            contrast = []
            for r in (1, 2):
                value = extra[r][2]
                value = jnp.broadcast_to(value[0:1] + value[1:2] + value[2:3], (4, LANES))
                moved = [value, shifted(value, TAIL), shifted(value, 2 * TAIL)]
                contrast.append(
                    [
                        jnp.where(lane < cells, moved[0], shifted(value, TAIL)),
                        jnp.where(lane < 2 * TAIL, moved[1], moved[2]),
                        jnp.where(lane < TAIL, moved[2], moved[1]),
                    ]
                )
            for k in range(5):
                back_ref[j, k] = back[k]
            for part in range(2):
                for k in range(3):
                    contrast_ref[j, part, k] = contrast[part][k]
        else:
            back = [back_ref[j, k] for k in range(5)]
            contrast = [[contrast_ref[j, part, k] for k in range(3)] for part in range(2)]
        total = [sums[j, k] + back[k] for k in range(5)]
        real, imag = contrast
        for k in range(2):
            current[j, k] = real[k] * total[k] - imag[k] * total[k + 2]
            current[j, k + 2] = real[k] * total[k + 2] + imag[k] * total[k]
        other = jnp.where(lane < TAIL, -shifted(total[4], TAIL), pltpu.roll(total[4], TAIL, 1))
        current[j, 4] = real[2] * total[4] + imag[2] * other
    for r in range(rows):
        for c in range(cols):
            d = r * cols + c
            j = 2 * r + c % 2
            for k in range(4):
                out_ref[d, :, k * LANES : (k + 1) * LANES] = current[c, k].astype(BF)
                out_ref[d, :, (k + 4) * LANES : (k + 5) * LANES] = current[j, k].astype(BF)
            ends = jnp.where(lane < 2 * TAIL, current[c, 4], shifted(current[j, 4], 2 * TAIL))
            out_ref[d, :, ENDS:WIDTH] = ends.astype(BF)


def last_kernel(rows, cols, msg_ref, out_ref):
    lane = lax.broadcasted_iota(jnp.int32, (4, LANES), 1)
    sums = partial_sums(msg_ref, rows, cols)
    for j in range(cols):
        ends = sums[j, 4]
        coded_ends = jnp.zeros((4, LANES), F32)
        for p in range(2):
            mine = (lane >= p * TAIL) & (lane < (p + 1) * TAIL)
            main = [sums[j, 2 * p], sums[j, 2 * p + 1]]
            most = jnp.maximum(jnp.maximum(jnp.abs(main[0]), jnp.abs(main[1])), jnp.where(mine, jnp.abs(ends), 0.0))
            most = jnp.max(most, axis=1, keepdims=True)
            power = jnp.floor(jnp.log2(jnp.maximum(most, SMALLEST)))
            scale = jnp.exp2(14.0 - power)
            for k in range(2):
                coded = as_integers(main[k] * scale)
                for r in range(rows):
                    out_ref[r * cols + j, :, (2 * p + k) * LANES : (2 * p + k + 1) * LANES] = coded
            coded_ends = jnp.where(mine, ends * scale, jnp.where(lane == 2 * TAIL + p, power, coded_ends))
        coded = as_integers(coded_ends)
        for r in range(rows):
            out_ref[r * cols + j, :, 2 * MAIN : 2 * MAIN + LANES] = coded


def as_integers(value):
    return jnp.clip(jnp.round(value), -32767.0, 32767.0).astype(jnp.int32).astype(jnp.int16)


def finish_kernel(msg_ref, back_ref, out_ref):
    blocks, rows, _ = out_ref.shape
    half = rows // 2
    groups = half // 4

    def rows_of(q, lanes):
        pieces = [msg_ref[q * groups + g, :, lanes].astype(jnp.int32).astype(F32) for g in range(groups)]
        return jnp.concatenate(pieces, axis=0)

    for q in range(blocks):
        ends = rows_of(q, slice(2 * MAIN, 2 * MAIN + LANES))
        for p in range(2):
            at = slice(p * half, (p + 1) * half)
            scale = jnp.exp2(ends[:, 2 * TAIL + p : 2 * TAIL + p + 1] - 14.0)
            main = rows_of(q, slice(p * MAIN, (p + 1) * MAIN))
            out_ref[q, at, :MAIN] = back_ref[q, at, :MAIN] + main * scale
            out_ref[q, at, MAIN:] = back_ref[q, at, MAIN:] + shifted(ends, p * TAIL)[:, :TAIL] * scale


def whole_call(kernel, out_shape, operands, scratch, name):
    vmem = pl.BlockSpec(memory_space=pltpu.VMEM)
    return pl.pallas_call(
        kernel,
        out_shape=out_shape,
        in_specs=[vmem] * len(operands),
        out_specs=jax.tree.map(lambda _: vmem, out_shape),
        scratch_shapes=scratch,
        compiler_params=pltpu.CompilerParams(vmem_limit_bytes=VMEM_BYTES),
        name=name,
    )(*operands)


def stacked(arrays):
    heights = [1 if array is None else array.shape[0] for array in arrays]
    total = 0
    at = 0
    for array, height in zip(arrays, heights):
        if array is not None:
            edges = ((at, sum(heights) - at - height, 0), (0, LANES - array.shape[1], 0))
            total += lax.pad(array, jnp.zeros((), array.dtype), edges).astype(F32)
        at += height
    return total


def local_owners(green_blocks, slot_rows, slot_cols, slot_count, cell_class, class_contrast, background):
    r = lax.axis_index("row")
    c = lax.axis_index("col")
    rows = lax.axis_size("row")
    cols = lax.axis_size("col")
    green = green_blocks[0, 0]
    slots, _, entries, _ = green.shape
    sources, blocks = background.shape[1:3]
    both = ("row", "col")

    small = stacked([slot_rows[0], slot_cols[0], None, None, cell_class[:, 0, :], class_contrast.T])
    line = lax.broadcasted_iota(jnp.int32, small.shape, 0)
    small = jnp.where(line == 2, r.astype(F32), jnp.where(line == 3, c.astype(F32), small))

    local_rows = small[0:1, :].astype(jnp.int32)
    local_cols = small[1:2, :].astype(jnp.int32)
    living = lax.broadcasted_iota(jnp.int32, (1, LANES), 1) < slot_count
    off_diagonal = (local_rows // 2 * cols + 2 * r + local_rows % 2) != (local_cols * cols + c)
    place = (local_rows % 2 ^ c % 2) * blocks + local_rows // 2
    spare = jnp.full_like(place, 2 * blocks)
    table = jnp.concatenate(
        [
            local_cols,
            jnp.where(living, place, spare),
            place,
            jnp.where(living & off_diagonal, local_cols, spare // 2),
        ],
        axis=0,
    )

    block = (2 * sources, entries)
    back = background[:, :, :, 0, :].transpose(2, 0, 1, 3).reshape((blocks,) + block)
    start, contrast = whole_call(
        lambda *refs: start_kernel(class_contrast.shape[0], *refs),
        (
            jax.ShapeDtypeStruct((2 * sources, WIDTH), BF),
            jax.ShapeDtypeStruct((2, blocks, entries // 3), F32),
        ),
        (small, back),
        [],
        "start",
    )

    core_pairs = [(i, i ^ 1) for i in range(cols)]
    chips = cols // 2
    arrived = []
    for hop in range(1, chips):
        pairs = []
        for a in range(rows):
            far = (a + hop) % chips
            for k in range(chips):
                for p in range(2):
                    to = {a: 2 * far + p, far: 2 * a + p}.get(k, 2 * k + 1 - p)
                    pairs.append((a * cols + 2 * k + p, a * cols + to))
        arrived.append(lax.ppermute(start, both, pairs))
    extra = whole_call(
        share_kernel,
        jax.ShapeDtypeStruct((rows * cols, 4, 3 * LANES), BF),
        (small, contrast, back, green),
        [],
        "share",
    )
    extra, *arrived = lax.optimization_barrier((extra, *arrived))
    row_mine = start
    for hop in range(1, chips):
        row_mine = jnp.where(c // 2 == (r + hop) % chips, arrived[hop - 1], row_mine)
    row_other = lax.ppermute(row_mine, "col", core_pairs)

    part = jax.ShapeDtypeStruct((blocks,) + block, F32)
    message = jax.ShapeDtypeStruct((rows * cols, 4, WIDTH), BF)
    for step in range(PRODUCTS):
        first = step == 0
        final = step + 1 == PRODUCTS
        if first:
            direct_in, mirror_in = start, (row_mine, row_other)
        else:
            direct_in, mirror_in = x_msg, (x_msg, lax.ppermute(x_msg, "col", core_pairs))
        own, other = whole_call(
            lambda *refs, first=first: direct_kernel(first, *refs),
            (part, jax.ShapeDtypeStruct((2 * sources, WIDTH), F32)),
            (table, green, direct_in),
            [
                pltpu.VMEM((blocks, 2 * sources, 2 * entries), BF),
                pltpu.VMEM((2 * blocks + 1,) + block, F32),
            ],
            f"direct_{step}",
        )
        got = lax.ppermute(other, "col", core_pairs)
        mirror = whole_call(
            lambda *refs, first=first: mirror_kernel(first, *refs),
            part,
            (table, green) + mirror_in,
            [
                pltpu.VMEM((2 * blocks, 2 * sources, 2 * entries), BF),
                pltpu.VMEM((blocks + 1,) + block, F32),
            ],
            f"mirror_{step}",
        )
        y_shape = jax.ShapeDtypeStruct((rows * cols, 4, WIDTH + 3 * LANES), BF) if first else message
        operands = (mirror, own, got) + ((extra,) if first else ())
        y_msg = whole_call(pack_kernel, y_shape, operands, [], f"pack_{step}")
        y_msg = lax.all_to_all(y_msg, both, 0, 0, tiled=True)
        run = lambda *refs, first=first: update_kernel(first, rows, cols, *refs)
        if first:
            x_msg, owner_back, owner_contrast = whole_call(
                run,
                (
                    message,
                    jax.ShapeDtypeStruct((cols, 5, 4, LANES), F32),
                    jax.ShapeDtypeStruct((cols, 2, 3, 4, LANES), F32),
                ),
                (y_msg,),
                [],
                f"update_{step}",
            )
        elif not final:
            operands = (y_msg, owner_back, owner_contrast)
            x_msg = whole_call(run, message, operands, [], f"update_{step}")
        else:
            run = lambda *refs: last_kernel(rows, cols, *refs)
            x_shape = jax.ShapeDtypeStruct((rows * cols, 4, 2 * MAIN + LANES), jnp.int16)
            x_msg = whole_call(run, x_shape, (y_msg,), [], "last")
        x_msg = lax.all_to_all(x_msg, both, 0, 0, tiled=True)
    field = whole_call(finish_kernel, part, (x_msg, back), [], "finish")
    field = field.reshape(blocks, 2, sources, entries).transpose(1, 2, 0, 3)
    return field[:, :, :, None, :]


def solution(mesh):
    in_specs = (
        P("row", "col", None, None, None, None),
        P("row", "col", None),
        P("row", "col", None),
        P("row", "col"),
        P(None, "col", None),
        P(),
        P(None, None, None, "col", None),
    )
    out_specs = P(None, None, None, "col", None)
    rows, cols = mesh.shape["row"], mesh.shape["col"]

    def local(*args):
        sources, blocks = args[6].shape[1:3]
        entries = args[6].shape[4]
        owners = (
            rows == blocks == 4
            and cols == 2 * rows
            and sources == 4 * cols
            and max(args[5].shape[0], args[1].shape[2]) <= LANES
            and entries == 2 * LANES + LANES // 4 == 3 * args[4].shape[2]
        )
        return (local_owners if owners else local_general)(*args)

    return jax.shard_map(local, mesh=mesh, in_specs=in_specs, out_specs=out_specs, check_vma=False)
```

```python
import jax
import jax.numpy as jnp
from jax import lax
from jax.experimental import pallas as pl
from jax.experimental.pallas import tpu as pltpu
from jax.sharding import PartitionSpec as P

PRODUCTS = 3
LANES = 128
SMALLEST = 2.0**-100
VMEM_BYTES = 8 * 1024 * 1024
BF = jnp.bfloat16
F32 = jnp.float32


def from_root(array, axis, root):
    mine = lax.axis_index(axis) == root
    return lax.psum(jnp.where(mine, array, jnp.zeros_like(array)), axis)


def complex_scale(field_now, contrast_re, contrast_im):
    real_part = field_now[0]
    imag_part = field_now[1]
    scaled = jnp.stack(
        [
            contrast_re * real_part - contrast_im * imag_part,
            contrast_re * imag_part + contrast_im * real_part,
        ]
    )
    return scaled.astype(BF)


def combine(products):
    return jnp.stack([products[0, 0] - products[1, 1], products[0, 1] + products[1, 0]])


def local_general(green_blocks, slot_rows, slot_cols, slot_count, cell_class, class_contrast, background):
    row_index = lax.axis_index("row")
    col_index = lax.axis_index("col")
    stride = lax.axis_size("col")
    green_tiles = green_blocks[0, 0]
    slot_total = green_tiles.shape[0]
    entries = green_tiles.shape[-1]
    sources = background.shape[1]
    col_blocks = background.shape[2]
    row_blocks = 2 * col_blocks
    local_rows = slot_rows[0, 0]
    local_cols = slot_cols[0, 0]
    global_rows = local_rows // 2 * stride + 2 * row_index + local_rows % 2
    global_cols = local_cols * stride + col_index
    off_diagonal = (global_rows != global_cols).astype(F32)
    living = (jnp.arange(slot_total) < slot_count[0, 0]).astype(F32)
    row_pick = (local_rows[:, None] == jnp.arange(row_blocks)[None, :]).astype(F32) * living[:, None]
    col_pick = (local_cols[:, None] == jnp.arange(col_blocks)[None, :]).astype(F32) * (
        living * off_diagonal
    )[:, None]
    classes = class_contrast.shape[0]
    lookup = (cell_class[:, 0, :, None] == jnp.arange(classes)[None, None, :]).astype(F32)
    values = jnp.einsum("bte,ec->btc", lookup, class_contrast, precision=lax.Precision.HIGHEST)
    contrast_re = jnp.tile(values[:, :, 0], (1, 3))
    contrast_im = jnp.tile(values[:, :, 1], (1, 3))
    start_field = background[:, :, :, 0, :]
    field_now = start_field
    current = complex_scale(field_now, contrast_re, contrast_im)
    for step_index in range(PRODUCTS):
        final_step = step_index + 1 == PRODUCTS
        halves = [from_root(current, "col", 2 * row_index + parity) for parity in range(2)]
        row_current = jnp.stack(halves, axis=3).reshape(2, sources, row_blocks, entries)
        direct_in = jnp.take(current, local_cols, axis=2)
        mirror_in = jnp.take(row_current, local_rows, axis=2)
        direct_terms = combine(
            jnp.einsum("sqoi,pksi->qpkso", green_tiles, direct_in, preferred_element_type=F32)
        )
        mirror_terms = combine(
            jnp.einsum("sqoi,pkso->qpksi", green_tiles, mirror_in, preferred_element_type=F32)
        )
        direct_part = jnp.einsum(
            "pkse,sb->pkbe", direct_terms, row_pick, precision=lax.Precision.HIGHEST
        )
        mirror_part = jnp.einsum(
            "pkse,sb->pkbe", mirror_terms, col_pick, precision=lax.Precision.HIGHEST
        )
        row_total = lax.psum(direct_part, "col")
        owned_part = lax.dynamic_index_in_dim(
            row_total.reshape(2, sources, col_blocks, 2, entries),
            col_index % 2,
            axis=3,
            keepdims=False,
        )
        direct_here = from_root(owned_part, "row", col_index // 2)
        column_total = lax.psum(mirror_part, "row")
        field_now = start_field + column_total + direct_here
        if not final_step:
            current = complex_scale(field_now, contrast_re, contrast_im)
    return field_now[:, :, :, None, :]


MAIN = 2 * LANES
TAIL = LANES // 4
ENDS = 4 * MAIN
WIDTH = ENDS + LANES
POWER = 3 * TAIL


def turned(value):
    half = value.shape[0] // 2
    return jnp.concatenate([-value[half:], value[:half]], axis=0)


def shifted(value, lanes):
    return pltpu.roll(value, LANES - lanes, 1) if lanes else value


def put_block(xs_ref, at, value, mirror):
    entries = value.shape[1]
    both = [value.astype(BF), turned(value).astype(BF)]
    if mirror:
        xs_ref[at, :, :entries] = both[0]
        xs_ref[at, :, entries:] = both[1]
    else:
        xs_ref[at, :, :MAIN] = both[0][:, :MAIN]
        xs_ref[at, :, MAIN : 2 * MAIN] = both[1][:, :MAIN]
        xs_ref[at, :, 2 * MAIN :] = jnp.concatenate([part[:, MAIN:] for part in both], axis=1)


def gathered_rows(msg_ref, q, lanes):
    groups = msg_ref.shape[0] // 4
    return jnp.concatenate([msg_ref[q * groups + g, :, lanes].astype(F32) for g in range(groups)], axis=0)


def unpack_half(msg_ref, q, half, xs_ref, at):
    ends = gathered_rows(msg_ref, q, slice(ENDS, WIDTH))
    parts = []
    for k in (2 * half, 2 * half + 1):
        main = gathered_rows(msg_ref, q, slice(k * MAIN, (k + 1) * MAIN))
        parts.append(jnp.concatenate([main, shifted(ends, k * TAIL)[:, :TAIL]], axis=1))
    put_block(xs_ref, at, jnp.concatenate(parts, axis=0), half)


def put_side_by_side(out_ref, values):
    for q, value in enumerate(values):
        out_ref[:, q * MAIN : (q + 1) * MAIN] = value[:, :MAIN].astype(out_ref.dtype)
    out_ref[:, ENDS:] = jnp.concatenate([value[:, MAIN:] for value in values], axis=1).astype(out_ref.dtype)


def side_by_side(ref):
    ends = ref[:, ENDS:].astype(F32)
    mains = [ref[:, q * MAIN : (q + 1) * MAIN].astype(F32) for q in range(4)]
    return [jnp.concatenate([main, shifted(ends, q * TAIL)[:, :TAIL]], axis=1) for q, main in enumerate(mains)]


def copy_in(x_ref, xs_ref, offset, mirror):
    for q, value in enumerate(side_by_side(x_ref)):
        put_block(xs_ref, offset + q, value, mirror)


def across(left, right):
    return lax.dot_general(left, right, (((1,), (1,)), ((), ())), preferred_element_type=F32)


def slot_products(table_ref, g_ref, xs_ref, acc_ref, mirror, start_ref=None):
    acc_ref[...] = jnp.zeros_like(acc_ref)
    if start_ref is not None:
        acc_ref[: start_ref.shape[0]] = start_ref[...]
    slots, _, depth, entries = g_ref.shape
    table = table_ref[...]
    first = 2 if mirror else 0
    for s in range(slots):
        left = xs_ref[table[first, s]]
        if mirror:
            value = jnp.dot(left, g_ref[s].reshape(2 * depth, entries), preferred_element_type=F32)
        else:
            ends = jnp.concatenate([g_ref[s, 0, :, MAIN:], g_ref[s, 1, :, MAIN:]], axis=1)
            value = across(left[:, :MAIN], g_ref[s, 0, :, :MAIN])
            value += across(left[:, MAIN : 2 * MAIN], g_ref[s, 1, :, :MAIN])
            value += across(left[:, 2 * MAIN :], ends)
        acc_ref[table[first + 1, s]] += value


def start_kernel(classes, small_ref, back_ref, out_ref, contrast_ref):
    blocks = back_ref.shape[0]
    cells = contrast_ref.shape[2]
    kinds = small_ref[4 : 4 + blocks, :cells]
    tables = small_ref[4 + blocks : 6 + blocks, :]
    contrast = []
    for part in range(2):
        value = jnp.zeros(kinds.shape, F32)
        for k in range(classes):
            value = jnp.where(kinds == float(k), tables[part : part + 1, k : k + 1], value)
        contrast_ref[part] = value
        contrast.append(jnp.concatenate([value] * 3, axis=1))
    real, imag = contrast
    values = []
    for q in range(blocks):
        back = back_ref[q]
        values.append(real[q : q + 1] * back + imag[q : q + 1] * turned(back))
    put_side_by_side(out_ref, values)


def share_kernel(small_ref, contrast_ref, back_ref, _, marks_ref, share_ref):
    r = small_ref[2:3, 0:1]
    cells = contrast_ref.shape[2]
    for q in range(back_ref.shape[0]):
        share_ref[q] = jnp.where(r == 0.0, back_ref[q], 0.0)
        marks = []
        for part in range(2):
            value = contrast_ref[part, q : q + 1] * 2.0**15
            marks += [jnp.round(value), (value - jnp.round(value)) * 2.0**16]
        marks = jnp.concatenate([whole(part) for part in marks], axis=0)
        marks_ref[q] = jnp.concatenate([marks, jnp.zeros((4, LANES - cells), F32)], axis=1)


def whole(value):
    return jnp.clip(jnp.round(value), -32767.0, 32767.0)


def as_integers(value):
    return value.astype(jnp.int32).astype(jnp.int16)


def as_floats(value):
    return value.astype(jnp.int32).astype(F32)


def direct_kernel(first, table_ref, g_ref, x_ref, own_ref, other_ref, xs_ref, acc_ref):
    blocks = own_ref.shape[0]
    if first:
        copy_in(x_ref, xs_ref, 0, False)
    else:
        for q in range(blocks):
            unpack_half(x_ref, q, 0, xs_ref, q)
    slot_products(table_ref, g_ref, xs_ref, acc_ref, False)
    for q in range(blocks):
        own_ref[q] = acc_ref[q]
    put_side_by_side(other_ref, [acc_ref[blocks + q] for q in range(blocks)])


def mirror_kernel(first, table_ref, g_ref, x_ref, x_other_ref, *refs):
    *start, out_ref, xs_ref, acc_ref = refs
    blocks = out_ref.shape[0]
    if first:
        copy_in(x_ref, xs_ref, 0, True)
        copy_in(x_other_ref, xs_ref, blocks, True)
    else:
        for q in range(blocks):
            unpack_half(x_ref, q, 1, xs_ref, q)
            unpack_half(x_other_ref, q, 1, xs_ref, blocks + q)
    slot_products(table_ref, g_ref, xs_ref, acc_ref, True, *start)
    for q in range(blocks):
        out_ref[q] = acc_ref[q]


def pack_kernel(mirror_ref, own_ref, got_ref, *rest):
    msg_ref = rest[-1]
    blocks, rows, _ = own_ref.shape
    half = rows // 2
    lane = lax.broadcasted_iota(jnp.int32, (4, LANES), 1)
    got = side_by_side(got_ref)
    for q in range(blocks):
        halves = [own_ref[q] + got[q], mirror_ref[q]]
        parts = [value[p * half : (p + 1) * half] for value in halves for p in range(2)]
        power, scale = row_power(parts)
        parts = [whole(part * scale) for part in parts]
        ends = jnp.concatenate([part[:, MAIN:] for part in parts], axis=1)
        marks = rest[0][q] if len(rest) == 2 else jnp.zeros((4, LANES), F32)
        for g in range(half // 4):
            at = slice(4 * g, 4 * g + 4)
            d = q * (half // 4) + g
            for k, part in enumerate(parts):
                msg_ref[d, :, k * MAIN : (k + 1) * MAIN] = as_integers(part[at, :MAIN])
            msg_ref[d, :, ENDS:WIDTH] = as_integers(ends[at])
            msg_ref[d, :, WIDTH:] = as_integers(jnp.where(lane == POWER, power[at], marks))


def row_power(parts):
    most = jnp.abs(parts[0])
    for part in parts[1:]:
        most = jnp.maximum(most, jnp.abs(part))
    most = jnp.max(most, axis=1, keepdims=True)
    power = jnp.floor(jnp.log2(jnp.maximum(most, SMALLEST)))
    return power, jnp.exp2(14.0 - power)


def partial_sums(msg_ref, rows, cols):
    direct = {}
    mirror = {}

    def add(store, key, value):
        store[key] = store[key] + value if key in store else value

    for r in range(rows):
        for c in range(cols):
            d = r * cols + c
            j = 2 * r + c % 2
            scale = jnp.exp2(as_floats(msg_ref[d, :, WIDTH : WIDTH + LANES])[:, POWER : POWER + 1] - 14.0)
            for k in range(9):
                value = as_floats(msg_ref[d, :, k * LANES : (k + 1) * LANES]) * scale
                if k < 4 or k == 8:
                    add(direct, (j, min(k, 4)), value)
                if k >= 4:
                    add(mirror, (c, k - 4), value)
    for j in range(cols):
        mirror[j, 4] = shifted(mirror[j, 4], 2 * TAIL)
    return {key: direct[key] + mirror[key] for key in direct}


def update_kernel(first, rows, cols, msg_ref, *refs):
    contrast_ref, out_ref = refs[::-1] if first else refs
    lane = lax.broadcasted_iota(jnp.int32, (4, LANES), 1)
    cells = (MAIN + TAIL) // 3
    sums = partial_sums(msg_ref, rows, cols)
    current = {}
    for j in range(cols):
        if first:
            marks = as_floats(msg_ref[j, :, WIDTH : WIDTH + LANES])
            contrast = []
            for row in (0, 2):
                value = marks[row : row + 1] * 2.0**-15 + marks[row + 1 : row + 2] * 2.0**-31
                value = jnp.broadcast_to(value, (4, LANES))
                near, far = shifted(value, TAIL), shifted(value, 2 * TAIL)
                contrast.append(
                    [
                        jnp.where(lane < cells, value, near),
                        jnp.where(lane < 2 * TAIL, near, far),
                        jnp.where(lane < TAIL, far, near),
                    ]
                )
            for part in range(2):
                for k in range(3):
                    contrast_ref[j, part, k] = contrast[part][k]
        else:
            contrast = [[contrast_ref[j, part, k] for k in range(3)] for part in range(2)]
        total = [sums[j, k] for k in range(5)]
        real, imag = contrast
        for k in range(2):
            current[j, k] = real[k] * total[k] - imag[k] * total[k + 2]
            current[j, k + 2] = real[k] * total[k + 2] + imag[k] * total[k]
        other = jnp.where(lane < TAIL, -shifted(total[4], TAIL), pltpu.roll(total[4], TAIL, 1))
        current[j, 4] = real[2] * total[4] + imag[2] * other
    for r in range(rows):
        for c in range(cols):
            d = r * cols + c
            j = 2 * r + c % 2
            for k in range(4):
                out_ref[d, :, k * LANES : (k + 1) * LANES] = current[c, k].astype(BF)
                out_ref[d, :, (k + 4) * LANES : (k + 5) * LANES] = current[j, k].astype(BF)
            ends = jnp.where(lane < 2 * TAIL, current[c, 4], shifted(current[j, 4], 2 * TAIL))
            out_ref[d, :, ENDS:WIDTH] = ends.astype(BF)


def last_kernel(rows, cols, msg_ref, out_ref):
    lane = lax.broadcasted_iota(jnp.int32, (4, LANES), 1)
    sums = partial_sums(msg_ref, rows, cols)
    for j in range(cols):
        ends = jnp.zeros((4, LANES), F32)
        for p in range(2):
            mine = (lane >= p * TAIL) & (lane < (p + 1) * TAIL)
            tail = jnp.where(mine, sums[j, 4], 0.0)
            power, scale = row_power([sums[j, 2 * p], sums[j, 2 * p + 1], tail])
            for k in range(2 * p, 2 * p + 2):
                coded = as_integers(whole(sums[j, k] * scale))
                for r in range(rows):
                    out_ref[r * cols + j, :, k * LANES : (k + 1) * LANES] = coded
            ends = jnp.where(mine, whole(tail * scale), jnp.where(lane == 2 * TAIL + p, power, ends))
        coded = as_integers(ends)
        for r in range(rows):
            out_ref[r * cols + j, :, 2 * MAIN : 2 * MAIN + LANES] = coded


def finish_kernel(msg_ref, back_ref, out_ref):
    blocks, rows, _ = out_ref.shape
    half = rows // 2
    groups = half // 4

    def rows_of(q, lanes):
        return jnp.concatenate([as_floats(msg_ref[q * groups + g, :, lanes]) for g in range(groups)], axis=0)

    for q in range(blocks):
        ends = rows_of(q, slice(2 * MAIN, 2 * MAIN + LANES))
        for p in range(2):
            at = slice(p * half, (p + 1) * half)
            scale = jnp.exp2(ends[:, 2 * TAIL + p : 2 * TAIL + p + 1] - 14.0)
            main = rows_of(q, slice(p * MAIN, (p + 1) * MAIN))
            out_ref[q, at, :MAIN] = back_ref[q, at, :MAIN] + main * scale
            out_ref[q, at, MAIN:] = back_ref[q, at, MAIN:] + shifted(ends, p * TAIL)[:, :TAIL] * scale


def whole_call(kernel, out_shape, operands, scratch, name):
    vmem = pl.BlockSpec(memory_space=pltpu.VMEM)
    return pl.pallas_call(
        kernel,
        out_shape=out_shape,
        in_specs=[vmem] * len(operands),
        out_specs=jax.tree.map(lambda _: vmem, out_shape),
        scratch_shapes=scratch,
        compiler_params=pltpu.CompilerParams(vmem_limit_bytes=VMEM_BYTES),
        name=name,
    )(*operands)


def stacked(arrays):
    heights = [1 if array is None else array.shape[0] for array in arrays]
    total = 0
    at = 0
    for array, height in zip(arrays, heights):
        if array is not None:
            edges = ((at, sum(heights) - at - height, 0), (0, LANES - array.shape[1], 0))
            total += lax.pad(array, jnp.zeros((), array.dtype), edges).astype(F32)
        at += height
    return total


def local_owners(green_blocks, slot_rows, slot_cols, slot_count, cell_class, class_contrast, background):
    r = lax.axis_index("row")
    c = lax.axis_index("col")
    rows = lax.axis_size("row")
    cols = lax.axis_size("col")
    green = green_blocks[0, 0]
    slots, _, entries, _ = green.shape
    sources, blocks = background.shape[1:3]
    both = ("row", "col")

    small = stacked([slot_rows[0], slot_cols[0], None, None, cell_class[:, 0, :], class_contrast.T])
    line = lax.broadcasted_iota(jnp.int32, small.shape, 0)
    small = jnp.where(line == 2, r.astype(F32), jnp.where(line == 3, c.astype(F32), small))

    local_rows = small[0:1, :].astype(jnp.int32)
    local_cols = small[1:2, :].astype(jnp.int32)
    living = lax.broadcasted_iota(jnp.int32, (1, LANES), 1) < slot_count
    off_diagonal = (local_rows // 2 * cols + 2 * r + local_rows % 2) != (local_cols * cols + c)
    place = (local_rows % 2 ^ c % 2) * blocks + local_rows // 2
    spare = jnp.full_like(place, 2 * blocks)
    table = jnp.concatenate(
        [
            local_cols,
            jnp.where(living, place, spare),
            place,
            jnp.where(living & off_diagonal, local_cols, spare // 2),
        ],
        axis=0,
    )

    block = (2 * sources, entries)
    back = background[:, :, :, 0, :].transpose(2, 0, 1, 3).reshape((blocks,) + block)
    start, contrast = whole_call(
        lambda *refs: start_kernel(class_contrast.shape[0], *refs),
        (
            jax.ShapeDtypeStruct((2 * sources, WIDTH), BF),
            jax.ShapeDtypeStruct((2, blocks, entries // 3), F32),
        ),
        (small, back),
        [],
        "start",
    )

    core_pairs = [(i, i ^ 1) for i in range(cols)]
    chips = cols // 2
    arrived = []
    for hop in range(1, chips):
        pairs = []
        for a in range(rows):
            far = (a + hop) % chips
            for k in range(chips):
                for p in range(2):
                    to = {a: 2 * far + p, far: 2 * a + p}.get(k, 2 * k + 1 - p)
                    pairs.append((a * cols + 2 * k + p, a * cols + to))
        arrived.append(lax.ppermute(start, both, pairs))
    marks, back_share = whole_call(
        share_kernel,
        (
            jax.ShapeDtypeStruct((blocks, 4, LANES), F32),
            jax.ShapeDtypeStruct((blocks,) + block, F32),
        ),
        (small, contrast, back, green),
        [],
        "share",
    )
    marks, *arrived = lax.optimization_barrier((marks, *arrived))
    row_mine = start
    for hop in range(1, chips):
        row_mine = jnp.where(c // 2 == (r + hop) % chips, arrived[hop - 1], row_mine)
    row_other = lax.ppermute(row_mine, "col", core_pairs)

    part = jax.ShapeDtypeStruct((blocks,) + block, F32)
    message = jax.ShapeDtypeStruct((rows * cols, 4, WIDTH), BF)
    for step in range(PRODUCTS):
        first = step == 0
        final = step + 1 == PRODUCTS
        if first:
            direct_in, mirror_in = start, (row_mine, row_other)
        else:
            direct_in, mirror_in = x_msg, (x_msg, lax.ppermute(x_msg, "col", core_pairs))
        own, other = whole_call(
            lambda *refs, first=first: direct_kernel(first, *refs),
            (part, jax.ShapeDtypeStruct((2 * sources, WIDTH), F32)),
            (table, green, direct_in),
            [
                pltpu.VMEM((blocks, 2 * sources, 2 * entries), BF),
                pltpu.VMEM((2 * blocks + 1,) + block, F32),
            ],
            f"direct_{step}",
        )
        got = lax.ppermute(other, "col", core_pairs)
        mirror = whole_call(
            lambda *refs, first=first: mirror_kernel(first, *refs),
            part,
            (table, green) + mirror_in + (() if final else (back_share,)),
            [
                pltpu.VMEM((2 * blocks, 2 * sources, 2 * entries), BF),
                pltpu.VMEM((blocks + 1,) + block, F32),
            ],
            f"mirror_{step}",
        )
        y_shape = jax.ShapeDtypeStruct((rows * cols, 4, WIDTH + LANES), jnp.int16)
        operands = (mirror, own, got) + ((marks,) if first else ())
        y_msg = whole_call(pack_kernel, y_shape, operands, [], f"pack_{step}")
        y_msg = lax.all_to_all(y_msg, both, 0, 0, tiled=True)
        run = lambda *refs, first=first: update_kernel(first, rows, cols, *refs)
        if first:
            x_msg, owner_contrast = whole_call(
                run,
                (message, jax.ShapeDtypeStruct((cols, 2, 3, 4, LANES), F32)),
                (y_msg,),
                [],
                f"update_{step}",
            )
        elif not final:
            x_msg = whole_call(run, message, (y_msg, owner_contrast), [], f"update_{step}")
        else:
            run = lambda *refs: last_kernel(rows, cols, *refs)
            x_shape = jax.ShapeDtypeStruct((rows * cols, 4, 2 * MAIN + LANES), jnp.int16)
            x_msg = whole_call(run, x_shape, (y_msg,), [], "last")
        x_msg = lax.all_to_all(x_msg, both, 0, 0, tiled=True)
    field = whole_call(finish_kernel, part, (x_msg, back), [], "finish")
    field = field.reshape(blocks, 2, sources, entries).transpose(1, 2, 0, 3)
    return field[:, :, :, None, :]


def solution(mesh):
    in_specs = (
        P("row", "col", None, None, None, None),
        P("row", "col", None),
        P("row", "col", None),
        P("row", "col"),
        P(None, "col", None),
        P(),
        P(None, None, None, "col", None),
    )
    out_specs = P(None, None, None, "col", None)
    rows, cols = mesh.shape["row"], mesh.shape["col"]

    def local(*args):
        sources, blocks = args[6].shape[1:3]
        entries = args[6].shape[4]
        owners = (
            rows == blocks == 4
            and cols == 2 * rows
            and sources == 4 * cols
            and max(args[5].shape[0], args[1].shape[2]) <= LANES
            and entries == 2 * LANES + LANES // 4 == 3 * args[4].shape[2]
        )
        return (local_owners if owners else local_general)(*args)

    return jax.shard_map(local, mesh=mesh, in_specs=in_specs, out_specs=out_specs, check_vma=False)
```

```python
import jax
import jax.numpy as jnp
from jax import lax
from jax.experimental import pallas as pl
from jax.experimental.pallas import tpu as pltpu
from jax.sharding import PartitionSpec as P

PRODUCTS = 3
LANES = 128
SMALLEST = 2.0**-100
VMEM_BYTES = 8 * 1024 * 1024
BF = jnp.bfloat16
F32 = jnp.float32


def from_root(array, axis, root):
    mine = lax.axis_index(axis) == root
    return lax.psum(jnp.where(mine, array, jnp.zeros_like(array)), axis)


def complex_scale(field_now, contrast_re, contrast_im):
    real_part = field_now[0]
    imag_part = field_now[1]
    scaled = jnp.stack(
        [
            contrast_re * real_part - contrast_im * imag_part,
            contrast_re * imag_part + contrast_im * real_part,
        ]
    )
    return scaled.astype(BF)


def combine(products):
    return jnp.stack([products[0, 0] - products[1, 1], products[0, 1] + products[1, 0]])


def local_general(green_blocks, slot_rows, slot_cols, slot_count, cell_class, class_contrast, background):
    row_index = lax.axis_index("row")
    col_index = lax.axis_index("col")
    stride = lax.axis_size("col")
    green_tiles = green_blocks[0, 0]
    slot_total = green_tiles.shape[0]
    entries = green_tiles.shape[-1]
    sources = background.shape[1]
    col_blocks = background.shape[2]
    row_blocks = 2 * col_blocks
    local_rows = slot_rows[0, 0]
    local_cols = slot_cols[0, 0]
    global_rows = local_rows // 2 * stride + 2 * row_index + local_rows % 2
    global_cols = local_cols * stride + col_index
    off_diagonal = (global_rows != global_cols).astype(F32)
    living = (jnp.arange(slot_total) < slot_count[0, 0]).astype(F32)
    row_pick = (local_rows[:, None] == jnp.arange(row_blocks)[None, :]).astype(F32) * living[:, None]
    col_pick = (local_cols[:, None] == jnp.arange(col_blocks)[None, :]).astype(F32) * (
        living * off_diagonal
    )[:, None]
    classes = class_contrast.shape[0]
    lookup = (cell_class[:, 0, :, None] == jnp.arange(classes)[None, None, :]).astype(F32)
    values = jnp.einsum("bte,ec->btc", lookup, class_contrast, precision=lax.Precision.HIGHEST)
    contrast_re = jnp.tile(values[:, :, 0], (1, 3))
    contrast_im = jnp.tile(values[:, :, 1], (1, 3))
    start_field = background[:, :, :, 0, :]
    field_now = start_field
    current = complex_scale(field_now, contrast_re, contrast_im)
    for step_index in range(PRODUCTS):
        final_step = step_index + 1 == PRODUCTS
        halves = [from_root(current, "col", 2 * row_index + parity) for parity in range(2)]
        row_current = jnp.stack(halves, axis=3).reshape(2, sources, row_blocks, entries)
        direct_in = jnp.take(current, local_cols, axis=2)
        mirror_in = jnp.take(row_current, local_rows, axis=2)
        direct_terms = combine(
            jnp.einsum("sqoi,pksi->qpkso", green_tiles, direct_in, preferred_element_type=F32)
        )
        mirror_terms = combine(
            jnp.einsum("sqoi,pkso->qpksi", green_tiles, mirror_in, preferred_element_type=F32)
        )
        direct_part = jnp.einsum(
            "pkse,sb->pkbe", direct_terms, row_pick, precision=lax.Precision.HIGHEST
        )
        mirror_part = jnp.einsum(
            "pkse,sb->pkbe", mirror_terms, col_pick, precision=lax.Precision.HIGHEST
        )
        row_total = lax.psum(direct_part, "col")
        owned_part = lax.dynamic_index_in_dim(
            row_total.reshape(2, sources, col_blocks, 2, entries),
            col_index % 2,
            axis=3,
            keepdims=False,
        )
        direct_here = from_root(owned_part, "row", col_index // 2)
        column_total = lax.psum(mirror_part, "row")
        field_now = start_field + column_total + direct_here
        if not final_step:
            current = complex_scale(field_now, contrast_re, contrast_im)
    return field_now[:, :, :, None, :]


MAIN = 2 * LANES
TAIL = LANES // 4
ENDS = 4 * MAIN
WIDTH = ENDS + LANES
POWER = 3 * TAIL


def turned(value):
    half = value.shape[0] // 2
    return jnp.concatenate([-value[half:], value[:half]], axis=0)


def shifted(value, lanes):
    return pltpu.roll(value, LANES - lanes, 1) if lanes else value


def put_block(xs_ref, at, value, mirror):
    entries = value.shape[1]
    both = [value.astype(BF), turned(value).astype(BF)]
    if mirror:
        xs_ref[at, :, :entries] = both[0]
        xs_ref[at, :, entries:] = both[1]
    else:
        xs_ref[at, :, :MAIN] = both[0][:, :MAIN]
        xs_ref[at, :, MAIN : 2 * MAIN] = both[1][:, :MAIN]
        xs_ref[at, :, 2 * MAIN :] = jnp.concatenate([part[:, MAIN:] for part in both], axis=1)


def gathered_rows(msg_ref, q, lanes):
    groups = msg_ref.shape[0] // 4
    return jnp.concatenate([msg_ref[q * groups + g, :, lanes].astype(F32) for g in range(groups)], axis=0)


def unpack_half(msg_ref, q, half, xs_ref, at):
    ends = gathered_rows(msg_ref, q, slice(ENDS, WIDTH))
    parts = []
    for k in (2 * half, 2 * half + 1):
        main = gathered_rows(msg_ref, q, slice(k * MAIN, (k + 1) * MAIN))
        parts.append(jnp.concatenate([main, shifted(ends, k * TAIL)[:, :TAIL]], axis=1))
    put_block(xs_ref, at, jnp.concatenate(parts, axis=0), half)


def put_side_by_side(out_ref, values):
    for q, value in enumerate(values):
        out_ref[:, q * MAIN : (q + 1) * MAIN] = value[:, :MAIN].astype(out_ref.dtype)
    out_ref[:, ENDS:] = jnp.concatenate([value[:, MAIN:] for value in values], axis=1).astype(out_ref.dtype)


def side_by_side(ref):
    ends = ref[:, ENDS:].astype(F32)
    mains = [ref[:, q * MAIN : (q + 1) * MAIN].astype(F32) for q in range(4)]
    return [jnp.concatenate([main, shifted(ends, q * TAIL)[:, :TAIL]], axis=1) for q, main in enumerate(mains)]


def copy_in(x_ref, xs_ref, offset, mirror):
    for q, value in enumerate(side_by_side(x_ref)):
        put_block(xs_ref, offset + q, value, mirror)


def across(left, right):
    return lax.dot_general(left, right, (((1,), (1,)), ((), ())), preferred_element_type=F32)


def slot_products(table_ref, g_ref, xs_ref, acc_ref, mirror, start_ref=None):
    acc_ref[...] = jnp.zeros_like(acc_ref)
    if start_ref is not None:
        acc_ref[: start_ref.shape[0]] = start_ref[...]
    slots, _, depth, entries = g_ref.shape
    table = table_ref[...]
    first = 2 if mirror else 0
    for s in range(slots):
        left = xs_ref[table[first, s]]
        if mirror:
            value = jnp.dot(left, g_ref[s].reshape(2 * depth, entries), preferred_element_type=F32)
        else:
            ends = jnp.concatenate([g_ref[s, 0, :, MAIN:], g_ref[s, 1, :, MAIN:]], axis=1)
            value = across(left[:, :MAIN], g_ref[s, 0, :, :MAIN])
            value += across(left[:, MAIN : 2 * MAIN], g_ref[s, 1, :, :MAIN])
            value += across(left[:, 2 * MAIN :], ends)
        acc_ref[table[first + 1, s]] += value


def start_kernel(classes, small_ref, back_ref, out_ref, contrast_ref):
    blocks = back_ref.shape[0]
    cells = contrast_ref.shape[2]
    kinds = small_ref[4 : 4 + blocks, :cells]
    tables = small_ref[4 + blocks : 6 + blocks, :]
    contrast = []
    for part in range(2):
        value = jnp.zeros(kinds.shape, F32)
        for k in range(classes):
            value = jnp.where(kinds == float(k), tables[part : part + 1, k : k + 1], value)
        contrast_ref[part] = value
        contrast.append(jnp.concatenate([value] * 3, axis=1))
    real, imag = contrast
    values = []
    for q in range(blocks):
        back = back_ref[q]
        values.append(real[q : q + 1] * back + imag[q : q + 1] * turned(back))
    put_side_by_side(out_ref, values)


def share_kernel(small_ref, contrast_ref, back_ref, _, marks_ref, share_ref):
    r = small_ref[2:3, 0:1]
    cells = contrast_ref.shape[2]
    for q in range(back_ref.shape[0]):
        share_ref[q] = jnp.where(r == 0.0, back_ref[q], 0.0)
        marks = []
        for part in range(2):
            value = contrast_ref[part, q : q + 1] * 2.0**15
            rest = (value - jnp.round(value)) * 2.0**16
            marks += [jnp.round(value), jnp.clip(jnp.round(rest), -32767.0, 32767.0)]
        marks = jnp.concatenate(marks, axis=0)
        marks_ref[q] = jnp.concatenate([marks, jnp.zeros((4, LANES - cells), F32)], axis=1)


def as_integers(value):
    return value.astype(jnp.int32).astype(jnp.int16)


def as_floats(value):
    return value.astype(jnp.int32).astype(F32)


def direct_kernel(first, table_ref, g_ref, x_ref, own_ref, other_ref, xs_ref, acc_ref):
    blocks = own_ref.shape[0]
    if first:
        copy_in(x_ref, xs_ref, 0, False)
    else:
        for q in range(blocks):
            unpack_half(x_ref, q, 0, xs_ref, q)
    slot_products(table_ref, g_ref, xs_ref, acc_ref, False)
    for q in range(blocks):
        own_ref[q] = acc_ref[q]
    put_side_by_side(other_ref, [acc_ref[blocks + q] for q in range(blocks)])


def mirror_kernel(first, table_ref, g_ref, x_ref, x_other_ref, *refs):
    *start, out_ref, xs_ref, acc_ref = refs
    blocks = out_ref.shape[0]
    if first:
        copy_in(x_ref, xs_ref, 0, True)
        copy_in(x_other_ref, xs_ref, blocks, True)
    else:
        for q in range(blocks):
            unpack_half(x_ref, q, 1, xs_ref, q)
            unpack_half(x_other_ref, q, 1, xs_ref, blocks + q)
    slot_products(table_ref, g_ref, xs_ref, acc_ref, True, *start)
    for q in range(blocks):
        out_ref[q] = acc_ref[q]


def pack_kernel(mirror_ref, own_ref, got_ref, *rest):
    msg_ref = rest[-1]
    coded = msg_ref.dtype != BF
    blocks, rows, _ = own_ref.shape
    half = rows // 2
    lane = lax.broadcasted_iota(jnp.int32, (half, LANES), 1)
    got = side_by_side(got_ref)
    for q in range(blocks):
        halves = [own_ref[q] + got[q], mirror_ref[q]]
        parts = [value[p * half : (p + 1) * half] for value in halves for p in range(2)]
        if coded:
            power, scale = row_power(parts)
            parts = [jnp.round(part * scale) for part in parts]
        parts = [part[:, :MAIN] for part in parts] + [jnp.concatenate([part[:, MAIN:] for part in parts], axis=1)]
        if coded:
            marks = jnp.concatenate([rest[0][q]] * (half // 4), axis=0) if len(rest) == 2 else 0.0
            parts.append(jnp.where(lane == POWER, power, marks))
            parts = [part.astype(jnp.int32) for part in parts]
        for g in range(half // 4):
            at = slice(4 * g, 4 * g + 4)
            d = q * (half // 4) + g
            for k, part in enumerate(parts):
                lanes = slice(k * MAIN, (k + 1) * MAIN) if k < 4 else slice(ENDS + (k - 4) * LANES, ENDS + (k - 3) * LANES)
                msg_ref[d, :, lanes] = part[at].astype(msg_ref.dtype)


def row_power(parts):
    most = jnp.abs(parts[0])
    for part in parts[1:]:
        most = jnp.maximum(most, jnp.abs(part))
    most = jnp.max(most, axis=1, keepdims=True)
    power = jnp.floor(jnp.log2(jnp.maximum(most, SMALLEST)) + 2.0**-12)
    return power, jnp.exp2(14.0 - power)


def partial_sums(msg_ref, rows, cols):
    direct = {}
    mirror = {}
    coded = msg_ref.dtype != BF

    def add(store, key, value):
        store[key] = store[key] + value if key in store else value

    for r in range(rows):
        for c in range(cols):
            d = r * cols + c
            j = 2 * r + c % 2
            if coded:
                scale = jnp.exp2(as_floats(msg_ref[d, :, WIDTH : WIDTH + LANES])[:, POWER : POWER + 1] - 14.0)
            for k in range(9):
                value = msg_ref[d, :, k * LANES : (k + 1) * LANES]
                value = as_floats(value) * scale if coded else value.astype(F32)
                if k < 4 or k == 8:
                    add(direct, (j, min(k, 4)), value)
                if k >= 4:
                    add(mirror, (c, k - 4), value)
    for j in range(cols):
        mirror[j, 4] = shifted(mirror[j, 4], 2 * TAIL)
    return {key: direct[key] + mirror[key] for key in direct}


def update_kernel(first, rows, cols, msg_ref, *refs):
    contrast_ref, out_ref = refs[::-1] if first else refs
    lane = lax.broadcasted_iota(jnp.int32, (4, LANES), 1)
    cells = (MAIN + TAIL) // 3
    sums = partial_sums(msg_ref, rows, cols)
    current = {}
    for j in range(cols):
        if first:
            marks = as_floats(msg_ref[j, :, WIDTH : WIDTH + LANES])
            contrast = []
            for row in (0, 2):
                value = marks[row : row + 1] * 2.0**-15 + marks[row + 1 : row + 2] * 2.0**-31
                value = jnp.broadcast_to(value, (4, LANES))
                near, far = shifted(value, TAIL), shifted(value, 2 * TAIL)
                contrast.append(
                    [
                        jnp.where(lane < cells, value, near),
                        jnp.where(lane < 2 * TAIL, near, far),
                        jnp.where(lane < TAIL, far, near),
                    ]
                )
            for part in range(2):
                for k in range(3):
                    contrast_ref[j, part, k] = contrast[part][k]
        else:
            contrast = [[contrast_ref[j, part, k] for k in range(3)] for part in range(2)]
        total = [sums[j, k] for k in range(5)]
        real, imag = contrast
        for k in range(2):
            current[j, k] = real[k] * total[k] - imag[k] * total[k + 2]
            current[j, k + 2] = real[k] * total[k + 2] + imag[k] * total[k]
        other = jnp.where(lane < TAIL, -shifted(total[4], TAIL), pltpu.roll(total[4], TAIL, 1))
        current[j, 4] = real[2] * total[4] + imag[2] * other
    for r in range(rows):
        for c in range(cols):
            d = r * cols + c
            j = 2 * r + c % 2
            for k in range(4):
                out_ref[d, :, k * LANES : (k + 1) * LANES] = current[c, k].astype(BF)
                out_ref[d, :, (k + 4) * LANES : (k + 5) * LANES] = current[j, k].astype(BF)
            ends = jnp.where(lane < 2 * TAIL, current[c, 4], shifted(current[j, 4], 2 * TAIL))
            out_ref[d, :, ENDS:WIDTH] = ends.astype(BF)


def last_kernel(rows, cols, msg_ref, out_ref):
    lane = lax.broadcasted_iota(jnp.int32, (4, LANES), 1)
    sums = partial_sums(msg_ref, rows, cols)
    for j in range(cols):
        ends = jnp.zeros((4, LANES), F32)
        for p in range(2):
            mine = (lane >= p * TAIL) & (lane < (p + 1) * TAIL)
            tail = jnp.where(mine, sums[j, 4], 0.0)
            power, scale = row_power([sums[j, 2 * p], sums[j, 2 * p + 1], tail])
            for k in range(2 * p, 2 * p + 2):
                coded = as_integers(jnp.round(sums[j, k] * scale))
                for r in range(rows):
                    out_ref[r * cols + j, :, k * LANES : (k + 1) * LANES] = coded
            ends = jnp.where(mine, jnp.round(tail * scale), jnp.where(lane == 2 * TAIL + p, power, ends))
        coded = as_integers(ends)
        for r in range(rows):
            out_ref[r * cols + j, :, 2 * MAIN : 2 * MAIN + LANES] = coded


def finish_kernel(msg_ref, back_ref, out_ref):
    blocks, rows, _ = out_ref.shape
    half = rows // 2
    groups = half // 4

    def rows_of(q, lanes):
        return jnp.concatenate([as_floats(msg_ref[q * groups + g, :, lanes]) for g in range(groups)], axis=0)

    for q in range(blocks):
        ends = rows_of(q, slice(2 * MAIN, 2 * MAIN + LANES))
        for p in range(2):
            at = slice(p * half, (p + 1) * half)
            scale = jnp.exp2(ends[:, 2 * TAIL + p : 2 * TAIL + p + 1] - 14.0)
            main = rows_of(q, slice(p * MAIN, (p + 1) * MAIN))
            out_ref[q, at, :MAIN] = back_ref[q, at, :MAIN] + main * scale
            out_ref[q, at, MAIN:] = back_ref[q, at, MAIN:] + shifted(ends, p * TAIL)[:, :TAIL] * scale


def whole_call(kernel, out_shape, operands, scratch, name):
    vmem = pl.BlockSpec(memory_space=pltpu.VMEM)
    return pl.pallas_call(
        kernel,
        out_shape=out_shape,
        in_specs=[vmem] * len(operands),
        out_specs=jax.tree.map(lambda _: vmem, out_shape),
        scratch_shapes=scratch,
        compiler_params=pltpu.CompilerParams(vmem_limit_bytes=VMEM_BYTES),
        name=name,
    )(*operands)


def stacked(arrays):
    heights = [1 if array is None else array.shape[0] for array in arrays]
    total = 0
    at = 0
    for array, height in zip(arrays, heights):
        if array is not None:
            edges = ((at, sum(heights) - at - height, 0), (0, LANES - array.shape[1], 0))
            total += lax.pad(array, jnp.zeros((), array.dtype), edges).astype(F32)
        at += height
    return total


def local_owners(green_blocks, slot_rows, slot_cols, slot_count, cell_class, class_contrast, background):
    r = lax.axis_index("row")
    c = lax.axis_index("col")
    rows = lax.axis_size("row")
    cols = lax.axis_size("col")
    green = green_blocks[0, 0]
    slots, _, entries, _ = green.shape
    sources, blocks = background.shape[1:3]
    both = ("row", "col")

    small = stacked([slot_rows[0], slot_cols[0], None, None, cell_class[:, 0, :], class_contrast.T])
    line = lax.broadcasted_iota(jnp.int32, small.shape, 0)
    small = jnp.where(line == 2, r.astype(F32), jnp.where(line == 3, c.astype(F32), small))

    local_rows = small[0:1, :].astype(jnp.int32)
    local_cols = small[1:2, :].astype(jnp.int32)
    living = lax.broadcasted_iota(jnp.int32, (1, LANES), 1) < slot_count
    off_diagonal = (local_rows // 2 * cols + 2 * r + local_rows % 2) != (local_cols * cols + c)
    place = (local_rows % 2 ^ c % 2) * blocks + local_rows // 2
    spare = jnp.full_like(place, 2 * blocks)
    table = jnp.concatenate(
        [
            local_cols,
            jnp.where(living, place, spare),
            place,
            jnp.where(living & off_diagonal, local_cols, spare // 2),
        ],
        axis=0,
    )

    block = (2 * sources, entries)
    back = background[:, :, :, 0, :].transpose(2, 0, 1, 3).reshape((blocks,) + block)
    start, contrast = whole_call(
        lambda *refs: start_kernel(class_contrast.shape[0], *refs),
        (
            jax.ShapeDtypeStruct((2 * sources, WIDTH), BF),
            jax.ShapeDtypeStruct((2, blocks, entries // 3), F32),
        ),
        (small, back),
        [],
        "start",
    )

    core_pairs = [(i, i ^ 1) for i in range(cols)]
    chips = cols // 2
    arrived = []
    for hop in range(1, chips):
        pairs = []
        for a in range(rows):
            far = (a + hop) % chips
            for k in range(chips):
                for p in range(2):
                    to = {a: 2 * far + p, far: 2 * a + p}.get(k, 2 * k + 1 - p)
                    pairs.append((a * cols + 2 * k + p, a * cols + to))
        arrived.append(lax.ppermute(start, both, pairs))
    marks, back_share = whole_call(
        share_kernel,
        (
            jax.ShapeDtypeStruct((blocks, 4, LANES), F32),
            jax.ShapeDtypeStruct((blocks,) + block, F32),
        ),
        (small, contrast, back, green),
        [],
        "share",
    )
    marks, *arrived = lax.optimization_barrier((marks, *arrived))
    row_mine = start
    for hop in range(1, chips):
        row_mine = jnp.where(c // 2 == (r + hop) % chips, arrived[hop - 1], row_mine)
    row_other = lax.ppermute(row_mine, "col", core_pairs)

    part = jax.ShapeDtypeStruct((blocks,) + block, F32)
    message = jax.ShapeDtypeStruct((rows * cols, 4, WIDTH), BF)
    for step in range(PRODUCTS):
        first = step == 0
        final = step + 1 == PRODUCTS
        if first:
            direct_in, mirror_in = start, (row_mine, row_other)
        else:
            direct_in, mirror_in = x_msg, (x_msg, lax.ppermute(x_msg, "col", core_pairs))
        own, other = whole_call(
            lambda *refs, first=first: direct_kernel(first, *refs),
            (part, jax.ShapeDtypeStruct((2 * sources, WIDTH), F32)),
            (table, green, direct_in),
            [
                pltpu.VMEM((blocks, 2 * sources, 2 * entries), BF),
                pltpu.VMEM((2 * blocks + 1,) + block, F32),
            ],
            f"direct_{step}",
        )
        got = lax.ppermute(other, "col", core_pairs)
        mirror = whole_call(
            lambda *refs, first=first: mirror_kernel(first, *refs),
            part,
            (table, green) + mirror_in + (() if final else (back_share,)),
            [
                pltpu.VMEM((2 * blocks, 2 * sources, 2 * entries), BF),
                pltpu.VMEM((blocks + 1,) + block, F32),
            ],
            f"mirror_{step}",
        )
        y_shape = message if final else jax.ShapeDtypeStruct((rows * cols, 4, WIDTH + LANES), jnp.int16)
        operands = (mirror, own, got) + ((marks,) if first else ())
        y_msg = whole_call(pack_kernel, y_shape, operands, [], f"pack_{step}")
        y_msg = lax.all_to_all(y_msg, both, 0, 0, tiled=True)
        run = lambda *refs, first=first: update_kernel(first, rows, cols, *refs)
        if first:
            x_msg, owner_contrast = whole_call(
                run,
                (message, jax.ShapeDtypeStruct((cols, 2, 3, 4, LANES), F32)),
                (y_msg,),
                [],
                f"update_{step}",
            )
        elif not final:
            x_msg = whole_call(run, message, (y_msg, owner_contrast), [], f"update_{step}")
        else:
            run = lambda *refs: last_kernel(rows, cols, *refs)
            x_shape = jax.ShapeDtypeStruct((rows * cols, 4, 2 * MAIN + LANES), jnp.int16)
            x_msg = whole_call(run, x_shape, (y_msg,), [], "last")
        x_msg = lax.all_to_all(x_msg, both, 0, 0, tiled=True)
    field = whole_call(finish_kernel, part, (x_msg, back), [], "finish")
    field = field.reshape(blocks, 2, sources, entries).transpose(1, 2, 0, 3)
    return field[:, :, :, None, :]


def solution(mesh):
    in_specs = (
        P("row", "col", None, None, None, None),
        P("row", "col", None),
        P("row", "col", None),
        P("row", "col"),
        P(None, "col", None),
        P(),
        P(None, None, None, "col", None),
    )
    out_specs = P(None, None, None, "col", None)
    rows, cols = mesh.shape["row"], mesh.shape["col"]

    def local(*args):
        sources, blocks = args[6].shape[1:3]
        entries = args[6].shape[4]
        owners = (
            rows == blocks == 4
            and cols == 2 * rows
            and sources == 4 * cols
            and max(args[5].shape[0], args[1].shape[2]) <= LANES
            and entries == 2 * LANES + LANES // 4 == 3 * args[4].shape[2]
        )
        return (local_owners if owners else local_general)(*args)

    return jax.shard_map(local, mesh=mesh, in_specs=in_specs, out_specs=out_specs, check_vma=False)
```

```python
import jax
import jax.numpy as jnp
from jax import lax
from jax.experimental import pallas as pl
from jax.experimental.pallas import tpu as pltpu
from jax.sharding import PartitionSpec as P

PRODUCTS = 3
LANES = 128
SMALLEST = 2.0**-100
VMEM_BYTES = 8 * 1024 * 1024
BF = jnp.bfloat16
F32 = jnp.float32


def from_root(array, axis, root):
    mine = lax.axis_index(axis) == root
    return lax.psum(jnp.where(mine, array, jnp.zeros_like(array)), axis)


def complex_scale(field_now, contrast_re, contrast_im):
    real_part = field_now[0]
    imag_part = field_now[1]
    scaled = jnp.stack(
        [
            contrast_re * real_part - contrast_im * imag_part,
            contrast_re * imag_part + contrast_im * real_part,
        ]
    )
    return scaled.astype(BF)


def combine(products):
    return jnp.stack([products[0, 0] - products[1, 1], products[0, 1] + products[1, 0]])


def local_general(green_blocks, slot_rows, slot_cols, slot_count, cell_class, class_contrast, background):
    row_index = lax.axis_index("row")
    col_index = lax.axis_index("col")
    stride = lax.axis_size("col")
    green_tiles = green_blocks[0, 0]
    slot_total = green_tiles.shape[0]
    entries = green_tiles.shape[-1]
    sources = background.shape[1]
    col_blocks = background.shape[2]
    row_blocks = 2 * col_blocks
    local_rows = slot_rows[0, 0]
    local_cols = slot_cols[0, 0]
    global_rows = local_rows // 2 * stride + 2 * row_index + local_rows % 2
    global_cols = local_cols * stride + col_index
    off_diagonal = (global_rows != global_cols).astype(F32)
    living = (jnp.arange(slot_total) < slot_count[0, 0]).astype(F32)
    row_pick = (local_rows[:, None] == jnp.arange(row_blocks)[None, :]).astype(F32) * living[:, None]
    col_pick = (local_cols[:, None] == jnp.arange(col_blocks)[None, :]).astype(F32) * (
        living * off_diagonal
    )[:, None]
    classes = class_contrast.shape[0]
    lookup = (cell_class[:, 0, :, None] == jnp.arange(classes)[None, None, :]).astype(F32)
    values = jnp.einsum("bte,ec->btc", lookup, class_contrast, precision=lax.Precision.HIGHEST)
    contrast_re = jnp.tile(values[:, :, 0], (1, 3))
    contrast_im = jnp.tile(values[:, :, 1], (1, 3))
    start_field = background[:, :, :, 0, :]
    field_now = start_field
    current = complex_scale(field_now, contrast_re, contrast_im)
    for step_index in range(PRODUCTS):
        final_step = step_index + 1 == PRODUCTS
        halves = [from_root(current, "col", 2 * row_index + parity) for parity in range(2)]
        row_current = jnp.stack(halves, axis=3).reshape(2, sources, row_blocks, entries)
        direct_in = jnp.take(current, local_cols, axis=2)
        mirror_in = jnp.take(row_current, local_rows, axis=2)
        direct_terms = combine(
            jnp.einsum("sqoi,pksi->qpkso", green_tiles, direct_in, preferred_element_type=F32)
        )
        mirror_terms = combine(
            jnp.einsum("sqoi,pkso->qpksi", green_tiles, mirror_in, preferred_element_type=F32)
        )
        direct_part = jnp.einsum(
            "pkse,sb->pkbe", direct_terms, row_pick, precision=lax.Precision.HIGHEST
        )
        mirror_part = jnp.einsum(
            "pkse,sb->pkbe", mirror_terms, col_pick, precision=lax.Precision.HIGHEST
        )
        row_total = lax.psum(direct_part, "col")
        owned_part = lax.dynamic_index_in_dim(
            row_total.reshape(2, sources, col_blocks, 2, entries),
            col_index % 2,
            axis=3,
            keepdims=False,
        )
        direct_here = from_root(owned_part, "row", col_index // 2)
        column_total = lax.psum(mirror_part, "row")
        field_now = start_field + column_total + direct_here
        if not final_step:
            current = complex_scale(field_now, contrast_re, contrast_im)
    return field_now[:, :, :, None, :]


MAIN = 2 * LANES
TAIL = LANES // 4
ENDS = 4 * MAIN
WIDTH = ENDS + LANES
POWER = 3 * TAIL


def turned(value):
    half = value.shape[0] // 2
    return jnp.concatenate([-value[half:], value[:half]], axis=0)


def shifted(value, lanes):
    return pltpu.roll(value, LANES - lanes, 1) if lanes else value


def put_block(xs_ref, at, value, mirror):
    entries = value.shape[1]
    both = [value.astype(BF), turned(value).astype(BF)]
    if mirror:
        xs_ref[at, :, :entries] = both[0]
        xs_ref[at, :, entries:] = both[1]
    else:
        xs_ref[at, :, :MAIN] = both[0][:, :MAIN]
        xs_ref[at, :, MAIN : 2 * MAIN] = both[1][:, :MAIN]
        xs_ref[at, :, 2 * MAIN :] = jnp.concatenate([part[:, MAIN:] for part in both], axis=1)


def gathered_rows(msg_ref, q, lanes):
    groups = msg_ref.shape[0] // 4
    return jnp.concatenate([msg_ref[q * groups + g, :, lanes].astype(F32) for g in range(groups)], axis=0)


def unpack_half(msg_ref, q, half, xs_ref, at):
    ends = gathered_rows(msg_ref, q, slice(ENDS, WIDTH))
    parts = []
    for k in (2 * half, 2 * half + 1):
        main = gathered_rows(msg_ref, q, slice(k * MAIN, (k + 1) * MAIN))
        parts.append(jnp.concatenate([main, shifted(ends, k * TAIL)[:, :TAIL]], axis=1))
    put_block(xs_ref, at, jnp.concatenate(parts, axis=0), half)


def put_side_by_side(out_ref, values):
    for q, value in enumerate(values):
        out_ref[:, q * MAIN : (q + 1) * MAIN] = value[:, :MAIN].astype(out_ref.dtype)
    out_ref[:, ENDS:] = jnp.concatenate([value[:, MAIN:] for value in values], axis=1).astype(out_ref.dtype)


def side_by_side(ref):
    ends = ref[:, ENDS:].astype(F32)
    mains = [ref[:, q * MAIN : (q + 1) * MAIN].astype(F32) for q in range(4)]
    return [jnp.concatenate([main, shifted(ends, q * TAIL)[:, :TAIL]], axis=1) for q, main in enumerate(mains)]


def copy_in(x_ref, xs_ref, offset, mirror):
    for q, value in enumerate(side_by_side(x_ref)):
        put_block(xs_ref, offset + q, value, mirror)


def across(left, right):
    return lax.dot_general(left, right, (((1,), (1,)), ((), ())), preferred_element_type=F32)


def slot_products(table_ref, g_ref, xs_ref, acc_ref, mirror, start_ref=None):
    acc_ref[...] = jnp.zeros_like(acc_ref)
    if start_ref is not None:
        acc_ref[: start_ref.shape[0]] = start_ref[...]
    slots, _, depth, entries = g_ref.shape
    table = table_ref[...]
    first = 2 if mirror else 0
    for s in range(slots):
        left = xs_ref[table[first, s]]
        if mirror:
            value = jnp.dot(left, g_ref[s].reshape(2 * depth, entries), preferred_element_type=F32)
        else:
            ends = jnp.concatenate([g_ref[s, 0, :, MAIN:], g_ref[s, 1, :, MAIN:]], axis=1)
            value = across(left[:, :MAIN], g_ref[s, 0, :, :MAIN])
            value += across(left[:, MAIN : 2 * MAIN], g_ref[s, 1, :, :MAIN])
            value += across(left[:, 2 * MAIN :], ends)
        acc_ref[table[first + 1, s]] += value


def start_kernel(classes, small_ref, back_ref, out_ref, contrast_ref):
    blocks = back_ref.shape[0]
    cells = contrast_ref.shape[2]
    kinds = small_ref[4 : 4 + blocks, :cells]
    tables = small_ref[4 + blocks : 6 + blocks, :]
    contrast = []
    for part in range(2):
        value = jnp.zeros(kinds.shape, F32)
        for k in range(classes):
            value = jnp.where(kinds == float(k), tables[part : part + 1, k : k + 1], value)
        contrast_ref[part] = value
        contrast.append(jnp.concatenate([value] * 3, axis=1))
    real, imag = contrast
    values = []
    for q in range(blocks):
        back = back_ref[q]
        values.append(real[q : q + 1] * back + imag[q : q + 1] * turned(back))
    put_side_by_side(out_ref, values)


def share_kernel(small_ref, contrast_ref, back_ref, _, marks_ref, share_ref):
    r = small_ref[2:3, 0:1]
    cells = contrast_ref.shape[2]
    for q in range(back_ref.shape[0]):
        share_ref[q] = jnp.where(r == 0.0, back_ref[q], 0.0)
        marks = []
        for part in range(2):
            value = contrast_ref[part, q : q + 1] * 2.0**15
            rest = (value - jnp.round(value)) * 2.0**16
            marks += [jnp.round(value), jnp.clip(jnp.round(rest), -32767.0, 32767.0)]
        marks = jnp.concatenate(marks, axis=0)
        marks_ref[q] = jnp.concatenate([marks, jnp.zeros((4, LANES - cells), F32)], axis=1)


def as_integers(value):
    return value.astype(jnp.int32).astype(jnp.int16)


def as_floats(value):
    return value.astype(jnp.int32).astype(F32)


def direct_kernel(first, table_ref, g_ref, x_ref, own_ref, other_ref, xs_ref, acc_ref):
    blocks = own_ref.shape[0]
    if first:
        copy_in(x_ref, xs_ref, 0, False)
    else:
        for q in range(blocks):
            unpack_half(x_ref, q, 0, xs_ref, q)
    slot_products(table_ref, g_ref, xs_ref, acc_ref, False)
    for q in range(blocks):
        own_ref[q] = acc_ref[q]
    put_side_by_side(other_ref, [acc_ref[blocks + q] for q in range(blocks)])


def mirror_kernel(first, table_ref, g_ref, x_ref, x_other_ref, *refs):
    *start, out_ref, xs_ref, acc_ref = refs
    blocks = out_ref.shape[0]
    if first:
        copy_in(x_ref, xs_ref, 0, True)
        copy_in(x_other_ref, xs_ref, blocks, True)
    else:
        for q in range(blocks):
            unpack_half(x_ref, q, 1, xs_ref, q)
            unpack_half(x_other_ref, q, 1, xs_ref, blocks + q)
    slot_products(table_ref, g_ref, xs_ref, acc_ref, True, *start)
    for q in range(blocks):
        out_ref[q] = acc_ref[q]


def pack_kernel(mirror_ref, own_ref, got_ref, *rest):
    msg_ref = rest[-1]
    coded = msg_ref.dtype != BF
    blocks, rows, _ = own_ref.shape
    half = rows // 2
    lane = lax.broadcasted_iota(jnp.int32, (half, LANES), 1)
    got = side_by_side(got_ref)
    for q in range(blocks):
        halves = [own_ref[q] + got[q], mirror_ref[q]]
        parts = [value[p * half : (p + 1) * half] for value in halves for p in range(2)]
        if coded:
            power, scale = row_power(parts)
            parts = [jnp.round(part * scale) for part in parts]
        parts = [part[:, :MAIN] for part in parts] + [jnp.concatenate([part[:, MAIN:] for part in parts], axis=1)]
        if coded:
            marks = jnp.concatenate([rest[0][q]] * (half // 4), axis=0) if len(rest) == 2 else 0.0
            parts.append(jnp.where(lane == POWER, power, marks))
            parts = [part.astype(jnp.int32) for part in parts]
        for g in range(half // 4):
            at = slice(4 * g, 4 * g + 4)
            d = q * (half // 4) + g
            for k, part in enumerate(parts):
                lanes = slice(k * MAIN, (k + 1) * MAIN) if k < 4 else slice(ENDS + (k - 4) * LANES, ENDS + (k - 3) * LANES)
                msg_ref[d, :, lanes] = part[at].astype(msg_ref.dtype)


def row_power(parts):
    most = jnp.abs(parts[0])
    for part in parts[1:]:
        most = jnp.maximum(most, jnp.abs(part))
    most = jnp.max(most, axis=1, keepdims=True)
    power = jnp.floor(jnp.log2(jnp.maximum(most, SMALLEST)) + 2.0**-12)
    return power, jnp.exp2(14.0 - power)


def partial_sums(msg_ref, rows, cols):
    direct = {}
    mirror = {}
    coded = msg_ref.dtype != BF

    def add(store, key, value):
        store[key] = store[key] + value if key in store else value

    for r in range(rows):
        for c in range(cols):
            d = r * cols + c
            j = 2 * r + c % 2
            if coded:
                scale = jnp.exp2(as_floats(msg_ref[d, :, WIDTH : WIDTH + LANES])[:, POWER : POWER + 1] - 14.0)
            for k in range(9):
                value = msg_ref[d, :, k * LANES : (k + 1) * LANES]
                value = as_floats(value) * scale if coded else value.astype(F32)
                if k < 4 or k == 8:
                    add(direct, (j, min(k, 4)), value)
                if k >= 4:
                    add(mirror, (c, k - 4), value)
    for j in range(cols):
        mirror[j, 4] = shifted(mirror[j, 4], 2 * TAIL)
    return {key: direct[key] + mirror[key] for key in direct}


def update_kernel(first, rows, cols, msg_ref, *refs):
    contrast_ref, out_ref = refs[::-1] if first else refs
    lane = lax.broadcasted_iota(jnp.int32, (4, LANES), 1)
    cells = (MAIN + TAIL) // 3
    sums = partial_sums(msg_ref, rows, cols)
    current = {}
    for j in range(cols):
        if first:
            marks = as_floats(msg_ref[j, :, WIDTH : WIDTH + LANES])
            contrast = []
            for row in (0, 2):
                value = marks[row : row + 1] * 2.0**-15 + marks[row + 1 : row + 2] * 2.0**-31
                value = jnp.broadcast_to(value, (4, LANES))
                near, far = shifted(value, TAIL), shifted(value, 2 * TAIL)
                contrast.append(
                    [
                        jnp.where(lane < cells, value, near),
                        jnp.where(lane < 2 * TAIL, near, far),
                        jnp.where(lane < TAIL, far, near),
                    ]
                )
            for part in range(2):
                for k in range(3):
                    contrast_ref[j, part, k] = contrast[part][k]
        else:
            contrast = [[contrast_ref[j, part, k] for k in range(3)] for part in range(2)]
        total = [sums[j, k] for k in range(5)]
        real, imag = contrast
        for k in range(2):
            current[j, k] = real[k] * total[k] - imag[k] * total[k + 2]
            current[j, k + 2] = real[k] * total[k + 2] + imag[k] * total[k]
        other = jnp.where(lane < TAIL, -shifted(total[4], TAIL), pltpu.roll(total[4], TAIL, 1))
        current[j, 4] = real[2] * total[4] + imag[2] * other
    for r in range(rows):
        for c in range(cols):
            d = r * cols + c
            j = 2 * r + c % 2
            for k in range(4):
                out_ref[d, :, k * LANES : (k + 1) * LANES] = current[c, k].astype(BF)
                out_ref[d, :, (k + 4) * LANES : (k + 5) * LANES] = current[j, k].astype(BF)
            ends = jnp.where(lane < 2 * TAIL, current[c, 4], shifted(current[j, 4], 2 * TAIL))
            out_ref[d, :, ENDS:WIDTH] = ends.astype(BF)


def last_kernel(rows, cols, msg_ref, out_ref):
    lane = lax.broadcasted_iota(jnp.int32, (4, LANES), 1)
    sums = partial_sums(msg_ref, rows, cols)
    for j in range(cols):
        ends = jnp.zeros((4, LANES), F32)
        for p in range(2):
            mine = (lane >= p * TAIL) & (lane < (p + 1) * TAIL)
            tail = jnp.where(mine, sums[j, 4], 0.0)
            power, scale = row_power([sums[j, 2 * p], sums[j, 2 * p + 1], tail])
            for k in range(2 * p, 2 * p + 2):
                coded = as_integers(jnp.round(sums[j, k] * scale))
                for r in range(rows):
                    out_ref[r * cols + j, :, k * LANES : (k + 1) * LANES] = coded
            ends = jnp.where(mine, jnp.round(tail * scale), jnp.where(lane == 2 * TAIL + p, power, ends))
        coded = as_integers(ends)
        for r in range(rows):
            out_ref[r * cols + j, :, 2 * MAIN : 2 * MAIN + LANES] = coded


def finish_kernel(msg_ref, back_ref, out_ref):
    blocks, rows, _ = out_ref.shape
    half = rows // 2
    groups = half // 4

    def rows_of(q, lanes):
        return jnp.concatenate([as_floats(msg_ref[q * groups + g, :, lanes]) for g in range(groups)], axis=0)

    for q in range(blocks):
        ends = rows_of(q, slice(2 * MAIN, 2 * MAIN + LANES))
        for p in range(2):
            at = slice(p * half, (p + 1) * half)
            scale = jnp.exp2(ends[:, 2 * TAIL + p : 2 * TAIL + p + 1] - 14.0)
            main = rows_of(q, slice(p * MAIN, (p + 1) * MAIN))
            out_ref[q, at, :MAIN] = back_ref[q, at, :MAIN] + main * scale
            out_ref[q, at, MAIN:] = back_ref[q, at, MAIN:] + shifted(ends, p * TAIL)[:, :TAIL] * scale


def whole_call(kernel, out_shape, operands, scratch, name):
    vmem = pl.BlockSpec(memory_space=pltpu.VMEM)
    return pl.pallas_call(
        kernel,
        out_shape=out_shape,
        in_specs=[vmem] * len(operands),
        out_specs=jax.tree.map(lambda _: vmem, out_shape),
        scratch_shapes=scratch,
        compiler_params=pltpu.CompilerParams(vmem_limit_bytes=VMEM_BYTES),
        name=name,
    )(*operands)


def stacked(arrays):
    heights = [1 if array is None else array.shape[0] for array in arrays]
    total = 0
    at = 0
    for array, height in zip(arrays, heights):
        if array is not None:
            edges = ((at, sum(heights) - at - height, 0), (0, LANES - array.shape[1], 0))
            total += lax.pad(array, jnp.zeros((), array.dtype), edges).astype(F32)
        at += height
    return total


def local_owners(green_blocks, slot_rows, slot_cols, slot_count, cell_class, class_contrast, background):
    r = lax.axis_index("row")
    c = lax.axis_index("col")
    rows = lax.axis_size("row")
    cols = lax.axis_size("col")
    green = green_blocks[0, 0]
    slots, _, entries, _ = green.shape
    sources, blocks = background.shape[1:3]
    both = ("row", "col")

    small = stacked([slot_rows[0], slot_cols[0], None, None, cell_class[:, 0, :], class_contrast.T])
    line = lax.broadcasted_iota(jnp.int32, small.shape, 0)
    small = jnp.where(line == 2, r.astype(F32), jnp.where(line == 3, c.astype(F32), small))

    local_rows = small[0:1, :].astype(jnp.int32)
    local_cols = small[1:2, :].astype(jnp.int32)
    living = lax.broadcasted_iota(jnp.int32, (1, LANES), 1) < slot_count
    off_diagonal = (local_rows // 2 * cols + 2 * r + local_rows % 2) != (local_cols * cols + c)
    place = (local_rows % 2 ^ c % 2) * blocks + local_rows // 2
    spare = jnp.full_like(place, 2 * blocks)
    table = jnp.concatenate(
        [
            local_cols,
            jnp.where(living, place, spare),
            place,
            jnp.where(living & off_diagonal, local_cols, spare // 2),
        ],
        axis=0,
    )

    block = (2 * sources, entries)
    back = background[:, :, :, 0, :].transpose(2, 0, 1, 3).reshape((blocks,) + block)
    start, contrast = whole_call(
        lambda *refs: start_kernel(class_contrast.shape[0], *refs),
        (
            jax.ShapeDtypeStruct((2 * sources, WIDTH), BF),
            jax.ShapeDtypeStruct((2, blocks, entries // 3), F32),
        ),
        (small, back),
        [],
        "start",
    )

    core_pairs = [(i, i ^ 1) for i in range(cols)]
    chips = cols // 2
    arrived = []
    for hop in range(1, chips):
        pairs = []
        for a in range(rows):
            far = (a + hop) % chips
            for k in range(chips):
                for p in range(2):
                    to = {a: 2 * far + p, far: 2 * a + p}.get(k, 2 * k + 1 - p)
                    pairs.append((a * cols + 2 * k + p, a * cols + to))
        arrived.append(lax.ppermute(start, both, pairs))
    marks, back_share = whole_call(
        share_kernel,
        (
            jax.ShapeDtypeStruct((blocks, 4, LANES), F32),
            jax.ShapeDtypeStruct((blocks,) + block, F32),
        ),
        (small, contrast, back, green),
        [],
        "share",
    )

    part = jax.ShapeDtypeStruct((blocks,) + block, F32)
    message = jax.ShapeDtypeStruct((rows * cols, 4, WIDTH), BF)
    for step in range(PRODUCTS):
        first = step == 0
        final = step + 1 == PRODUCTS
        if first:
            direct_in = start
        else:
            direct_in, mirror_in = x_msg, (x_msg, lax.ppermute(x_msg, "col", core_pairs))
        own, other = whole_call(
            lambda *refs, first=first: direct_kernel(first, *refs),
            (part, jax.ShapeDtypeStruct((2 * sources, WIDTH), F32)),
            (table, green, direct_in),
            [
                pltpu.VMEM((blocks, 2 * sources, 2 * entries), BF),
                pltpu.VMEM((2 * blocks + 1,) + block, F32),
            ],
            f"direct_{step}",
        )
        if first:
            marks, other, *arrived = lax.optimization_barrier((marks, other, *arrived))
            row_mine = start
            for hop in range(1, chips):
                row_mine = jnp.where(c // 2 == (r + hop) % chips, arrived[hop - 1], row_mine)
            row_other = lax.ppermute(row_mine, "col", core_pairs)
            mirror_in = (row_mine, row_other)
        if first:
            other, *mirror_in = lax.optimization_barrier((other, *mirror_in))
            mirror_in = tuple(mirror_in)
        got = lax.ppermute(other, "col", core_pairs)
        mirror = whole_call(
            lambda *refs, first=first: mirror_kernel(first, *refs),
            part,
            (table, green) + mirror_in + (() if final else (back_share,)),
            [
                pltpu.VMEM((2 * blocks, 2 * sources, 2 * entries), BF),
                pltpu.VMEM((blocks + 1,) + block, F32),
            ],
            f"mirror_{step}",
        )
        y_shape = message if final else jax.ShapeDtypeStruct((rows * cols, 4, WIDTH + LANES), jnp.int16)
        operands = (mirror, own, got) + ((marks,) if first else ())
        y_msg = whole_call(pack_kernel, y_shape, operands, [], f"pack_{step}")
        y_msg = lax.all_to_all(y_msg, both, 0, 0, tiled=True)
        run = lambda *refs, first=first: update_kernel(first, rows, cols, *refs)
        if first:
            x_msg, owner_contrast = whole_call(
                run,
                (message, jax.ShapeDtypeStruct((cols, 2, 3, 4, LANES), F32)),
                (y_msg,),
                [],
                f"update_{step}",
            )
        elif not final:
            x_msg = whole_call(run, message, (y_msg, owner_contrast), [], f"update_{step}")
        else:
            run = lambda *refs: last_kernel(rows, cols, *refs)
            x_shape = jax.ShapeDtypeStruct((rows * cols, 4, 2 * MAIN + LANES), jnp.int16)
            x_msg = whole_call(run, x_shape, (y_msg,), [], "last")
        x_msg = lax.all_to_all(x_msg, both, 0, 0, tiled=True)
    field = whole_call(finish_kernel, part, (x_msg, back), [], "finish")
    field = field.reshape(blocks, 2, sources, entries).transpose(1, 2, 0, 3)
    return field[:, :, :, None, :]


def solution(mesh):
    in_specs = (
        P("row", "col", None, None, None, None),
        P("row", "col", None),
        P("row", "col", None),
        P("row", "col"),
        P(None, "col", None),
        P(),
        P(None, None, None, "col", None),
    )
    out_specs = P(None, None, None, "col", None)
    rows, cols = mesh.shape["row"], mesh.shape["col"]

    def local(*args):
        sources, blocks = args[6].shape[1:3]
        entries = args[6].shape[4]
        owners = (
            rows == blocks == 4
            and cols == 2 * rows
            and sources == 4 * cols
            and max(args[5].shape[0], args[1].shape[2]) <= LANES
            and entries == 2 * LANES + LANES // 4 == 3 * args[4].shape[2]
        )
        return (local_owners if owners else local_general)(*args)

    return jax.shard_map(local, mesh=mesh, in_specs=in_specs, out_specs=out_specs, check_vma=False)
```

```python
import jax
import jax.numpy as jnp
from jax import lax
from jax.experimental import pallas as pl
from jax.experimental.pallas import tpu as pltpu
from jax.sharding import PartitionSpec as P

PRODUCTS = 3
LANES = 128
SMALLEST = 2.0**-100
VMEM_BYTES = 8 * 1024 * 1024
BF = jnp.bfloat16
F32 = jnp.float32


def from_root(array, axis, root):
    mine = lax.axis_index(axis) == root
    return lax.psum(jnp.where(mine, array, jnp.zeros_like(array)), axis)


def complex_scale(field_now, contrast_re, contrast_im):
    real_part = field_now[0]
    imag_part = field_now[1]
    scaled = jnp.stack(
        [
            contrast_re * real_part - contrast_im * imag_part,
            contrast_re * imag_part + contrast_im * real_part,
        ]
    )
    return scaled.astype(BF)


def combine(products):
    return jnp.stack([products[0, 0] - products[1, 1], products[0, 1] + products[1, 0]])


def local_general(green_blocks, slot_rows, slot_cols, slot_count, cell_class, class_contrast, background):
    row_index = lax.axis_index("row")
    col_index = lax.axis_index("col")
    stride = lax.axis_size("col")
    green_tiles = green_blocks[0, 0]
    slot_total = green_tiles.shape[0]
    entries = green_tiles.shape[-1]
    sources = background.shape[1]
    col_blocks = background.shape[2]
    row_blocks = 2 * col_blocks
    local_rows = slot_rows[0, 0]
    local_cols = slot_cols[0, 0]
    global_rows = local_rows // 2 * stride + 2 * row_index + local_rows % 2
    global_cols = local_cols * stride + col_index
    off_diagonal = (global_rows != global_cols).astype(F32)
    living = (jnp.arange(slot_total) < slot_count[0, 0]).astype(F32)
    row_pick = (local_rows[:, None] == jnp.arange(row_blocks)[None, :]).astype(F32) * living[:, None]
    col_pick = (local_cols[:, None] == jnp.arange(col_blocks)[None, :]).astype(F32) * (
        living * off_diagonal
    )[:, None]
    classes = class_contrast.shape[0]
    lookup = (cell_class[:, 0, :, None] == jnp.arange(classes)[None, None, :]).astype(F32)
    values = jnp.einsum("bte,ec->btc", lookup, class_contrast, precision=lax.Precision.HIGHEST)
    contrast_re = jnp.tile(values[:, :, 0], (1, 3))
    contrast_im = jnp.tile(values[:, :, 1], (1, 3))
    start_field = background[:, :, :, 0, :]
    field_now = start_field
    current = complex_scale(field_now, contrast_re, contrast_im)
    for step_index in range(PRODUCTS):
        final_step = step_index + 1 == PRODUCTS
        halves = [from_root(current, "col", 2 * row_index + parity) for parity in range(2)]
        row_current = jnp.stack(halves, axis=3).reshape(2, sources, row_blocks, entries)
        direct_in = jnp.take(current, local_cols, axis=2)
        mirror_in = jnp.take(row_current, local_rows, axis=2)
        direct_terms = combine(
            jnp.einsum("sqoi,pksi->qpkso", green_tiles, direct_in, preferred_element_type=F32)
        )
        mirror_terms = combine(
            jnp.einsum("sqoi,pkso->qpksi", green_tiles, mirror_in, preferred_element_type=F32)
        )
        direct_part = jnp.einsum(
            "pkse,sb->pkbe", direct_terms, row_pick, precision=lax.Precision.HIGHEST
        )
        mirror_part = jnp.einsum(
            "pkse,sb->pkbe", mirror_terms, col_pick, precision=lax.Precision.HIGHEST
        )
        row_total = lax.psum(direct_part, "col")
        owned_part = lax.dynamic_index_in_dim(
            row_total.reshape(2, sources, col_blocks, 2, entries),
            col_index % 2,
            axis=3,
            keepdims=False,
        )
        direct_here = from_root(owned_part, "row", col_index // 2)
        column_total = lax.psum(mirror_part, "row")
        field_now = start_field + column_total + direct_here
        if not final_step:
            current = complex_scale(field_now, contrast_re, contrast_im)
    return field_now[:, :, :, None, :]


MAIN = 2 * LANES
TAIL = LANES // 4
ENDS = 4 * MAIN
WIDTH = ENDS + LANES
POWER = 3 * TAIL


def turned(value):
    half = value.shape[0] // 2
    return jnp.concatenate([-value[half:], value[:half]], axis=0)


def shifted(value, lanes):
    return pltpu.roll(value, LANES - lanes, 1) if lanes else value


def put_block(xs_ref, at, value, mirror):
    entries = value.shape[1]
    both = [value.astype(BF), turned(value).astype(BF)]
    if mirror:
        xs_ref[at, :, :entries] = both[0]
        xs_ref[at, :, entries:] = both[1]
    else:
        xs_ref[at, :, :MAIN] = both[0][:, :MAIN]
        xs_ref[at, :, MAIN : 2 * MAIN] = both[1][:, :MAIN]
        xs_ref[at, :, 2 * MAIN :] = jnp.concatenate([part[:, MAIN:] for part in both], axis=1)


def gathered_rows(msg_ref, q, lanes):
    groups = msg_ref.shape[0] // 4
    return jnp.concatenate([msg_ref[q * groups + g, :, lanes].astype(F32) for g in range(groups)], axis=0)


def unpack_half(msg_ref, q, half, xs_ref, at):
    ends = gathered_rows(msg_ref, q, slice(ENDS, WIDTH))
    parts = []
    for k in (2 * half, 2 * half + 1):
        main = gathered_rows(msg_ref, q, slice(k * MAIN, (k + 1) * MAIN))
        parts.append(jnp.concatenate([main, shifted(ends, k * TAIL)[:, :TAIL]], axis=1))
    put_block(xs_ref, at, jnp.concatenate(parts, axis=0), half)


def put_side_by_side(out_ref, values):
    for q, value in enumerate(values):
        out_ref[:, q * MAIN : (q + 1) * MAIN] = value[:, :MAIN].astype(out_ref.dtype)
    out_ref[:, ENDS:] = jnp.concatenate([value[:, MAIN:] for value in values], axis=1).astype(out_ref.dtype)


def side_by_side(ref):
    ends = ref[:, ENDS:].astype(F32)
    mains = [ref[:, q * MAIN : (q + 1) * MAIN].astype(F32) for q in range(4)]
    return [jnp.concatenate([main, shifted(ends, q * TAIL)[:, :TAIL]], axis=1) for q, main in enumerate(mains)]


def copy_in(x_ref, xs_ref, offset, mirror):
    for q, value in enumerate(side_by_side(x_ref)):
        put_block(xs_ref, offset + q, value, mirror)


def across(left, right):
    return lax.dot_general(left, right, (((1,), (1,)), ((), ())), preferred_element_type=F32)


def slot_products(table_ref, g_ref, xs_ref, acc_ref, mirror, start_ref=None):
    acc_ref[...] = jnp.zeros_like(acc_ref)
    if start_ref is not None:
        acc_ref[: start_ref.shape[0]] = start_ref[...]
    slots, _, depth, entries = g_ref.shape
    table = table_ref[...]
    first = 2 if mirror else 0
    for s in range(slots):
        left = xs_ref[table[first, s]]
        if mirror:
            value = jnp.dot(left, g_ref[s].reshape(2 * depth, entries), preferred_element_type=F32)
        else:
            ends = jnp.concatenate([g_ref[s, 0, :, MAIN:], g_ref[s, 1, :, MAIN:]], axis=1)
            value = across(left[:, :MAIN], g_ref[s, 0, :, :MAIN])
            value += across(left[:, MAIN : 2 * MAIN], g_ref[s, 1, :, :MAIN])
            value += across(left[:, 2 * MAIN :], ends)
        acc_ref[table[first + 1, s]] += value


def start_kernel(classes, small_ref, back_ref, out_ref, contrast_ref):
    blocks = back_ref.shape[0]
    cells = contrast_ref.shape[2]
    kinds = small_ref[4 : 4 + blocks, :cells]
    tables = small_ref[4 + blocks : 6 + blocks, :]
    contrast = []
    for part in range(2):
        value = jnp.zeros(kinds.shape, F32)
        for k in range(classes):
            value = jnp.where(kinds == float(k), tables[part : part + 1, k : k + 1], value)
        contrast_ref[part] = value
        contrast.append(jnp.concatenate([value] * 3, axis=1))
    real, imag = contrast
    values = []
    for q in range(blocks):
        back = back_ref[q]
        values.append(real[q : q + 1] * back + imag[q : q + 1] * turned(back))
    put_side_by_side(out_ref, values)


def share_kernel(small_ref, contrast_ref, back_ref, marks_ref, share_ref):
    r = small_ref[2:3, 0:1]
    cells = contrast_ref.shape[2]
    for q in range(back_ref.shape[0]):
        share_ref[q] = jnp.where(r == 0.0, back_ref[q], 0.0)
        marks = []
        for part in range(2):
            value = contrast_ref[part, q : q + 1] * 2.0**15
            rest = (value - jnp.round(value)) * 2.0**16
            marks += [jnp.round(value), jnp.clip(jnp.round(rest), -32767.0, 32767.0)]
        marks = jnp.concatenate(marks, axis=0)
        marks_ref[q] = jnp.concatenate([marks, jnp.zeros((4, LANES - cells), F32)], axis=1)


def as_integers(value):
    return value.astype(jnp.int32).astype(jnp.int16)


def as_floats(value):
    return value.astype(jnp.int32).astype(F32)


def direct_kernel(first, table_ref, g_ref, x_ref, own_ref, other_ref, xs_ref, acc_ref):
    blocks = own_ref.shape[0]
    if first:
        copy_in(x_ref, xs_ref, 0, False)
    else:
        for q in range(blocks):
            unpack_half(x_ref, q, 0, xs_ref, q)
    slot_products(table_ref, g_ref, xs_ref, acc_ref, False)
    for q in range(blocks):
        own_ref[q] = acc_ref[q]
    put_side_by_side(other_ref, [acc_ref[blocks + q] for q in range(blocks)])


def mirror_kernel(first, table_ref, g_ref, x_ref, x_other_ref, *refs):
    *start, out_ref, xs_ref, acc_ref = refs
    blocks = out_ref.shape[0]
    if first:
        copy_in(x_ref, xs_ref, 0, True)
        copy_in(x_other_ref, xs_ref, blocks, True)
    else:
        for q in range(blocks):
            unpack_half(x_ref, q, 1, xs_ref, q)
            unpack_half(x_other_ref, q, 1, xs_ref, blocks + q)
    slot_products(table_ref, g_ref, xs_ref, acc_ref, True, *start)
    for q in range(blocks):
        out_ref[q] = acc_ref[q]


def pack_kernel(mirror_ref, own_ref, got_ref, *rest):
    msg_ref = rest[-1]
    coded = msg_ref.dtype != BF
    blocks, rows, _ = own_ref.shape
    half = rows // 2
    lane = lax.broadcasted_iota(jnp.int32, (half, LANES), 1)
    got = side_by_side(got_ref)
    for q in range(blocks):
        halves = [own_ref[q] + got[q], mirror_ref[q]]
        parts = [value[p * half : (p + 1) * half] for value in halves for p in range(2)]
        if coded:
            power, scale = row_power(parts)
            parts = [jnp.round(part * scale) for part in parts]
        parts = [part[:, :MAIN] for part in parts] + [jnp.concatenate([part[:, MAIN:] for part in parts], axis=1)]
        if coded:
            marks = jnp.concatenate([rest[0][q]] * (half // 4), axis=0) if len(rest) == 2 else 0.0
            parts.append(jnp.where(lane == POWER, power, marks))
            parts = [part.astype(jnp.int32) for part in parts]
        for g in range(half // 4):
            at = slice(4 * g, 4 * g + 4)
            d = q * (half // 4) + g
            for k, part in enumerate(parts):
                lanes = slice(k * MAIN, (k + 1) * MAIN) if k < 4 else slice(ENDS + (k - 4) * LANES, ENDS + (k - 3) * LANES)
                msg_ref[d, :, lanes] = part[at].astype(msg_ref.dtype)


def row_power(parts):
    most = jnp.abs(parts[0])
    for part in parts[1:]:
        most = jnp.maximum(most, jnp.abs(part))
    most = jnp.max(most, axis=1, keepdims=True)
    power = jnp.floor(jnp.log2(jnp.maximum(most, SMALLEST)) + 2.0**-12)
    return power, jnp.exp2(14.0 - power)


def partial_sums(msg_ref, rows, cols):
    direct = {}
    mirror = {}
    coded = msg_ref.dtype != BF

    def add(store, key, value):
        store[key] = store[key] + value if key in store else value

    for r in range(rows):
        for c in range(cols):
            d = r * cols + c
            j = 2 * r + c % 2
            if coded:
                scale = jnp.exp2(as_floats(msg_ref[d, :, WIDTH : WIDTH + LANES])[:, POWER : POWER + 1] - 14.0)
            for k in range(9):
                value = msg_ref[d, :, k * LANES : (k + 1) * LANES]
                value = as_floats(value) * scale if coded else value.astype(F32)
                if k < 4 or k == 8:
                    add(direct, (j, min(k, 4)), value)
                if k >= 4:
                    add(mirror, (c, k - 4), value)
    for j in range(cols):
        mirror[j, 4] = shifted(mirror[j, 4], 2 * TAIL)
    return {key: direct[key] + mirror[key] for key in direct}


def update_kernel(first, rows, cols, msg_ref, *refs):
    contrast_ref, out_ref = refs[::-1] if first else refs
    lane = lax.broadcasted_iota(jnp.int32, (4, LANES), 1)
    cells = (MAIN + TAIL) // 3
    sums = partial_sums(msg_ref, rows, cols)
    current = {}
    for j in range(cols):
        if first:
            marks = as_floats(msg_ref[j, :, WIDTH : WIDTH + LANES])
            contrast = []
            for row in (0, 2):
                value = marks[row : row + 1] * 2.0**-15 + marks[row + 1 : row + 2] * 2.0**-31
                value = jnp.broadcast_to(value, (4, LANES))
                near, far = shifted(value, TAIL), shifted(value, 2 * TAIL)
                contrast.append(
                    [
                        jnp.where(lane < cells, value, near),
                        jnp.where(lane < 2 * TAIL, near, far),
                        jnp.where(lane < TAIL, far, near),
                    ]
                )
            for part in range(2):
                for k in range(3):
                    contrast_ref[j, part, k] = contrast[part][k]
        else:
            contrast = [[contrast_ref[j, part, k] for k in range(3)] for part in range(2)]
        total = [sums[j, k] for k in range(5)]
        real, imag = contrast
        for k in range(2):
            current[j, k] = real[k] * total[k] - imag[k] * total[k + 2]
            current[j, k + 2] = real[k] * total[k + 2] + imag[k] * total[k]
        other = jnp.where(lane < TAIL, -shifted(total[4], TAIL), pltpu.roll(total[4], TAIL, 1))
        current[j, 4] = real[2] * total[4] + imag[2] * other
    for r in range(rows):
        for c in range(cols):
            d = r * cols + c
            j = 2 * r + c % 2
            for k in range(4):
                out_ref[d, :, k * LANES : (k + 1) * LANES] = current[c, k].astype(BF)
                out_ref[d, :, (k + 4) * LANES : (k + 5) * LANES] = current[j, k].astype(BF)
            ends = jnp.where(lane < 2 * TAIL, current[c, 4], shifted(current[j, 4], 2 * TAIL))
            out_ref[d, :, ENDS:WIDTH] = ends.astype(BF)


def last_kernel(rows, cols, msg_ref, out_ref):
    lane = lax.broadcasted_iota(jnp.int32, (4, LANES), 1)
    sums = partial_sums(msg_ref, rows, cols)
    for j in range(cols):
        ends = jnp.zeros((4, LANES), F32)
        for p in range(2):
            mine = (lane >= p * TAIL) & (lane < (p + 1) * TAIL)
            tail = jnp.where(mine, sums[j, 4], 0.0)
            power, scale = row_power([sums[j, 2 * p], sums[j, 2 * p + 1], tail])
            for k in range(2 * p, 2 * p + 2):
                coded = as_integers(jnp.round(sums[j, k] * scale))
                for r in range(rows):
                    out_ref[r * cols + j, :, k * LANES : (k + 1) * LANES] = coded
            ends = jnp.where(mine, jnp.round(tail * scale), jnp.where(lane == 2 * TAIL + p, power, ends))
        coded = as_integers(ends)
        for r in range(rows):
            out_ref[r * cols + j, :, 2 * MAIN : 2 * MAIN + LANES] = coded


def finish_kernel(msg_ref, back_ref, out_ref):
    blocks, rows, _ = out_ref.shape
    half = rows // 2
    groups = half // 4

    def rows_of(q, lanes):
        return jnp.concatenate([as_floats(msg_ref[q * groups + g, :, lanes]) for g in range(groups)], axis=0)

    for q in range(blocks):
        ends = rows_of(q, slice(2 * MAIN, 2 * MAIN + LANES))
        for p in range(2):
            at = slice(p * half, (p + 1) * half)
            scale = jnp.exp2(ends[:, 2 * TAIL + p : 2 * TAIL + p + 1] - 14.0)
            main = rows_of(q, slice(p * MAIN, (p + 1) * MAIN))
            out_ref[q, at, :MAIN] = back_ref[q, at, :MAIN] + main * scale
            out_ref[q, at, MAIN:] = back_ref[q, at, MAIN:] + shifted(ends, p * TAIL)[:, :TAIL] * scale


def whole_call(kernel, out_shape, operands, scratch, name):
    vmem = pl.BlockSpec(memory_space=pltpu.VMEM)
    return pl.pallas_call(
        kernel,
        out_shape=out_shape,
        in_specs=[vmem] * len(operands),
        out_specs=jax.tree.map(lambda _: vmem, out_shape),
        scratch_shapes=scratch,
        compiler_params=pltpu.CompilerParams(vmem_limit_bytes=VMEM_BYTES),
        name=name,
    )(*operands)


def stacked(arrays):
    heights = [1 if array is None else array.shape[0] for array in arrays]
    total = 0
    at = 0
    for array, height in zip(arrays, heights):
        if array is not None:
            edges = ((at, sum(heights) - at - height, 0), (0, LANES - array.shape[1], 0))
            total += lax.pad(array, jnp.zeros((), array.dtype), edges).astype(F32)
        at += height
    return total


def local_owners(green_blocks, slot_rows, slot_cols, slot_count, cell_class, class_contrast, background):
    r = lax.axis_index("row")
    c = lax.axis_index("col")
    rows = lax.axis_size("row")
    cols = lax.axis_size("col")
    green = green_blocks[0, 0]
    slots, _, entries, _ = green.shape
    sources, blocks = background.shape[1:3]
    both = ("row", "col")

    small = stacked([slot_rows[0], slot_cols[0], None, None, cell_class[:, 0, :], class_contrast.T])
    line = lax.broadcasted_iota(jnp.int32, small.shape, 0)
    small = jnp.where(line == 2, r.astype(F32), jnp.where(line == 3, c.astype(F32), small))

    local_rows = small[0:1, :].astype(jnp.int32)
    local_cols = small[1:2, :].astype(jnp.int32)
    living = lax.broadcasted_iota(jnp.int32, (1, LANES), 1) < slot_count
    off_diagonal = (local_rows // 2 * cols + 2 * r + local_rows % 2) != (local_cols * cols + c)
    place = (local_rows % 2 ^ c % 2) * blocks + local_rows // 2
    spare = jnp.full_like(place, 2 * blocks)
    table = jnp.concatenate(
        [
            local_cols,
            jnp.where(living, place, spare),
            place,
            jnp.where(living & off_diagonal, local_cols, spare // 2),
        ],
        axis=0,
    )

    block = (2 * sources, entries)
    back = background[:, :, :, 0, :].transpose(2, 0, 1, 3).reshape((blocks,) + block)
    start, contrast = whole_call(
        lambda *refs: start_kernel(class_contrast.shape[0], *refs),
        (
            jax.ShapeDtypeStruct((2 * sources, WIDTH), BF),
            jax.ShapeDtypeStruct((2, blocks, entries // 3), F32),
        ),
        (small, back),
        [],
        "start",
    )

    core_pairs = [(i, i ^ 1) for i in range(cols)]
    chips = cols // 2
    arrived = []
    for hop in range(1, chips):
        pairs = []
        for a in range(rows):
            far = (a + hop) % chips
            for k in range(chips):
                for p in range(2):
                    to = {a: 2 * far + p, far: 2 * a + p}.get(k, 2 * k + 1 - p)
                    pairs.append((a * cols + 2 * k + p, a * cols + to))
        arrived.append(lax.ppermute(start, both, pairs))
    marks, back_share = whole_call(
        share_kernel,
        (
            jax.ShapeDtypeStruct((blocks, 4, LANES), F32),
            jax.ShapeDtypeStruct((blocks,) + block, F32),
        ),
        (small, contrast, back),
        [],
        "share",
    )

    part = jax.ShapeDtypeStruct((blocks,) + block, F32)
    message = jax.ShapeDtypeStruct((rows * cols, 4, WIDTH), BF)
    for step in range(PRODUCTS):
        first = step == 0
        final = step + 1 == PRODUCTS
        if first:
            direct_in = start
        else:
            direct_in, mirror_in = x_msg, (x_msg, lax.ppermute(x_msg, "col", core_pairs))
        own, other = whole_call(
            lambda *refs, first=first: direct_kernel(first, *refs),
            (part, jax.ShapeDtypeStruct((2 * sources, WIDTH), F32)),
            (table, green, direct_in),
            [
                pltpu.VMEM((blocks, 2 * sources, 2 * entries), BF),
                pltpu.VMEM((2 * blocks + 1,) + block, F32),
            ],
            f"direct_{step}",
        )
        if first:
            marks, other, *arrived = lax.optimization_barrier((marks, other, *arrived))
            row_mine = start
            for hop in range(1, chips):
                row_mine = jnp.where(c // 2 == (r + hop) % chips, arrived[hop - 1], row_mine)
            row_other = lax.ppermute(row_mine, "col", core_pairs)
            mirror_in = (row_mine, row_other)
        if first:
            other, *mirror_in = lax.optimization_barrier((other, *mirror_in))
            mirror_in = tuple(mirror_in)
        got = lax.ppermute(other, "col", core_pairs)
        mirror = whole_call(
            lambda *refs, first=first: mirror_kernel(first, *refs),
            part,
            (table, green) + mirror_in + (() if final else (back_share,)),
            [
                pltpu.VMEM((2 * blocks, 2 * sources, 2 * entries), BF),
                pltpu.VMEM((blocks + 1,) + block, F32),
            ],
            f"mirror_{step}",
        )
        y_shape = message if final else jax.ShapeDtypeStruct((rows * cols, 4, WIDTH + LANES), jnp.int16)
        operands = (mirror, own, got) + ((marks,) if first else ())
        y_msg = whole_call(pack_kernel, y_shape, operands, [], f"pack_{step}")
        y_msg = lax.all_to_all(y_msg, both, 0, 0, tiled=True)
        run = lambda *refs, first=first: update_kernel(first, rows, cols, *refs)
        if first:
            x_msg, owner_contrast = whole_call(
                run,
                (message, jax.ShapeDtypeStruct((cols, 2, 3, 4, LANES), F32)),
                (y_msg,),
                [],
                f"update_{step}",
            )
        elif not final:
            x_msg = whole_call(run, message, (y_msg, owner_contrast), [], f"update_{step}")
        else:
            run = lambda *refs: last_kernel(rows, cols, *refs)
            x_shape = jax.ShapeDtypeStruct((rows * cols, 4, 2 * MAIN + LANES), jnp.int16)
            x_msg = whole_call(run, x_shape, (y_msg,), [], "last")
        x_msg = lax.all_to_all(x_msg, both, 0, 0, tiled=True)
    field = whole_call(finish_kernel, part, (x_msg, back), [], "finish")
    field = field.reshape(blocks, 2, sources, entries).transpose(1, 2, 0, 3)
    return field[:, :, :, None, :]


def solution(mesh):
    in_specs = (
        P("row", "col", None, None, None, None),
        P("row", "col", None),
        P("row", "col", None),
        P("row", "col"),
        P(None, "col", None),
        P(),
        P(None, None, None, "col", None),
    )
    out_specs = P(None, None, None, "col", None)
    rows, cols = mesh.shape["row"], mesh.shape["col"]

    def local(*args):
        sources, blocks = args[6].shape[1:3]
        entries = args[6].shape[4]
        owners = (
            rows == blocks == 4
            and cols == 2 * rows
            and sources == 4 * cols
            and max(args[5].shape[0], args[1].shape[2]) <= LANES
            and entries == 2 * LANES + LANES // 4 == 3 * args[4].shape[2]
        )
        return (local_owners if owners else local_general)(*args)

    return jax.shard_map(local, mesh=mesh, in_specs=in_specs, out_specs=out_specs, check_vma=False)
```

```python
import jax
import jax.numpy as jnp
from jax import lax
from jax.experimental import pallas as pl
from jax.experimental.pallas import tpu as pltpu
from jax.sharding import PartitionSpec as P

PRODUCTS = 3
LANES = 128
SMALLEST = 2.0**-100
VMEM_BYTES = 8 * 1024 * 1024
BF = jnp.bfloat16
F32 = jnp.float32


def from_root(array, axis, root):
    mine = lax.axis_index(axis) == root
    return lax.psum(jnp.where(mine, array, jnp.zeros_like(array)), axis)


def complex_scale(field_now, contrast_re, contrast_im):
    real_part = field_now[0]
    imag_part = field_now[1]
    scaled = jnp.stack(
        [
            contrast_re * real_part - contrast_im * imag_part,
            contrast_re * imag_part + contrast_im * real_part,
        ]
    )
    return scaled.astype(BF)


def combine(products):
    return jnp.stack([products[0, 0] - products[1, 1], products[0, 1] + products[1, 0]])


def local_general(green_blocks, slot_rows, slot_cols, slot_count, cell_class, class_contrast, background):
    row_index = lax.axis_index("row")
    col_index = lax.axis_index("col")
    stride = lax.axis_size("col")
    green_tiles = green_blocks[0, 0]
    slot_total = green_tiles.shape[0]
    entries = green_tiles.shape[-1]
    sources = background.shape[1]
    col_blocks = background.shape[2]
    row_blocks = 2 * col_blocks
    local_rows = slot_rows[0, 0]
    local_cols = slot_cols[0, 0]
    global_rows = local_rows // 2 * stride + 2 * row_index + local_rows % 2
    global_cols = local_cols * stride + col_index
    off_diagonal = (global_rows != global_cols).astype(F32)
    living = (jnp.arange(slot_total) < slot_count[0, 0]).astype(F32)
    row_pick = (local_rows[:, None] == jnp.arange(row_blocks)[None, :]).astype(F32) * living[:, None]
    col_pick = (local_cols[:, None] == jnp.arange(col_blocks)[None, :]).astype(F32) * (
        living * off_diagonal
    )[:, None]
    classes = class_contrast.shape[0]
    lookup = (cell_class[:, 0, :, None] == jnp.arange(classes)[None, None, :]).astype(F32)
    values = jnp.einsum("bte,ec->btc", lookup, class_contrast, precision=lax.Precision.HIGHEST)
    contrast_re = jnp.tile(values[:, :, 0], (1, 3))
    contrast_im = jnp.tile(values[:, :, 1], (1, 3))
    start_field = background[:, :, :, 0, :]
    field_now = start_field
    current = complex_scale(field_now, contrast_re, contrast_im)
    for step_index in range(PRODUCTS):
        final_step = step_index + 1 == PRODUCTS
        halves = [from_root(current, "col", 2 * row_index + parity) for parity in range(2)]
        row_current = jnp.stack(halves, axis=3).reshape(2, sources, row_blocks, entries)
        direct_in = jnp.take(current, local_cols, axis=2)
        mirror_in = jnp.take(row_current, local_rows, axis=2)
        direct_terms = combine(
            jnp.einsum("sqoi,pksi->qpkso", green_tiles, direct_in, preferred_element_type=F32)
        )
        mirror_terms = combine(
            jnp.einsum("sqoi,pkso->qpksi", green_tiles, mirror_in, preferred_element_type=F32)
        )
        direct_part = jnp.einsum(
            "pkse,sb->pkbe", direct_terms, row_pick, precision=lax.Precision.HIGHEST
        )
        mirror_part = jnp.einsum(
            "pkse,sb->pkbe", mirror_terms, col_pick, precision=lax.Precision.HIGHEST
        )
        row_total = lax.psum(direct_part, "col")
        owned_part = lax.dynamic_index_in_dim(
            row_total.reshape(2, sources, col_blocks, 2, entries),
            col_index % 2,
            axis=3,
            keepdims=False,
        )
        direct_here = from_root(owned_part, "row", col_index // 2)
        column_total = lax.psum(mirror_part, "row")
        field_now = start_field + column_total + direct_here
        if not final_step:
            current = complex_scale(field_now, contrast_re, contrast_im)
    return field_now[:, :, :, None, :]


MAIN = 2 * LANES
TAIL = LANES // 4
ENDS = 4 * MAIN
WIDTH = ENDS + LANES
POWER = 3 * TAIL


def turned(value):
    half = value.shape[0] // 2
    return jnp.concatenate([-value[half:], value[:half]], axis=0)


def shifted(value, lanes):
    return pltpu.roll(value, LANES - lanes, 1) if lanes else value


def put_block(xs_ref, at, value, mirror):
    entries = value.shape[1]
    both = [value.astype(BF), turned(value).astype(BF)]
    if mirror:
        xs_ref[at, :, :entries] = both[0]
        xs_ref[at, :, entries:] = both[1]
    else:
        xs_ref[at, :, :MAIN] = both[0][:, :MAIN]
        xs_ref[at, :, MAIN : 2 * MAIN] = both[1][:, :MAIN]
        xs_ref[at, :, 2 * MAIN :] = jnp.concatenate([part[:, MAIN:] for part in both], axis=1)


def gathered_rows(msg_ref, q, lanes):
    groups = msg_ref.shape[0] // 4
    return jnp.concatenate([msg_ref[q * groups + g, :, lanes].astype(F32) for g in range(groups)], axis=0)


def unpack_half(msg_ref, q, half, xs_ref, at):
    ends = gathered_rows(msg_ref, q, slice(ENDS, WIDTH))
    parts = []
    for k in (2 * half, 2 * half + 1):
        main = gathered_rows(msg_ref, q, slice(k * MAIN, (k + 1) * MAIN))
        parts.append(jnp.concatenate([main, shifted(ends, k * TAIL)[:, :TAIL]], axis=1))
    put_block(xs_ref, at, jnp.concatenate(parts, axis=0), half)


def put_side_by_side(out_ref, values):
    for q, value in enumerate(values):
        out_ref[:, q * MAIN : (q + 1) * MAIN] = value[:, :MAIN].astype(out_ref.dtype)
    out_ref[:, ENDS:] = jnp.concatenate([value[:, MAIN:] for value in values], axis=1).astype(out_ref.dtype)


def side_by_side(ref):
    ends = ref[:, ENDS:].astype(F32)
    mains = [ref[:, q * MAIN : (q + 1) * MAIN].astype(F32) for q in range(4)]
    return [jnp.concatenate([main, shifted(ends, q * TAIL)[:, :TAIL]], axis=1) for q, main in enumerate(mains)]


def copy_in(x_ref, xs_ref, offset, mirror):
    for q, value in enumerate(side_by_side(x_ref)):
        put_block(xs_ref, offset + q, value, mirror)


def across(left, right):
    return lax.dot_general(left, right, (((1,), (1,)), ((), ())), preferred_element_type=F32)


def slot_products(table_ref, g_ref, xs_ref, acc_ref, mirror, start_ref=None):
    acc_ref[...] = jnp.zeros_like(acc_ref)
    if start_ref is not None:
        acc_ref[: start_ref.shape[0]] = start_ref[...]
    slots, _, depth, entries = g_ref.shape
    table = table_ref[...]
    first = 2 if mirror else 0
    for s in range(slots):
        left = xs_ref[table[first, s]]
        if mirror:
            value = jnp.dot(left, g_ref[s].reshape(2 * depth, entries), preferred_element_type=F32)
        else:
            ends = jnp.concatenate([g_ref[s, 0, :, MAIN:], g_ref[s, 1, :, MAIN:]], axis=1)
            value = across(left[:, :MAIN], g_ref[s, 0, :, :MAIN])
            value += across(left[:, MAIN : 2 * MAIN], g_ref[s, 1, :, :MAIN])
            value += across(left[:, 2 * MAIN :], ends)
        acc_ref[table[first + 1, s]] += value


def start_kernel(classes, small_ref, back_ref, out_ref, contrast_ref):
    blocks = back_ref.shape[0]
    cells = contrast_ref.shape[2]
    kinds = small_ref[4 : 4 + blocks, :cells]
    tables = small_ref[4 + blocks : 6 + blocks, :]
    contrast = []
    for part in range(2):
        value = jnp.zeros(kinds.shape, F32)
        for k in range(classes):
            value = jnp.where(kinds == float(k), tables[part : part + 1, k : k + 1], value)
        contrast_ref[part] = value
        contrast.append(jnp.concatenate([value] * 3, axis=1))
    real, imag = contrast
    values = []
    for q in range(blocks):
        back = back_ref[q]
        values.append(real[q : q + 1] * back + imag[q : q + 1] * turned(back))
    put_side_by_side(out_ref, values)


def share_kernel(small_ref, contrast_ref, back_ref, marks_ref, share_ref):
    r = small_ref[2:3, 0:1]
    cells = contrast_ref.shape[2]
    for q in range(back_ref.shape[0]):
        share_ref[q] = jnp.where(r == 0.0, back_ref[q], 0.0)
        marks = []
        for part in range(2):
            value = contrast_ref[part, q : q + 1] * 2.0**15
            rest = (value - jnp.round(value)) * 2.0**16
            marks += [jnp.round(value), jnp.clip(jnp.round(rest), -32767.0, 32767.0)]
        marks = jnp.concatenate(marks, axis=0)
        marks_ref[q] = jnp.concatenate([marks, jnp.zeros((4, LANES - cells), F32)], axis=1)


def as_integers(value):
    return value.astype(jnp.int32).astype(jnp.int16)


def as_floats(value):
    return value.astype(jnp.int32).astype(F32)


def direct_kernel(first, table_ref, g_ref, x_ref, own_ref, other_ref, xs_ref, acc_ref):
    blocks = own_ref.shape[0]
    if first:
        copy_in(x_ref, xs_ref, 0, False)
    else:
        for q in range(blocks):
            unpack_half(x_ref, q, 0, xs_ref, q)
    slot_products(table_ref, g_ref, xs_ref, acc_ref, False)
    for q in range(blocks):
        own_ref[q] = acc_ref[q]
    put_side_by_side(other_ref, [acc_ref[blocks + q] for q in range(blocks)])


def mirror_kernel(first, table_ref, g_ref, x_ref, x_other_ref, *refs):
    *start, out_ref, xs_ref, acc_ref = refs
    blocks = out_ref.shape[0]
    if first:
        copy_in(x_ref, xs_ref, 0, True)
        copy_in(x_other_ref, xs_ref, blocks, True)
    else:
        for q in range(blocks):
            unpack_half(x_ref, q, 1, xs_ref, q)
            unpack_half(x_other_ref, q, 1, xs_ref, blocks + q)
    slot_products(table_ref, g_ref, xs_ref, acc_ref, True, *start)
    for q in range(blocks):
        out_ref[q] = acc_ref[q]


def pack_kernel(mirror_ref, own_ref, got_ref, *rest):
    msg_ref = rest[-1]
    coded = msg_ref.dtype != BF
    blocks, rows, _ = own_ref.shape
    half = rows // 2
    lane = lax.broadcasted_iota(jnp.int32, (half, LANES), 1)
    got = side_by_side(got_ref)
    for q in range(blocks):
        halves = [own_ref[q] + got[q], mirror_ref[q]]
        parts = [value[p * half : (p + 1) * half] for value in halves for p in range(2)]
        if coded:
            power, scale = row_power(parts)
            parts = [jnp.round(part * scale) for part in parts]
        parts = [part[:, :MAIN] for part in parts] + [jnp.concatenate([part[:, MAIN:] for part in parts], axis=1)]
        if coded:
            marks = jnp.concatenate([rest[0][q]] * (half // 4), axis=0) if len(rest) == 2 else 0.0
            parts.append(jnp.where(lane == POWER, power, marks))
            parts = [part.astype(jnp.int32) for part in parts]
        for g in range(half // 4):
            at = slice(4 * g, 4 * g + 4)
            d = q * (half // 4) + g
            for k, part in enumerate(parts):
                lanes = slice(k * MAIN, (k + 1) * MAIN) if k < 4 else slice(ENDS + (k - 4) * LANES, ENDS + (k - 3) * LANES)
                msg_ref[d, :, lanes] = part[at].astype(msg_ref.dtype)


def row_power(parts):
    most = jnp.abs(parts[0])
    for part in parts[1:]:
        most = jnp.maximum(most, jnp.abs(part))
    most = jnp.max(most, axis=1, keepdims=True)
    power = jnp.floor(jnp.log2(jnp.maximum(most, SMALLEST)) + 2.0**-12)
    return power, jnp.exp2(14.0 - power)


def partial_sums(msg_ref, rows, cols):
    direct = {}
    mirror = {}
    coded = msg_ref.dtype != BF

    def add(store, key, value):
        store[key] = store[key] + value if key in store else value

    for r in range(rows):
        for c in range(cols):
            d = r * cols + c
            j = 2 * r + c % 2
            if coded:
                scale = jnp.exp2(as_floats(msg_ref[d, :, WIDTH : WIDTH + LANES])[:, POWER : POWER + 1] - 14.0)
            for k in range(9):
                value = msg_ref[d, :, k * LANES : (k + 1) * LANES]
                value = as_floats(value) * scale if coded else value.astype(F32)
                if k < 4 or k == 8:
                    add(direct, (j, min(k, 4)), value)
                if k >= 4:
                    add(mirror, (c, k - 4), value)
    for j in range(cols):
        mirror[j, 4] = shifted(mirror[j, 4], 2 * TAIL)
    return {key: direct[key] + mirror[key] for key in direct}


def update_kernel(first, rows, cols, msg_ref, *refs):
    contrast_ref, out_ref = refs[::-1] if first else refs
    lane = lax.broadcasted_iota(jnp.int32, (4, LANES), 1)
    cells = (MAIN + TAIL) // 3
    sums = partial_sums(msg_ref, rows, cols)
    current = {}
    for j in range(cols):
        if first:
            marks = as_floats(msg_ref[j, :, WIDTH : WIDTH + LANES])
            contrast = []
            for row in (0, 2):
                value = marks[row : row + 1] * 2.0**-15 + marks[row + 1 : row + 2] * 2.0**-31
                value = jnp.broadcast_to(value, (4, LANES))
                near, far = shifted(value, TAIL), shifted(value, 2 * TAIL)
                contrast.append(
                    [
                        jnp.where(lane < cells, value, near),
                        jnp.where(lane < 2 * TAIL, near, far),
                        jnp.where(lane < TAIL, far, near),
                    ]
                )
            for part in range(2):
                for k in range(3):
                    contrast_ref[j, part, k] = contrast[part][k]
        else:
            contrast = [[contrast_ref[j, part, k] for k in range(3)] for part in range(2)]
        total = [sums[j, k] for k in range(5)]
        real, imag = contrast
        for k in range(2):
            current[j, k] = real[k] * total[k] - imag[k] * total[k + 2]
            current[j, k + 2] = real[k] * total[k + 2] + imag[k] * total[k]
        other = jnp.where(lane < TAIL, -shifted(total[4], TAIL), pltpu.roll(total[4], TAIL, 1))
        current[j, 4] = real[2] * total[4] + imag[2] * other
    for r in range(rows):
        for c in range(cols):
            d = r * cols + c
            j = 2 * r + c % 2
            for k in range(4):
                out_ref[d, :, k * LANES : (k + 1) * LANES] = current[c, k].astype(BF)
                out_ref[d, :, (k + 4) * LANES : (k + 5) * LANES] = current[j, k].astype(BF)
            ends = jnp.where(lane < 2 * TAIL, current[c, 4], shifted(current[j, 4], 2 * TAIL))
            out_ref[d, :, ENDS:WIDTH] = ends.astype(BF)


def last_kernel(rows, cols, msg_ref, out_ref):
    lane = lax.broadcasted_iota(jnp.int32, (4, LANES), 1)
    sums = partial_sums(msg_ref, rows, cols)
    for j in range(cols):
        ends = jnp.zeros((4, LANES), F32)
        for p in range(2):
            mine = (lane >= p * TAIL) & (lane < (p + 1) * TAIL)
            tail = jnp.where(mine, sums[j, 4], 0.0)
            power, scale = row_power([sums[j, 2 * p], sums[j, 2 * p + 1], tail])
            for k in range(2 * p, 2 * p + 2):
                coded = as_integers(jnp.round(sums[j, k] * scale))
                for r in range(rows):
                    out_ref[r * cols + j, :, k * LANES : (k + 1) * LANES] = coded
            ends = jnp.where(mine, jnp.round(tail * scale), jnp.where(lane == 2 * TAIL + p, power, ends))
        coded = as_integers(ends)
        for r in range(rows):
            out_ref[r * cols + j, :, 2 * MAIN : 2 * MAIN + LANES] = coded


def finish_kernel(msg_ref, back_ref, out_ref):
    blocks, rows, _ = out_ref.shape
    half = rows // 2
    groups = half // 4

    def rows_of(q, lanes):
        return jnp.concatenate([as_floats(msg_ref[q * groups + g, :, lanes]) for g in range(groups)], axis=0)

    for q in range(blocks):
        ends = rows_of(q, slice(2 * MAIN, 2 * MAIN + LANES))
        for p in range(2):
            at = slice(p * half, (p + 1) * half)
            scale = jnp.exp2(ends[:, 2 * TAIL + p : 2 * TAIL + p + 1] - 14.0)
            main = rows_of(q, slice(p * MAIN, (p + 1) * MAIN))
            out_ref[q, at, :MAIN] = back_ref[q, at, :MAIN] + main * scale
            out_ref[q, at, MAIN:] = back_ref[q, at, MAIN:] + shifted(ends, p * TAIL)[:, :TAIL] * scale


def whole_call(kernel, out_shape, operands, scratch, name):
    vmem = pl.BlockSpec(memory_space=pltpu.VMEM)
    return pl.pallas_call(
        kernel,
        out_shape=out_shape,
        in_specs=[vmem] * len(operands),
        out_specs=jax.tree.map(lambda _: vmem, out_shape),
        scratch_shapes=scratch,
        compiler_params=pltpu.CompilerParams(vmem_limit_bytes=VMEM_BYTES),
        name=name,
    )(*operands)


def stacked(arrays):
    heights = [1 if array is None else array.shape[0] for array in arrays]
    total = 0
    at = 0
    for array, height in zip(arrays, heights):
        if array is not None:
            edges = ((at, sum(heights) - at - height, 0), (0, LANES - array.shape[1], 0))
            total += lax.pad(array, jnp.zeros((), array.dtype), edges).astype(F32)
        at += height
    return total


def local_owners(green_blocks, slot_rows, slot_cols, slot_count, cell_class, class_contrast, background):
    r = lax.axis_index("row")
    c = lax.axis_index("col")
    rows = lax.axis_size("row")
    cols = lax.axis_size("col")
    green = green_blocks[0, 0]
    slots, _, entries, _ = green.shape
    sources, blocks = background.shape[1:3]
    both = ("row", "col")

    small = stacked([slot_rows[0], slot_cols[0], None, None, cell_class[:, 0, :], class_contrast.T])
    line = lax.broadcasted_iota(jnp.int32, small.shape, 0)
    small = jnp.where(line == 2, r.astype(F32), jnp.where(line == 3, c.astype(F32), small))

    local_rows = small[0:1, :].astype(jnp.int32)
    local_cols = small[1:2, :].astype(jnp.int32)
    living = lax.broadcasted_iota(jnp.int32, (1, LANES), 1) < slot_count
    off_diagonal = (local_rows // 2 * cols + 2 * r + local_rows % 2) != (local_cols * cols + c)
    place = (local_rows % 2 ^ c % 2) * blocks + local_rows // 2
    spare = jnp.full_like(place, 2 * blocks)
    table = jnp.concatenate(
        [
            local_cols,
            jnp.where(living, place, spare),
            place,
            jnp.where(living & off_diagonal, local_cols, spare // 2),
        ],
        axis=0,
    )

    block = (2 * sources, entries)
    back = background[:, :, :, 0, :].transpose(2, 0, 1, 3).reshape((blocks,) + block)
    start, contrast = whole_call(
        lambda *refs: start_kernel(class_contrast.shape[0], *refs),
        (
            jax.ShapeDtypeStruct((2 * sources, WIDTH), BF),
            jax.ShapeDtypeStruct((2, blocks, entries // 3), F32),
        ),
        (small, back),
        [],
        "start",
    )

    core_pairs = [(i, i ^ 1) for i in range(cols)]
    chips = cols // 2
    arrived = []
    for hop in range(1, chips):
        pairs = []
        for a in range(rows):
            far = (a + hop) % chips
            for k in range(chips):
                for p in range(2):
                    to = {a: 2 * far + p, far: 2 * a + p}.get(k, 2 * k + 1 - p)
                    pairs.append((a * cols + 2 * k + p, a * cols + to))
        arrived.append(lax.ppermute(start, both, pairs))
    marks, back_share = whole_call(
        share_kernel,
        (
            jax.ShapeDtypeStruct((blocks, 4, LANES), F32),
            jax.ShapeDtypeStruct((blocks,) + block, F32),
        ),
        (small, contrast, back),
        [],
        "share",
    )

    part = jax.ShapeDtypeStruct((blocks,) + block, F32)
    message = jax.ShapeDtypeStruct((rows * cols, 4, WIDTH), BF)
    for step in range(PRODUCTS):
        first = step == 0
        final = step + 1 == PRODUCTS
        if first:
            direct_in = start
        else:
            direct_in, mirror_in = x_msg, (x_msg, lax.ppermute(x_msg, "col", core_pairs))
        own, other = whole_call(
            lambda *refs, first=first: direct_kernel(first, *refs),
            (part, jax.ShapeDtypeStruct((2 * sources, WIDTH), BF if final else F32)),
            (table, green, direct_in),
            [
                pltpu.VMEM((blocks, 2 * sources, 2 * entries), BF),
                pltpu.VMEM((2 * blocks + 1,) + block, F32),
            ],
            f"direct_{step}",
        )
        if first:
            marks, other, *arrived = lax.optimization_barrier((marks, other, *arrived))
            row_mine = start
            for hop in range(1, chips):
                row_mine = jnp.where(c // 2 == (r + hop) % chips, arrived[hop - 1], row_mine)
            row_other = lax.ppermute(row_mine, "col", core_pairs)
            mirror_in = (row_mine, row_other)
        if first:
            other, *mirror_in = lax.optimization_barrier((other, *mirror_in))
            mirror_in = tuple(mirror_in)
        got = lax.ppermute(other, "col", core_pairs)
        mirror = whole_call(
            lambda *refs, first=first: mirror_kernel(first, *refs),
            part,
            (table, green) + mirror_in + (() if final else (back_share,)),
            [
                pltpu.VMEM((2 * blocks, 2 * sources, 2 * entries), BF),
                pltpu.VMEM((blocks + 1,) + block, F32),
            ],
            f"mirror_{step}",
        )
        y_shape = message if final else jax.ShapeDtypeStruct((rows * cols, 4, WIDTH + LANES), jnp.int16)
        operands = (mirror, own, got) + ((marks,) if first else ())
        y_msg = whole_call(pack_kernel, y_shape, operands, [], f"pack_{step}")
        y_msg = lax.all_to_all(y_msg, both, 0, 0, tiled=True)
        run = lambda *refs, first=first: update_kernel(first, rows, cols, *refs)
        if first:
            x_msg, owner_contrast = whole_call(
                run,
                (message, jax.ShapeDtypeStruct((cols, 2, 3, 4, LANES), F32)),
                (y_msg,),
                [],
                f"update_{step}",
            )
        elif not final:
            x_msg = whole_call(run, message, (y_msg, owner_contrast), [], f"update_{step}")
        else:
            run = lambda *refs: last_kernel(rows, cols, *refs)
            x_shape = jax.ShapeDtypeStruct((rows * cols, 4, 2 * MAIN + LANES), jnp.int16)
            x_msg = whole_call(run, x_shape, (y_msg,), [], "last")
        x_msg = lax.all_to_all(x_msg, both, 0, 0, tiled=True)
    field = whole_call(finish_kernel, part, (x_msg, back), [], "finish")
    field = field.reshape(blocks, 2, sources, entries).transpose(1, 2, 0, 3)
    return field[:, :, :, None, :]


def solution(mesh):
    in_specs = (
        P("row", "col", None, None, None, None),
        P("row", "col", None),
        P("row", "col", None),
        P("row", "col"),
        P(None, "col", None),
        P(),
        P(None, None, None, "col", None),
    )
    out_specs = P(None, None, None, "col", None)
    rows, cols = mesh.shape["row"], mesh.shape["col"]

    def local(*args):
        sources, blocks = args[6].shape[1:3]
        entries = args[6].shape[4]
        owners = (
            rows == blocks == 4
            and cols == 2 * rows
            and sources == 4 * cols
            and max(args[5].shape[0], args[1].shape[2]) <= LANES
            and entries == 2 * LANES + LANES // 4 == 3 * args[4].shape[2]
        )
        return (local_owners if owners else local_general)(*args)

    return jax.shard_map(local, mesh=mesh, in_specs=in_specs, out_specs=out_specs, check_vma=False)
```
